512 devices in a mesh: dom: 32 (over z, y_hi), blk: 16 (over y_lo, x, core).
Axes of the slice: x: 4, y: 8 (y_hi: 4, y_lo: 2; y = y_hi * 2 + y_lo), z: 8, core: 2. Of those that a mesh axis runs over, the one named last changes fastest.
Arguments:
- queries: bfloat16 [65536, 512], P(('dom', 'blk')), may hold values from -22 to 22
- keys: bfloat16 [65536, 512], P(('dom', 'blk')), may hold values from -22 to 22
- values: bfloat16 [65536, 512], P(('dom', 'blk')), may hold values from -12 to 12
- grad_out: bfloat16 [65536, 512], P(('dom', 'blk')), may hold values from -6 to 6
- tile_keys: int32 [512, 16], P(('dom', 'blk')), may hold values from 0 to 15, as said below
- tile_count: int32 [512], P(('dom', 'blk')), may hold values from 1 to 16, as said below
- send_rows: int32 [512, 32, 16], P(('dom', 'blk')), may hold values from 0 to 127, as said below
Outputs:
- attended: bfloat16 [65536, 512], P(('dom', 'blk'))
- grad_q: bfloat16 [65536, 512], P(('dom', 'blk'))
- grad_k: bfloat16 [65536, 512], P(('dom', 'blk'))
- grad_v: bfloat16 [65536, 512], P(('dom', 'blk'))
The draws below stay inside these ranges and needn't reach their ends.
Inputs may be any that keep to these rules, and one draw needn't show every extreme that they name: `tile_keys`: each row is an ordering of the 16 places of a group, and its first entry is the block's own place. `tile_count`: some block's count is 16. `send_rows`: the 16 entries for one block and one group are distinct; entries for the block's own group are not used.
All inputs are finite; a program needn't handle non-finite values.
Results may differ from the reference program's by a relative error of at most 0.027.
Values may be sent and summed in bfloat16 or wider, within the bound.
A program may use at most 64 MiB of HBM per device.

```python
import math
import jax
import jax.numpy as jnp
from jax import lax

D = 512
HEADS = 8
HEAD = 64
BLOCK = 128
SLOT = 16
BLOCKS = 512
NODES = 65536
N_DOM = 32
N_BLK = 16


def draw_queries(key, part):
    key = jax.random.fold_in(key, 11)
    drawn = 1.4 * jnp.clip(jax.random.normal(key, (NODES, D), jnp.float32), -6.0, 6.0)
    return drawn.astype(jnp.bfloat16)


def draw_keys(key, part):
    key = jax.random.fold_in(key, 12)
    drawn = 1.4 * jnp.clip(jax.random.normal(key, (NODES, D), jnp.float32), -6.0, 6.0)
    return drawn.astype(jnp.bfloat16)


def draw_tile_keys(key, part):
    key = jax.random.fold_in(key, 21)
    orders = jax.vmap(lambda single: jax.random.permutation(single, N_BLK))(jax.random.split(key, BLOCKS)).astype(jnp.int32)
    own = (jnp.arange(BLOCKS) % N_BLK).astype(jnp.int32)
    where_own = jnp.argmax(orders == own[:, None], axis=1)
    numbers = jnp.arange(BLOCKS)
    leading = orders[:, 0]
    orders = orders.at[numbers, where_own].set(leading)
    orders = orders.at[:, 0].set(own)
    return orders.astype(jnp.int32)


def draw_tile_count(key, part):
    key = jax.random.fold_in(key, 31)
    first_key, second_key, third_key = jax.random.split(key, 3)
    first_draw = jax.random.randint(first_key, (BLOCKS,), 1, N_BLK + 1)
    second_draw = jax.random.randint(second_key, (BLOCKS,), 1, N_BLK + 1)
    counts = jnp.minimum(first_draw, second_draw)
    busiest = jax.random.randint(third_key, (), 0, BLOCKS)
    return counts.at[busiest].set(N_BLK).astype(jnp.int32)


def draw_send_rows(key, part):
    key = jax.random.fold_in(key, 41)
    pieces = jax.random.split(key, BLOCKS * N_DOM)
    lists = jax.vmap(lambda single: jax.random.permutation(single, BLOCK)[:SLOT])(pieces)
    return lists.reshape(BLOCKS, N_DOM, SLOT).astype(jnp.int32)


def block_levels(key, shape, shards, smallest, largest):
    loudness, own = 1.0, jax.random.fold_in(key, 6)
    for dim, blocks in shards:
        steps = jnp.exp(jax.random.uniform(jax.random.fold_in(own, dim), (blocks,), jnp.float32, smallest / len(shards), largest / len(shards)))
        loudness = loudness * jnp.repeat(steps, shape[dim] // blocks).reshape([-1 if axis == dim else 1 for axis in range(len(shape))])
    return loudness


def bell_draw(stream_key, dims, width, bound, shards=(), held_as=jnp.bfloat16):
    array = jax.random.normal(stream_key, dims, jnp.float32) * width
    if len(shards) > 0:
        array = block_levels(stream_key, dims, shards, -0.22, 0.18) * array
    return jnp.clip(array, min=-bound, max=bound).astype(held_as)


def setup_inputs(seed: int = 0) -> dict:
    seeds = jax.random.split(jax.random.key(seed), 8)
    queries = draw_queries(jax.random.fold_in(seeds[7], 71), 0)
    keys = draw_keys(jax.random.fold_in(seeds[7], 71), 0)
    values = bell_draw(seeds[2], (NODES, D), 2.0, 12.0, ((0, 512),))
    grad_out = bell_draw(seeds[3], (NODES, D), 1.0, 6.0, ((0, 512),))
    tile_keys = draw_tile_keys(jax.random.fold_in(seeds[7], 71), 0)
    tile_count = draw_tile_count(jax.random.fold_in(seeds[7], 71), 0)
    send_rows = draw_send_rows(jax.random.fold_in(seeds[7], 71), 0)
    return dict(queries=queries, keys=keys, values=values, grad_out=grad_out, tile_keys=tile_keys, tile_count=tile_count, send_rows=send_rows)


def split_heads(matrix):
    return matrix.astype(jnp.float32).reshape(matrix.shape[0], HEADS, HEAD)

def rounded(values):
    return lax.optimization_barrier(values.astype(jnp.bfloat16)).astype(jnp.float32)

def reference(queries, keys, values, grad_out, tile_keys, tile_count, send_rows):
    scale = 1.0 / math.sqrt(HEAD)
    paired = jnp.concatenate([keys, values], axis=1)
    near_rows = N_BLK * BLOCK
    far_rows = N_DOM * SLOT

    def one_block(grads, index):
        group = index // N_BLK
        place = index % N_BLK
        group_start = (group * near_rows).astype(jnp.int32)
        near = lax.dynamic_slice_in_dim(paired, group_start, near_rows, 0)
        order = tile_keys[index]
        chosen = (jnp.arange(N_BLK, dtype=jnp.int32) < tile_count[index]).astype(jnp.int32)
        listed = jnp.zeros((N_BLK,), jnp.int32).at[order].set(chosen)
        senders = (jnp.arange(N_DOM, dtype=jnp.int32) * N_BLK + place).astype(jnp.int32)
        picked = send_rows[senders, group]
        far_index = (senders[:, None] * BLOCK + picked).reshape(far_rows).astype(jnp.int32)
        far = paired[far_index]
        other = (jnp.arange(N_DOM, dtype=jnp.int32) != group).astype(jnp.int32)
        live = jnp.concatenate([jnp.repeat(listed, BLOCK), jnp.repeat(other, SLOT)]) > 0
        candidates = jnp.concatenate([near, far], axis=0)
        own = (index * BLOCK).astype(jnp.int32)
        query_rows = split_heads(lax.dynamic_slice_in_dim(queries, own, BLOCK, 0))
        cotangent = split_heads(lax.dynamic_slice_in_dim(grad_out, own, BLOCK, 0))
        key_rows = split_heads(candidates[:, :D])
        value_rows = split_heads(candidates[:, D:])
        scores = jnp.einsum('qhe,khe->hqk', query_rows, key_rows) * scale
        scores = jnp.where(live[None, None, :], scores, -jnp.inf)
        peak = lax.optimization_barrier(jnp.max(scores, axis=2, keepdims=True))
        log_total = peak + jnp.log(lax.optimization_barrier(jnp.sum(jnp.exp(scores - peak), axis=2, keepdims=True)))
        chances = jnp.exp(scores - log_total)
        weights = rounded(chances)
        attended = jnp.einsum('hqk,khe->qhe', weights, value_rows).reshape(BLOCK, D).astype(jnp.bfloat16)
        delta = jnp.einsum('qhe,qhe->hq', cotangent, split_heads(attended))[:, :, None]
        moves = jnp.einsum('qhe,khe->hqk', cotangent, value_rows)
        slopes = rounded(chances * (moves - delta))
        grad_q = (scale * jnp.einsum('hqk,khe->qhe', slopes, key_rows)).reshape(BLOCK, D).astype(jnp.bfloat16)
        key_terms = scale * jnp.einsum('hqk,qhe->khe', slopes, query_rows)
        value_terms = jnp.einsum('hqk,qhe->khe', weights, cotangent)
        terms = jnp.concatenate([key_terms.reshape(-1, D), value_terms.reshape(-1, D)], axis=1)
        terms = rounded(terms)
        current = lax.dynamic_slice_in_dim(grads, group_start, near_rows, 0)
        updated = lax.dynamic_update_slice_in_dim(grads, current + terms[:near_rows], group_start, 0)
        updated = updated.at[far_index].add(terms[near_rows:])
        return (updated, (attended, grad_q))
    start = jnp.zeros((NODES, 2 * D), jnp.float32)
    grads, outputs = lax.scan(one_block, start, jnp.arange(BLOCKS, dtype=jnp.int32))
    attended = outputs[0].reshape(NODES, D)
    grad_q = outputs[1].reshape(NODES, D)
    grad_k = grads[:, :D].astype(jnp.bfloat16)
    grad_v = grads[:, D:].astype(jnp.bfloat16)
    return (attended, grad_q, grad_k, grad_v)
```

```python
import functools

import jax
import jax.numpy as jnp
from jax import lax
from jax.experimental import pallas as pl
from jax.experimental.pallas import tpu as pltpu
from jax.sharding import PartitionSpec as P

HEADS = 8
PAIRS = 4
PHASES = 2
PER_PHASE = PAIRS // PHASES
BLOCK = 128
SLOT = 16
HIDDEN = -1e30
MESH = pl.DeviceIdType.MESH
F32 = jnp.float32
BF16 = jnp.bfloat16


def dot_nn(a, b):
    return lax.dot_general(a, b, (((1,), (0,)), ((), ())), preferred_element_type=F32)


def dot_nt(a, b):
    return lax.dot_general(a, b, (((1,), (1,)), ((), ())), preferred_element_type=F32)


def dot_tn(a, b):
    return lax.dot_general(a, b, (((0,), (0,)), ((), ())), preferred_element_type=F32)


def lanes_of(pair):
    return pl.ds(pl.multiple_of(pair * 128, 128), 128)


def kernel(
    n_dom, n_blk,
    q_ref, k_ref, v_ref, g_ref, order_ref, count_ref, rows_ref,
    att_ref, dq_ref, dk_ref, dv_ref,
    kv, qg, far_out, far_in, terms, ret, stats_out, stats_in,
    qst, gst, kst, vst, picks, bias, far_bias,
    s_near, p_near, peak, m_near, l_near, a_near, factor, delta_ref, far_dq, near_dk, near_dv, stat_cols,
    ag_send, ag_recv, far_send, far_recv, ret_send, ret_recv, stat_send, stat_recv,
):
    me_d = lax.axis_index("dom")
    me_b = lax.axis_index("blk")
    far_rows = n_dom * SLOT
    near_rows = n_blk * BLOCK
    chips = n_blk // 2

    barrier = pltpu.get_barrier_semaphore()

    def greet_dom(step, carry):
        pl.semaphore_signal(barrier, inc=1, device_id=(lax.rem(me_d + step, n_dom), me_b), device_id_type=MESH)
        return carry

    def greet_blk(step, carry):
        pl.semaphore_signal(barrier, inc=1, device_id=(me_d, lax.rem(me_b + step, n_blk)), device_id_type=MESH)
        return carry

    lax.fori_loop(1, n_blk, greet_blk, 0)
    lax.fori_loop(1, n_dom, greet_dom, 0)

    kv[me_b, 0] = k_ref[...]
    kv[me_b, 1] = v_ref[...]
    qg[me_b, 0] = q_ref[...]
    qg[me_b, 1] = g_ref[...]
    node = lax.broadcasted_iota(jnp.int32, (BLOCK, far_rows), 0)
    picks[...] = jnp.where(rows_ref[...] == node, 1.0, 0.0).astype(BF16)
    low = lax.broadcasted_iota(jnp.int32, (BLOCK, 128), 1) < 64

    def prepare(pair, carry):
        lanes = lanes_of(pair)
        phase = pair // PER_PHASE
        place = lax.rem(pair, PER_PHASE) * 256
        k_lanes = pl.ds(pl.multiple_of(place, 128), 128)
        v_lanes = pl.ds(pl.multiple_of(place + 128, 128), 128)
        k_own, v_own = k_ref[:, lanes], v_ref[:, lanes]
        spread = picks[...]
        far_out[phase, :, :, k_lanes] = dot_tn(spread, k_own).astype(BF16).reshape(n_dom, SLOT, 128)
        far_out[phase, :, :, v_lanes] = dot_tn(spread, v_own).astype(BF16).reshape(n_dom, SLOT, 128)
        for target, rows, scale in (
            (qst, q_ref[:, lanes], 0.125),
            (gst, g_ref[:, lanes], 1.0),
            (kst, k_own, 0.125),
            (vst, v_own, 1.0),
        ):
            wide = rows.astype(F32) * scale
            target[pair, 0:BLOCK, :] = jnp.where(low, wide, 0.0).astype(BF16)
            target[pair, BLOCK : 2 * BLOCK, :] = jnp.where(low, 0.0, wide).astype(BF16)
        return carry

    lax.fori_loop(0, PAIRS, prepare, 0)

    blank = jnp.zeros((SLOT, PER_PHASE * 256), BF16)
    for phase in range(PHASES):
        far_in[phase, me_d] = blank
        ret[phase, me_d] = blank
    tile = lax.broadcasted_iota(jnp.int32, (1, near_rows), 1) // BLOCK
    hidden = jnp.full((1, near_rows), HIDDEN, F32)
    for t in range(n_blk):
        wanted = jnp.where(t < count_ref[0], order_ref[0, t], -1)
        hidden = jnp.where(tile == wanted, 0.0, hidden)
    bias[...] = hidden
    slot_group = lax.broadcasted_iota(jnp.int32, (1, far_rows), 1) // SLOT
    far_bias[...] = jnp.where(slot_group == me_d, HIDDEN, 0.0)
    peak[...] = jnp.full(peak.shape, -3e38, F32)

    pl.semaphore_wait(barrier, n_dom + n_blk - 2)

    core = lax.rem(me_b, 2)
    x0 = lax.rem(me_b // 2, 4)
    y0 = me_b // 8
    x_right, x_left, x_far = lax.rem(x0 + 1, 4), lax.rem(x0 + 3, 4), lax.rem(x0 + 2, 4)
    y1, other = 1 - y0, 1 - core

    def block_id(y, x, c):
        return (y * 4 + x) * 2 + c

    sibling = block_id(y0, x0, other)
    right, left = block_id(y0, x_right, core), block_id(y0, x_left, core)
    across = block_id(y1, x0, core)
    started = []

    def send(part, block, device, half=None):
        buffer = (kv, qg)[part]
        ref = buffer.at[block] if half is None else buffer.at[block, half]
        copy = pltpu.make_async_remote_copy(
            src_ref=ref,
            dst_ref=ref,
            send_sem=ag_send.at[len(started)],
            recv_sem=ag_recv.at[part, block, 0 if half is None else half],
            device_id=(me_d, device),
            device_id_type=MESH,
        )
        copy.start()
        started.append(copy)

    def arrived(part, block, half=None):
        buffer = (kv, qg)[part]
        ref = buffer.at[block] if half is None else buffer.at[block, half]
        sem = ag_recv.at[part, block, 0 if half is None else half]
        pltpu.make_async_copy(ref, ref, sem).wait()

    def gather_own(part):
        for device in (right, left, across, sibling):
            send(part, me_b, device)

    def gather_ring(part, y):
        from_left, from_right = block_id(y, x_left, core), block_id(y, x_right, core)
        arrived(part, from_left)
        send(part, from_left, right, 0)
        send(part, from_left, sibling)
        arrived(part, from_right)
        send(part, from_right, left, 1)
        send(part, from_right, sibling)

    def gather_across(part):
        block = block_id(y1, x0, core)
        arrived(part, block)
        for device in (right, left, sibling):
            send(part, block, device)

    def gather_far(part, y):
        block = block_id(y, x_far, core)
        arrived(part, block, 0)
        arrived(part, block, 1)
        send(part, block, sibling)

    gather_own(0)

    def spread_order(step):
        hops_z, hops_y = step // 4, lax.rem(step, 4)
        dz = jnp.where(lax.rem(hops_z, 2) == 1, (hops_z + 1) // 2, 8 - hops_z // 2)
        dy = jnp.where(lax.rem(hops_y, 2) == 1, (hops_y + 1) // 2, 4 - hops_y // 2)
        z, y = lax.rem(me_d // 4 + dz, 8), lax.rem(lax.rem(me_d, 4) + dy, 4)
        return z * 4 + y

    def exchange(source, target, send_sem, recv_sem, phase):
        def one(step, carry):
            group = spread_order(step)
            pltpu.make_async_remote_copy(
                src_ref=source.at[phase, group],
                dst_ref=target.at[phase, me_d],
                send_sem=send_sem.at[phase],
                recv_sem=recv_sem.at[phase],
                device_id=(group, me_b),
                device_id_type=MESH,
            ).start()
            return carry

        lax.fori_loop(1, n_dom, one, 0)

    def exchanged(buffer, sem, phase):
        ref = buffer.at[phase, pl.ds(0, n_dom - 1)]
        pltpu.make_async_copy(ref, ref, sem.at[phase]).wait()

    for phase in range(PHASES):
        exchange(far_out, far_in, far_send, far_recv, phase)

    def score_chip(y, x):
        chip = y * 4 + x

        def one(pair, carry):
            key_rows = kv[pl.ds(2 * chip, 2), 0, :, lanes_of(pair)].reshape(256, 128)
            row = bias[:, pl.ds(pl.multiple_of(chip * 256, 256), 256)]
            scores = dot_nt(qst[pair], key_rows) + row
            s_near[chip, pair] = scores
            peak[pair] = jnp.maximum(peak[pair], jnp.maximum(scores[:, :128], scores[:, 128:]))
            return carry

        lax.fori_loop(0, PAIRS, one, 0)

    def score_sibling(y, x):
        arrived(0, block_id(y, x, other))
        score_chip(y, x)

    score_sibling(y0, x0)
    gather_ring(0, y0)
    gather_across(0)
    score_sibling(y0, x_left)
    score_sibling(y0, x_right)
    gather_far(0, y0)
    score_sibling(y1, x0)
    gather_ring(0, y1)
    score_sibling(y0, x_far)
    gather_far(0, y1)
    gather_own(1)
    score_sibling(y1, x_left)
    score_sibling(y1, x_right)
    score_sibling(y1, x_far)

    def weigh(pair, carry):
        top = jnp.max(peak[pair], axis=1, keepdims=True)

        def one(chip, held):
            total, out = held
            exps = jnp.exp(s_near[chip, pair] - top)
            total = total + exps[:, :128] + exps[:, 128:]
            narrow = exps.astype(BF16)
            p_near[chip, pair] = narrow
            value_rows = kv[pl.ds(2 * chip, 2), 1, :, lanes_of(pair)].reshape(256, 128)
            return total, out + dot_nn(narrow, value_rows)

        zero = jnp.zeros((256, 128), F32)
        total, out = lax.fori_loop(0, chips, one, (zero, zero))
        m_near[pair] = top
        l_near[pair] = jnp.sum(total, axis=1, keepdims=True)
        a_near[pair] = out
        return carry

    gather_ring(1, y0)
    lax.fori_loop(0, PAIRS // 2, weigh, 0)
    gather_across(1)
    gather_far(1, y0)
    lax.fori_loop(PAIRS // 2, PAIRS, weigh, 0)
    gather_ring(1, y1)

    column = lax.broadcasted_iota(jnp.int32, (BLOCK, 128), 1)

    def far_pair(phase, place):
        pair = phase * PER_PHASE + place
        lanes = lanes_of(pair)
        k_lanes, v_lanes = pl.ds(place * 256, 128), pl.ds(place * 256 + 128, 128)
        key_rows = far_in[phase, :, :, k_lanes].reshape(far_rows, 128)
        value_rows = far_in[phase, :, :, v_lanes].reshape(far_rows, 128)
        queries, cotangent = qst[pair], gst[pair]
        scores = dot_nt(queries, key_rows) + far_bias[...]
        moves = dot_nt(cotangent, value_rows)
        top = jnp.max(scores, axis=1, keepdims=True)
        exps = jnp.exp(scores - top)
        total = jnp.sum(exps, axis=1, keepdims=True)
        far_att = dot_nn(exps.astype(BF16), value_rows)
        near_top = m_near[pair]
        highest = jnp.maximum(top, near_top)
        near_scale, far_scale = jnp.exp(near_top - highest), jnp.exp(top - highest)
        whole = near_scale * l_near[pair] + far_scale * total
        near_scale, far_scale = near_scale / whole, far_scale / whole
        out = a_near[pair] * near_scale + far_att * far_scale
        attended = jnp.where(low, out[:BLOCK], out[BLOCK:]).astype(BF16)
        att_ref[:, lanes] = attended
        product = g_ref[:, lanes].astype(F32) * attended.astype(F32)
        delta0 = jnp.sum(jnp.where(low, product, 0.0), axis=1, keepdims=True)
        delta1 = jnp.sum(jnp.where(low, 0.0, product), axis=1, keepdims=True)
        delta = jnp.concatenate([delta0, delta1], axis=0)
        log_total = highest + jnp.log(whole)
        chances = exps * far_scale
        weights = chances.astype(BF16)
        slopes = (chances * (moves - delta)).astype(BF16)
        terms[phase, :, :, k_lanes] = dot_tn(slopes, queries).astype(BF16).reshape(n_dom, SLOT, 128)
        terms[phase, :, :, v_lanes] = dot_tn(weights, cotangent).astype(BF16).reshape(n_dom, SLOT, 128)
        far_dq[pair] = dot_nn(slopes, key_rows)
        factor[pair] = near_scale
        delta_ref[pair] = delta
        held = stat_cols[...]
        held = jnp.where(column == 2 * pair, log_total[:BLOCK], held)
        held = jnp.where(column == 2 * pair + 1, log_total[BLOCK:], held)
        held = jnp.where(column == HEADS + 2 * pair, delta0, held)
        held = jnp.where(column == HEADS + 2 * pair + 1, delta1, held)
        stat_cols[...] = held

    stat_cols[...] = jnp.zeros((BLOCK, 128), F32)
    for phase in range(PHASES):
        exchanged(far_in, far_recv, phase)
        for place in range(PER_PHASE):
            far_pair(phase, place)
        exchange(terms, ret, ret_send, ret_recv, phase)
        if phase == 0:
            gather_far(1, y1)

    stat_rows = stat_cols[...].T
    for block in range(n_blk):
        row = bias[:, block * BLOCK : (block + 1) * BLOCK]
        stats_out[block, 0:HEADS, :] = stat_rows[0:HEADS] - row
        stats_out[block, HEADS : 2 * HEADS, :] = stat_rows[HEADS : 2 * HEADS]
    stats_in[me_b] = stats_out[me_b]

    def tell(step, carry):
        block = lax.rem(me_b + step, n_blk)
        pltpu.make_async_remote_copy(
            src_ref=stats_out.at[block],
            dst_ref=stats_in.at[me_b],
            send_sem=stat_send.at[0],
            recv_sem=stat_recv.at[0],
            device_id=(me_d, block),
            device_id_type=MESH,
        ).start()
        return carry

    lax.fori_loop(1, n_blk, tell, 0)

    def query_pair(pair, carry):
        lanes = lanes_of(pair)
        cotangent, delta = gst[pair], delta_ref[pair]

        def one(chip, held):
            key_rows = kv[pl.ds(2 * chip, 2), 0, :, lanes].reshape(256, 128)
            value_rows = kv[pl.ds(2 * chip, 2), 1, :, lanes].reshape(256, 128)
            moves = dot_nt(cotangent, value_rows)
            slopes = (p_near[chip, pair].astype(F32) * (moves - delta)).astype(BF16)
            return held + dot_nn(slopes, key_rows)

        near = lax.fori_loop(0, chips, one, jnp.zeros((256, 128), F32))
        both = (far_dq[pair] + near * factor[pair]) * 0.125
        dq_ref[:, lanes] = jnp.where(low, both[:BLOCK], both[BLOCK:]).astype(BF16)
        return carry

    lax.fori_loop(0, PAIRS, query_pair, 0)

    all_stats = stats_in.at[pl.ds(0, n_blk - 1)]
    pltpu.make_async_copy(all_stats, all_stats, stat_recv.at[0]).wait()
    for y in (y0, y1):
        for x in (x0, x_left, x_right, x_far):
            arrived(1, block_id(y, x, other))

    def key_pair(pair, carry):
        lanes = lanes_of(pair)
        own_keys, own_values = kst[pair], vst[pair]

        def stat_row(chip, first):
            parts = [
                jnp.concatenate([stats_in[2 * chip, pl.ds(row, 1), :], stats_in[2 * chip + 1, pl.ds(row, 1), :]], axis=1)
                for row in (first, first + 1)
            ]
            return parts

        def one(chip, held):
            sum_k, sum_v = held
            query_rows = qg[pl.ds(2 * chip, 2), 0, :, lanes].reshape(256, 128)
            grad_rows = qg[pl.ds(2 * chip, 2), 1, :, lanes].reshape(256, 128)
            scores = dot_nt(own_keys, query_rows)
            moves = dot_nt(own_values, grad_rows)
            log0, log1 = stat_row(chip, 2 * pair)
            delta0, delta1 = stat_row(chip, HEADS + 2 * pair)
            chances0 = jnp.exp(scores[:BLOCK] - log0)
            chances1 = jnp.exp(scores[BLOCK:] - log1)
            slopes0 = chances0 * (moves[:BLOCK] - delta0)
            slopes1 = chances1 * (moves[BLOCK:] - delta1)
            weights = jnp.concatenate([chances0, chances1], axis=0).astype(BF16)
            slopes = jnp.concatenate([slopes0, slopes1], axis=0).astype(BF16)
            return sum_k + dot_nn(slopes, query_rows), sum_v + dot_nn(weights, grad_rows)

        zero = jnp.zeros((256, 128), F32)
        sum_k, sum_v = lax.fori_loop(0, chips, one, (zero, zero))
        near_dk[pair] = jnp.where(low, sum_k[:BLOCK], sum_k[BLOCK:]) * 0.125
        near_dv[pair] = jnp.where(low, sum_v[:BLOCK], sum_v[BLOCK:])
        return carry

    lax.fori_loop(0, PAIRS, key_pair, 0)

    for phase in range(PHASES):
        exchanged(ret, ret_recv, phase)
        for place in range(PER_PHASE):
            pair = phase * PER_PHASE + place
            cols = slice(pair * 128, pair * 128 + 128)
            spread = picks[...]
            back_k = ret[phase, :, :, place * 256 : place * 256 + 128].reshape(far_rows, 128)
            back_v = ret[phase, :, :, place * 256 + 128 : place * 256 + 256].reshape(far_rows, 128)
            dk_ref[:, cols] = (near_dk[pair] + dot_nn(spread, back_k)).astype(BF16)
            dv_ref[:, cols] = (near_dv[pair] + dot_nn(spread, back_v)).astype(BF16)

    for copy in started:
        copy.wait_send()
    for phase in range(PHASES):
        exchanged(far_out, far_send, phase)
        exchanged(terms, ret_send, phase)
    sent_stats = stats_out.at[pl.ds(0, n_blk - 1)]
    pltpu.make_async_copy(sent_stats, sent_stats, stat_send.at[0]).wait()


def on_device(n_dom, n_blk, queries, keys, values, grad_out, tile_keys, tile_count, send_rows):
    rows, width = queries.shape
    far_rows = n_dom * SLOT
    chips = n_blk // 2
    vmem = pl.BlockSpec(memory_space=pltpu.VMEM)
    smem = pl.BlockSpec(memory_space=pltpu.SMEM)
    far_shape = (PHASES, n_dom, SLOT, PER_PHASE * 256)
    stack = pltpu.VMEM((PAIRS, 256, 128), BF16)
    wide = pltpu.VMEM((PAIRS, 256, 128), F32)
    thin = pltpu.VMEM((PAIRS, 256, 1), F32)
    own = pltpu.VMEM((PAIRS, BLOCK, 128), F32)
    dma = pltpu.SemaphoreType.DMA
    return pl.pallas_call(
        functools.partial(kernel, n_dom, n_blk),
        out_shape=[jax.ShapeDtypeStruct((rows, width), BF16)] * 4,
        in_specs=[vmem, vmem, vmem, vmem, smem, smem, vmem],
        out_specs=[vmem] * 4,
        scratch_shapes=[
            pltpu.VMEM((n_blk, 2, BLOCK, width), BF16),
            pltpu.VMEM((n_blk, 2, BLOCK, width), BF16),
            pltpu.VMEM(far_shape, BF16),
            pltpu.VMEM(far_shape, BF16),
            pltpu.VMEM(far_shape, BF16),
            pltpu.VMEM(far_shape, BF16),
            pltpu.VMEM((n_blk, 2 * HEADS, BLOCK), F32),
            pltpu.VMEM((n_blk, 2 * HEADS, BLOCK), F32),
            stack, stack, stack, stack,
            pltpu.VMEM((BLOCK, far_rows), BF16),
            pltpu.VMEM((1, n_blk * BLOCK), F32),
            pltpu.VMEM((1, far_rows), F32),
            pltpu.VMEM((chips, PAIRS, 256, 256), F32),
            pltpu.VMEM((chips, PAIRS, 256, 256), BF16),
            wide,
            thin, thin,
            wide,
            thin, thin,
            wide,
            own, own,
            pltpu.VMEM((BLOCK, 128), F32),
            dma((34,)), dma((2, n_blk, 2)),
            dma((PHASES,)), dma((PHASES,)), dma((PHASES,)), dma((PHASES,)),
            dma((1,)), dma((1,)),
        ],
        compiler_params=pltpu.CompilerParams(
            collective_id=0, has_side_effects=True, vmem_limit_bytes=50 * 1024 * 1024
        ),
        cost_estimate=pl.CostEstimate(flops=2_500_000_000, bytes_accessed=2_000_000, transcendentals=5_000_000),
    )(queries, keys, values, grad_out, tile_keys, tile_count, send_rows.reshape(1, far_rows))


def solution(mesh):
    n_dom, n_blk = mesh.shape["dom"], mesh.shape["blk"]
    both = ("dom", "blk")
    flat = P(both, None)
    return jax.shard_map(
        functools.partial(on_device, n_dom, n_blk),
        mesh=mesh,
        in_specs=(flat, flat, flat, flat, flat, P(both), P(both, None, None)),
        out_specs=(flat,) * 4,
        check_vma=False,
    )
```

```python
import functools

import jax
import jax.numpy as jnp
from jax import lax
from jax.experimental import pallas as pl
from jax.experimental.pallas import tpu as pltpu
from jax.sharding import PartitionSpec as P

HEADS = 8
PAIRS = 4
PHASES = 2
PER_PHASE = PAIRS // PHASES
BLOCK = 128
SLOT = 16
RELAYED = 11
HIDDEN = -1e30
MESH = pl.DeviceIdType.MESH
F32 = jnp.float32
BF16 = jnp.bfloat16


def dot_nn(a, b):
    return lax.dot_general(a, b, (((1,), (0,)), ((), ())), preferred_element_type=F32)


def dot_nt(a, b):
    return lax.dot_general(a, b, (((1,), (1,)), ((), ())), preferred_element_type=F32)


def dot_tn(a, b):
    return lax.dot_general(a, b, (((0,), (0,)), ((), ())), preferred_element_type=F32)


def lanes_of(pair):
    return pl.ds(pl.multiple_of(pair * 128, 128), 128)


def kernel(
    n_dom, n_blk,
    q_in, k_in, v_in, g_in, order_in, count_ref, rows_in,
    att_out, dq_out, dk_out, dv_out,
    kv, qg, far_out, far_in, terms, ret, out_relay, back_relay, stats_out, stats_in,
    order_ref, rows_ref, qst, gst, kst, vst, picks, bias, far_bias,
    s_near, p_near, peak, m_near, l_near, a_near, factor, delta_ref, far_dq, near_dk, near_dv, stat_cols,
    in_sem, ag_send, ag_recv, far_send, far_recv, far_mid, far_next, ret_send, ret_recv, ret_mid, ret_next,
    stat_send, stat_recv, att_ref, dq_ref, dk_ref, dv_ref, out_sem,
):
    me_d = lax.axis_index("dom")
    me_b = lax.axis_index("blk")
    far_rows = n_dom * SLOT
    near_rows = n_blk * BLOCK
    row_blocks = n_blk // 2
    row_keys = row_blocks * BLOCK

    barrier = pltpu.get_barrier_semaphore()

    def greet_dom(step, carry):
        pl.semaphore_signal(barrier, inc=1, device_id=(lax.rem(me_d + step, n_dom), me_b), device_id_type=MESH)
        return carry

    def greet_blk(step, carry):
        pl.semaphore_signal(barrier, inc=1, device_id=(me_d, lax.rem(me_b + step, n_blk)), device_id_type=MESH)
        return carry

    lax.fori_loop(1, n_blk, greet_blk, 0)
    lax.fori_loop(1, n_dom, greet_dom, 0)

    loads = [
        pltpu.make_async_copy(source, target, in_sem.at[number])
        for number, (source, target) in enumerate(
            (
                (order_in, order_ref),
                (rows_in, rows_ref),
                (k_in, kv.at[me_b, 0]),
                (v_in, kv.at[me_b, 1]),
                (q_in, qg.at[me_b, 0]),
                (g_in, qg.at[me_b, 1]),
            )
        )
    ]
    for load in loads:
        load.start()
    for load in loads:
        load.wait()
    k_ref, v_ref, q_ref, g_ref = kv.at[me_b, 0], kv.at[me_b, 1], qg.at[me_b, 0], qg.at[me_b, 1]
    group_of = lax.broadcasted_iota(jnp.int32, (n_dom, far_rows), 1) // SLOT
    widen = jnp.where(group_of == lax.broadcasted_iota(jnp.int32, (n_dom, far_rows), 0), 1.0, 0.0).astype(BF16)
    repeated = dot_nn(rows_ref[0].astype(F32).astype(BF16), widen)
    slot_of = lax.rem(lax.broadcasted_iota(jnp.int32, (SLOT, far_rows), 1), SLOT)
    slot = lax.broadcasted_iota(jnp.int32, (SLOT, far_rows), 0)
    row_list = jnp.sum(jnp.where(slot_of == slot, repeated, 0.0), axis=0, keepdims=True)
    node = lax.broadcasted_iota(jnp.int32, (BLOCK, far_rows), 0).astype(F32)
    hits = jnp.where(row_list == node, 1.0, 0.0)
    picks[...] = hits.astype(BF16)
    spread = hits.T.astype(BF16)
    low = lax.broadcasted_iota(jnp.int32, (BLOCK, 128), 1) < 64

    for pair in range(PAIRS):
        lanes = slice(pair * 128, pair * 128 + 128)
        phase, place = divmod(pair, PER_PHASE)
        k_own, v_own = k_ref[:, lanes], v_ref[:, lanes]
        for own, first in ((k_own, place * 256), (v_own, place * 256 + 128)):
            moved = dot_nn(spread, own).astype(BF16).reshape(n_dom, SLOT, 128)
            far_out[phase, :, :, first : first + 128] = moved
        for target, rows, scale in (
            (qst, q_ref[:, lanes], 0.125),
            (gst, g_ref[:, lanes], 1.0),
            (kst, k_own, 0.125),
            (vst, v_own, 1.0),
        ):
            wide = rows.astype(F32) * scale
            target[pair, 0:BLOCK, :] = jnp.where(low, wide, 0.0).astype(BF16)
            target[pair, BLOCK : 2 * BLOCK, :] = jnp.where(low, 0.0, wide).astype(BF16)

    blank = jnp.zeros((SLOT, PER_PHASE * 256), BF16)
    for phase in range(PHASES):
        far_in[phase, me_d] = blank
        ret[phase, me_d] = blank
    tile = lax.broadcasted_iota(jnp.int32, (1, near_rows), 1) // BLOCK
    hidden = jnp.full((1, near_rows), HIDDEN, F32)
    for t in range(n_blk):
        wanted = jnp.where(t < count_ref[0], order_ref[0, t], -1)
        hidden = jnp.where(tile == wanted, 0.0, hidden)
    bias[...] = hidden
    slot_group = lax.broadcasted_iota(jnp.int32, (1, far_rows), 1) // SLOT
    far_bias[...] = jnp.where(slot_group == me_d, HIDDEN, 0.0)
    peak[...] = jnp.full(peak.shape, -3e38, F32)

    pl.semaphore_wait(barrier, n_dom + n_blk - 2)

    core = lax.rem(me_b, 2)
    x0 = lax.rem(me_b // 2, 4)
    y0 = me_b // 8
    x_right, x_left, x_far = lax.rem(x0 + 1, 4), lax.rem(x0 + 3, 4), lax.rem(x0 + 2, 4)
    y1, other = 1 - y0, 1 - core

    def block_id(y, x, c):
        return (y * 4 + x) * 2 + c

    sibling = block_id(y0, x0, other)
    right, left = block_id(y0, x_right, core), block_id(y0, x_left, core)
    across = block_id(y1, x0, core)
    started = []

    def send(part, block, device, half=None):
        buffer = (kv, qg)[part]
        ref = buffer.at[block] if half is None else buffer.at[block, half]
        copy = pltpu.make_async_remote_copy(
            src_ref=ref,
            dst_ref=ref,
            send_sem=ag_send.at[len(started)],
            recv_sem=ag_recv.at[part, block, 0 if half is None else half],
            device_id=(me_d, device),
            device_id_type=MESH,
        )
        copy.start()
        started.append(copy)

    def arrived(part, block, half=None):
        buffer = (kv, qg)[part]
        ref = buffer.at[block] if half is None else buffer.at[block, half]
        sem = ag_recv.at[part, block, 0 if half is None else half]
        pltpu.make_async_copy(ref, ref, sem).wait()

    def gather_own(part):
        for device in (right, left, across, sibling):
            send(part, me_b, device)

    def gather_ring(part, y):
        from_left, from_right = block_id(y, x_left, core), block_id(y, x_right, core)
        arrived(part, from_left)
        send(part, from_left, right, 0)
        send(part, from_left, sibling)
        arrived(part, from_right)
        send(part, from_right, left, 1)
        send(part, from_right, sibling)

    def gather_across(part):
        block = block_id(y1, x0, core)
        arrived(part, block)
        for device in (right, left, sibling):
            send(part, block, device)

    def gather_far(part, y):
        block = block_id(y, x_far, core)
        arrived(part, block, 0)
        arrived(part, block, 1)
        send(part, block, sibling)

    gather_own(0)

    def zigzag(step, size):
        return jnp.where(lax.rem(step, 2) == 1, (step + 1) // 2, lax.rem(size - step // 2, size))

    def at_offset(dz, dy):
        z = lax.rem(me_d // 4 + dz + 16, 8)
        y = lax.rem(lax.rem(me_d, 4) + dy + 8, 4)
        return z * 4 + y

    def legs(step, way):
        along_z = step < 4
        dz = jnp.where(along_z, 4, zigzag(step - 4, 8))
        dy = jnp.where(along_z, step, 2)
        first_z = jnp.where(along_z, 2 * way, dz)
        first_y = jnp.where(dy == 2, way, dy)
        return dz, dy, first_z, first_y

    def push(source, target, send_sem, recv_sem, group):
        pltpu.make_async_remote_copy(
            src_ref=source,
            dst_ref=target,
            send_sem=send_sem,
            recv_sem=recv_sem,
            device_id=(group, me_b),
            device_id_type=MESH,
        ).start()

    def exchange(source, relay, target, send_sem, mid_sem, recv_sem, phase):
        way = 1 - 2 * phase

        def indirect(step, carry):
            dz, dy, first_z, first_y = legs(step, way)
            push(
                source.at[phase, at_offset(dz, dy)], relay.at[phase, step],
                send_sem.at[phase], mid_sem.at[phase], at_offset(first_z, first_y),
            )
            return carry

        def direct(step, carry):
            group = at_offset(zigzag(step // 3, 8), zigzag(lax.rem(step, 3), 4))
            push(source.at[phase, group], target.at[phase, me_d], send_sem.at[phase], recv_sem.at[phase], group)
            return carry

        lax.fori_loop(0, RELAYED, indirect, 0)
        lax.fori_loop(1, 21, direct, 0)

    def pass_on(relay, target, mid_sem, next_sem, recv_sem, phase):
        way = 1 - 2 * phase
        pltpu.make_async_copy(relay.at[phase], relay.at[phase], mid_sem.at[phase]).wait()

        def one(step, carry):
            dz, dy, first_z, first_y = legs(step, way)
            push(
                relay.at[phase, step], target.at[phase, at_offset(-first_z, -first_y)],
                next_sem.at[phase], recv_sem.at[phase], at_offset(dz - first_z, dy - first_y),
            )
            return carry

        lax.fori_loop(0, RELAYED, one, 0)

    def exchanged(buffer, sem, phase):
        ref = buffer.at[phase, pl.ds(0, n_dom - 1)]
        pltpu.make_async_copy(ref, ref, sem.at[phase]).wait()

    for phase in range(PHASES):
        exchange(far_out, out_relay, far_in, far_send, far_mid, far_recv, phase)

    def score_chip(row, y, x):
        chip = y * 4 + x
        hidden_keys = bias[:, pl.ds(pl.multiple_of(chip * 256, 256), 256)]
        lanes = pl.ds(pl.multiple_of(x * 256, 256), 256)
        for pair in range(PAIRS):
            key_rows = kv[pl.ds(2 * chip, 2), 0, :, pair * 128 : pair * 128 + 128].reshape(256, 128)
            scores = dot_nt(qst[pair], key_rows) + hidden_keys
            s_near[row, pair, :, lanes] = scores
            peak[row, pair] = jnp.maximum(peak[row, pair], jnp.maximum(scores[:, :128], scores[:, 128:]))

    def score_sibling(row, x):
        y = (y0, y1)[row]
        arrived(0, block_id(y, x, other))
        score_chip(row, y, x)

    def weigh(row, y):
        def one(pair, carry):
            top = jnp.max(peak[row, pair], axis=1, keepdims=True)
            exps = jnp.exp(s_near[row, pair] - top)
            narrow = exps.astype(BF16)
            p_near[row, pair] = narrow
            value_rows = kv[pl.ds(y * row_blocks, row_blocks), 1, :, lanes_of(pair)].reshape(row_keys, 128)
            m_near[row, pair] = top
            l_near[row, pair] = jnp.sum(exps, axis=1, keepdims=True)
            a_near[row, pair] = dot_nn(narrow, value_rows)
            return carry

        lax.fori_loop(0, PAIRS, one, 0)

    out_path = (out_relay, far_in, far_mid, far_next, far_recv)
    back_path = (back_relay, ret, ret_mid, ret_next, ret_recv)

    score_sibling(0, x0)
    gather_ring(0, y0)
    gather_across(0)
    score_sibling(0, x_left)
    score_sibling(0, x_right)
    gather_far(0, y0)
    pass_on(*out_path, 0)
    score_sibling(0, x_far)
    score_sibling(1, x0)
    gather_ring(0, y1)
    weigh(0, y0)
    pass_on(*out_path, 1)
    gather_far(0, y1)
    gather_own(1)
    score_sibling(1, x_left)
    score_sibling(1, x_right)
    score_sibling(1, x_far)
    weigh(1, y1)

    column = lax.broadcasted_iota(jnp.int32, (BLOCK, 128), 1)

    def far_pair(phase, place):
        pair = phase * PER_PHASE + place
        lanes = lanes_of(pair)
        k_lanes, v_lanes = pl.ds(place * 256, 128), pl.ds(place * 256 + 128, 128)
        key_rows = far_in[phase, :, :, k_lanes].reshape(far_rows, 128)
        value_rows = far_in[phase, :, :, v_lanes].reshape(far_rows, 128)
        queries, cotangent = qst[pair], gst[pair]
        scores = dot_nt(queries, key_rows) + far_bias[...]
        moves = dot_nt(cotangent, value_rows)
        top = jnp.max(scores, axis=1, keepdims=True)
        exps = jnp.exp(scores - top)
        total = jnp.sum(exps, axis=1, keepdims=True)
        far_att = dot_nn(exps.astype(BF16), value_rows)
        top0, top1 = m_near[0, pair], m_near[1, pair]
        highest = jnp.maximum(top, jnp.maximum(top0, top1))
        scale0, scale1 = jnp.exp(top0 - highest), jnp.exp(top1 - highest)
        far_scale = jnp.exp(top - highest)
        whole = scale0 * l_near[0, pair] + scale1 * l_near[1, pair] + far_scale * total
        scale0, scale1, far_scale = scale0 / whole, scale1 / whole, far_scale / whole
        out = a_near[0, pair] * scale0 + a_near[1, pair] * scale1 + far_att * far_scale
        attended = jnp.where(low, out[:BLOCK], out[BLOCK:]).astype(BF16)
        att_ref[:, lanes] = attended
        product = g_ref[:, lanes].astype(F32) * attended.astype(F32)
        delta0 = jnp.sum(jnp.where(low, product, 0.0), axis=1, keepdims=True)
        delta1 = jnp.sum(jnp.where(low, 0.0, product), axis=1, keepdims=True)
        delta = jnp.concatenate([delta0, delta1], axis=0)
        log_total = highest + jnp.log(whole)
        chances = exps * far_scale
        weights = chances.astype(BF16)
        slopes = (chances * (moves - delta)).astype(BF16)
        terms[phase, :, :, k_lanes] = dot_tn(slopes, queries).astype(BF16).reshape(n_dom, SLOT, 128)
        terms[phase, :, :, v_lanes] = dot_tn(weights, cotangent).astype(BF16).reshape(n_dom, SLOT, 128)
        far_dq[pair] = dot_nn(slopes, key_rows)
        factor[0, pair] = scale0
        factor[1, pair] = scale1
        delta_ref[pair] = delta
        held = stat_cols[...]
        held = jnp.where(column == 2 * pair, log_total[:BLOCK], held)
        held = jnp.where(column == 2 * pair + 1, log_total[BLOCK:], held)
        held = jnp.where(column == HEADS + 2 * pair, delta0, held)
        held = jnp.where(column == HEADS + 2 * pair + 1, delta1, held)
        stat_cols[...] = held

    stat_cols[...] = jnp.zeros((BLOCK, 128), F32)
    for phase in range(PHASES):
        exchanged(far_in, far_recv, phase)
        for place in range(PER_PHASE):
            far_pair(phase, place)
        exchange(terms, back_relay, ret, ret_send, ret_mid, ret_recv, phase)
        if phase == 0:
            gather_ring(1, y0)
            gather_across(1)

    stat_rows = stat_cols[...].T
    for block in range(n_blk):
        row = bias[:, block * BLOCK : (block + 1) * BLOCK]
        stats_out[block, 0:HEADS, :] = stat_rows[0:HEADS] - row
        stats_out[block, HEADS : 2 * HEADS, :] = stat_rows[HEADS : 2 * HEADS]
    stats_in[me_b] = stats_out[me_b]

    def tell(step, carry):
        block = lax.rem(me_b + step, n_blk)
        pltpu.make_async_remote_copy(
            src_ref=stats_out.at[block],
            dst_ref=stats_in.at[me_b],
            send_sem=stat_send.at[0],
            recv_sem=stat_recv.at[0],
            device_id=(me_d, block),
            device_id_type=MESH,
        ).start()
        return carry

    lax.fori_loop(1, n_blk, tell, 0)

    def query_pair(pair, carry):
        lanes = lanes_of(pair)
        cotangent, delta = gst[pair], delta_ref[pair]
        both = far_dq[pair]
        for row, y in enumerate((y0, y1)):
            blocks = pl.ds(y * row_blocks, row_blocks)
            key_rows = kv[blocks, 0, :, lanes].reshape(row_keys, 128)
            value_rows = kv[blocks, 1, :, lanes].reshape(row_keys, 128)
            moves = dot_nt(cotangent, value_rows)
            slopes = (p_near[row, pair].astype(F32) * (moves - delta)).astype(BF16)
            both += dot_nn(slopes, key_rows) * factor[row, pair]
        both *= 0.125
        dq_ref[:, lanes] = jnp.where(low, both[:BLOCK], both[BLOCK:]).astype(BF16)
        return carry

    gather_far(1, y0)
    lax.fori_loop(0, PAIRS // 2, query_pair, 0)
    pass_on(*back_path, 0)
    gather_ring(1, y1)
    lax.fori_loop(PAIRS // 2, PAIRS, query_pair, 0)
    pass_on(*back_path, 1)
    gather_far(1, y1)

    def written(number, source, target):
        return pltpu.make_async_copy(source, target, out_sem.at[number])

    att_copy, dq_copy = written(0, att_ref, att_out), written(1, dq_ref, dq_out)
    att_copy.start()
    dq_copy.start()

    all_stats = stats_in.at[pl.ds(0, n_blk - 1)]
    pltpu.make_async_copy(all_stats, all_stats, stat_recv.at[0]).wait()
    for y in (y0, y1):
        for x in (x0, x_left, x_right, x_far):
            arrived(1, block_id(y, x, other))

    def key_pair(pair, carry):
        lanes = lanes_of(pair)
        own_keys, own_values = kst[pair], vst[pair]

        def stat_row(start, row):
            return jnp.concatenate([stats_in[start + n, pl.ds(row, 1), :] for n in range(4)], axis=1)

        sum_k = sum_v = jnp.zeros((256, 128), F32)
        for start in range(0, n_blk, 4):
            query_rows = qg[start : start + 4, 0, :, lanes].reshape(4 * BLOCK, 128)
            grad_rows = qg[start : start + 4, 1, :, lanes].reshape(4 * BLOCK, 128)
            scores = dot_nt(own_keys, query_rows)
            moves = dot_nt(own_values, grad_rows)
            weights, slopes = [], []
            for head in range(2):
                rows = slice(head * BLOCK, head * BLOCK + BLOCK)
                chances = jnp.exp(scores[rows] - stat_row(start, 2 * pair + head))
                weights.append(chances.astype(BF16))
                slopes.append((chances * (moves[rows] - stat_row(start, HEADS + 2 * pair + head))).astype(BF16))
            sum_k += dot_nn(jnp.concatenate(slopes, axis=0), query_rows)
            sum_v += dot_nn(jnp.concatenate(weights, axis=0), grad_rows)
        near_dk[pair] = jnp.where(low, sum_k[:BLOCK], sum_k[BLOCK:]) * 0.125
        near_dv[pair] = jnp.where(low, sum_v[:BLOCK], sum_v[BLOCK:])
        return carry

    lax.fori_loop(0, PAIRS, key_pair, 0)

    for phase in range(PHASES):
        exchanged(ret, ret_recv, phase)
        for place in range(PER_PHASE):
            pair = phase * PER_PHASE + place
            cols = slice(pair * 128, pair * 128 + 128)
            hits = picks[...]
            back_k = ret[phase, :, :, place * 256 : place * 256 + 128].reshape(far_rows, 128)
            back_v = ret[phase, :, :, place * 256 + 128 : place * 256 + 256].reshape(far_rows, 128)
            dk_ref[:, cols] = (near_dk[pair] + dot_nn(hits, back_k)).astype(BF16)
            dv_ref[:, cols] = (near_dv[pair] + dot_nn(hits, back_v)).astype(BF16)

    dk_copy, dv_copy = written(2, dk_ref, dk_out), written(3, dv_ref, dv_out)
    dk_copy.start()
    dv_copy.start()
    for copy in started:
        copy.wait_send()
    for phase in range(PHASES):
        exchanged(far_out, far_send, phase)
        exchanged(terms, ret_send, phase)
        pltpu.make_async_copy(out_relay.at[phase], out_relay.at[phase], far_next.at[phase]).wait()
        pltpu.make_async_copy(back_relay.at[phase], back_relay.at[phase], ret_next.at[phase]).wait()
    sent_stats = stats_out.at[pl.ds(0, n_blk - 1)]
    pltpu.make_async_copy(sent_stats, sent_stats, stat_send.at[0]).wait()
    for copy in (att_copy, dq_copy, dk_copy, dv_copy):
        copy.wait()


def write_out(a, b, c, d, a_out, b_out, c_out, d_out, sems):
    pairs = ((a, a_out), (b, b_out), (c, c_out), (d, d_out))
    copies = [pltpu.make_async_copy(here, there, sems.at[n]) for n, (here, there) in enumerate(pairs)]
    for copy in copies:
        copy.start()
    for copy in copies:
        copy.wait()


def on_device(n_dom, n_blk, queries, keys, values, grad_out, tile_keys, tile_count, send_rows):
    rows, width = queries.shape
    far_rows = n_dom * SLOT
    row_keys = n_blk // 2 * BLOCK
    hbm = pl.BlockSpec(memory_space=pltpu.HBM)
    smem = pl.BlockSpec(memory_space=pltpu.SMEM)
    far_shape = (PHASES, n_dom, SLOT, PER_PHASE * 256)
    stack = pltpu.VMEM((PAIRS, 256, 128), BF16)
    relay = pltpu.VMEM((PHASES, RELAYED, SLOT, PER_PHASE * 256), BF16)
    wide = pltpu.VMEM((PAIRS, 256, 128), F32)
    wide_rows = pltpu.VMEM((2, PAIRS, 256, 128), F32)
    thin = pltpu.VMEM((PAIRS, 256, 1), F32)
    thin_rows = pltpu.VMEM((2, PAIRS, 256, 1), F32)
    whole = pltpu.VMEM((rows, width), BF16)
    own = pltpu.VMEM((PAIRS, BLOCK, 128), F32)
    dma = pltpu.SemaphoreType.DMA
    held = pl.pallas_call(
        functools.partial(kernel, n_dom, n_blk),
        out_shape=[jax.ShapeDtypeStruct((rows, width), BF16)] * 4,
        in_specs=[hbm, hbm, hbm, hbm, hbm, smem, hbm],
        out_specs=[hbm] * 4,
        scratch_shapes=[
            pltpu.VMEM((n_blk, 2, BLOCK, width), BF16),
            pltpu.VMEM((n_blk, 2, BLOCK, width), BF16),
            pltpu.VMEM(far_shape, BF16),
            pltpu.VMEM(far_shape, BF16),
            pltpu.VMEM(far_shape, BF16),
            pltpu.VMEM(far_shape, BF16),
            relay, relay,
            pltpu.VMEM((n_blk, 2 * HEADS, BLOCK), F32),
            pltpu.VMEM((n_blk, 2 * HEADS, BLOCK), F32),
            pltpu.SMEM((1, n_blk), jnp.int32),
            pltpu.VMEM((1, SLOT, n_dom), jnp.int32),
            stack, stack, stack, stack,
            pltpu.VMEM((BLOCK, far_rows), BF16),
            pltpu.VMEM((1, n_blk * BLOCK), F32),
            pltpu.VMEM((1, far_rows), F32),
            pltpu.VMEM((2, PAIRS, 256, row_keys), F32),
            pltpu.VMEM((2, PAIRS, 256, row_keys), BF16),
            wide_rows,
            thin_rows, thin_rows,
            wide_rows,
            thin_rows, thin,
            wide,
            own, own,
            pltpu.VMEM((BLOCK, 128), F32),
            dma((6,)), dma((34,)), dma((2, n_blk, 2)),
            dma((PHASES,)), dma((PHASES,)), dma((PHASES,)), dma((PHASES,)),
            dma((PHASES,)), dma((PHASES,)), dma((PHASES,)), dma((PHASES,)),
            dma((1,)), dma((1,)),
            whole, whole, whole, whole, dma((4,)),
        ],
        compiler_params=pltpu.CompilerParams(
            collective_id=0, has_side_effects=True, vmem_limit_bytes=63 * 1024 * 1024
        ),
        cost_estimate=pl.CostEstimate(flops=2_500_000_000, bytes_accessed=2_000_000, transcendentals=5_000_000),
    )(queries, keys, values, grad_out, tile_keys, tile_count, send_rows.transpose(0, 2, 1))
    return pl.pallas_call(
        write_out,
        out_shape=[jax.ShapeDtypeStruct((rows, width), BF16)] * 4,
        in_specs=[hbm] * 4,
        out_specs=[hbm] * 4,
        scratch_shapes=[dma((4,))],
        compiler_params=pltpu.CompilerParams(vmem_limit_bytes=63 * 1024 * 1024),
    )(*held)


def solution(mesh):
    n_dom, n_blk = mesh.shape["dom"], mesh.shape["blk"]
    both = ("dom", "blk")
    flat = P(both, None)
    return jax.shard_map(
        functools.partial(on_device, n_dom, n_blk),
        mesh=mesh,
        in_specs=(flat, flat, flat, flat, flat, P(both), P(both, None, None)),
        out_specs=(flat,) * 4,
        check_vma=False,
    )
```

```python
import functools

import jax
import jax.numpy as jnp
from jax import lax
from jax.experimental import pallas as pl
from jax.experimental.pallas import tpu as pltpu
from jax.sharding import PartitionSpec as P

HEADS = 8
PAIRS = 4
PHASES = 2
PER_PHASE = PAIRS // PHASES
BLOCK = 128
SLOT = 16
RELAYED = 11
HIDDEN = -1e30
MESH = pl.DeviceIdType.MESH
F32 = jnp.float32
BF16 = jnp.bfloat16


def dot_nn(a, b):
    return lax.dot_general(a, b, (((1,), (0,)), ((), ())), preferred_element_type=F32)


def dot_nt(a, b):
    return lax.dot_general(a, b, (((1,), (1,)), ((), ())), preferred_element_type=F32)


def dot_tn(a, b):
    return lax.dot_general(a, b, (((0,), (0,)), ((), ())), preferred_element_type=F32)


def lanes_of(pair):
    return pl.ds(pl.multiple_of(pair * 128, 128), 128)


def kernel(
    n_dom, n_blk,
    q_in, k_in, v_in, g_in, order_in, count_ref, rows_in,
    att_out, dq_out, dk_out, dv_out,
    kv, qg, far_out, far_in, terms, ret, out_relay, back_relay, stats_out, stats_in,
    order_ref, rows_ref, qst, gst, kst, vst, picks, bias, far_bias,
    s_near, p_near, peak, m_near, l_near, a_near, factor, delta_ref, far_dq, near_dk, near_dv, stat_cols,
    in_sem, ag_send, ag_recv, far_send, far_recv, far_mid, far_next, ret_send, ret_recv, ret_mid, ret_next,
    stat_send, stat_recv, att_ref, dq_ref, dk_ref, dv_ref, out_sem,
):
    me_d = lax.axis_index("dom")
    me_b = lax.axis_index("blk")
    far_rows = n_dom * SLOT
    near_rows = n_blk * BLOCK
    row_blocks = n_blk // 2
    row_keys = row_blocks * BLOCK

    barrier = pltpu.get_barrier_semaphore()

    def greet_dom(step, carry):
        pl.semaphore_signal(barrier, inc=1, device_id=(lax.rem(me_d + step, n_dom), me_b), device_id_type=MESH)
        return carry

    def greet_blk(step, carry):
        pl.semaphore_signal(barrier, inc=1, device_id=(me_d, lax.rem(me_b + step, n_blk)), device_id_type=MESH)
        return carry

    lax.fori_loop(1, n_blk, greet_blk, 0)
    lax.fori_loop(1, n_dom, greet_dom, 0)

    loads = [
        pltpu.make_async_copy(source, target, in_sem.at[number])
        for number, (source, target) in enumerate(
            (
                (order_in, order_ref),
                (rows_in, rows_ref),
                (k_in, kv.at[me_b, 0]),
                (v_in, kv.at[me_b, 1]),
                (q_in, qg.at[me_b, 0]),
                (g_in, qg.at[me_b, 1]),
            )
        )
    ]
    for load in loads:
        load.start()
    for load in loads:
        load.wait()
    k_ref, v_ref, q_ref, g_ref = kv.at[me_b, 0], kv.at[me_b, 1], qg.at[me_b, 0], qg.at[me_b, 1]
    group_of = lax.broadcasted_iota(jnp.int32, (n_dom, far_rows), 1) // SLOT
    widen = jnp.where(group_of == lax.broadcasted_iota(jnp.int32, (n_dom, far_rows), 0), 1.0, 0.0).astype(BF16)
    repeated = dot_nn(rows_ref[0].astype(F32).astype(BF16), widen)
    slot_of = lax.rem(lax.broadcasted_iota(jnp.int32, (SLOT, far_rows), 1), SLOT)
    slot = lax.broadcasted_iota(jnp.int32, (SLOT, far_rows), 0)
    row_list = jnp.sum(jnp.where(slot_of == slot, repeated, 0.0), axis=0, keepdims=True)
    node = lax.broadcasted_iota(jnp.int32, (BLOCK, far_rows), 0).astype(F32)
    hits = jnp.where(row_list == node, 1.0, 0.0)
    picks[...] = hits.astype(BF16)
    spread = hits.T.astype(BF16)
    low = lax.broadcasted_iota(jnp.int32, (BLOCK, 128), 1) < 64

    for pair in range(PAIRS):
        lanes = slice(pair * 128, pair * 128 + 128)
        phase, place = divmod(pair, PER_PHASE)
        k_own, v_own = k_ref[:, lanes], v_ref[:, lanes]
        for own, first in ((k_own, place * 256), (v_own, place * 256 + 128)):
            moved = dot_nn(spread, own).astype(BF16).reshape(n_dom, SLOT, 128)
            far_out[phase, :, :, first : first + 128] = moved

    pl.semaphore_wait(barrier, n_dom + n_blk - 2)

    core = lax.rem(me_b, 2)
    x0 = lax.rem(me_b // 2, 4)
    y0 = me_b // 8
    x_right, x_left, x_far = lax.rem(x0 + 1, 4), lax.rem(x0 + 3, 4), lax.rem(x0 + 2, 4)
    y1, other = 1 - y0, 1 - core

    def block_id(y, x, c):
        return (y * 4 + x) * 2 + c

    sibling = block_id(y0, x0, other)
    right, left = block_id(y0, x_right, core), block_id(y0, x_left, core)
    across = block_id(y1, x0, core)
    started = []

    def send(part, block, device, half=None):
        buffer = (kv, qg)[part]
        ref = buffer.at[block] if half is None else buffer.at[block, half]
        copy = pltpu.make_async_remote_copy(
            src_ref=ref,
            dst_ref=ref,
            send_sem=ag_send.at[len(started)],
            recv_sem=ag_recv.at[part, block, 0 if half is None else half],
            device_id=(me_d, device),
            device_id_type=MESH,
        )
        copy.start()
        started.append(copy)

    def arrived(part, block, half=None):
        buffer = (kv, qg)[part]
        ref = buffer.at[block] if half is None else buffer.at[block, half]
        sem = ag_recv.at[part, block, 0 if half is None else half]
        pltpu.make_async_copy(ref, ref, sem).wait()

    def gather_own(part):
        for device in (across, right, left, sibling):
            if part == 0 or device is not across:
                send(part, me_b, device)

    def gather_ring(part, y):
        from_left, from_right = block_id(y, x_left, core), block_id(y, x_right, core)
        arrived(part, from_left)
        send(part, from_left, right, 0)
        send(part, from_left, sibling)
        arrived(part, from_right)
        send(part, from_right, left, 1)
        send(part, from_right, sibling)

    def gather_across(part):
        block = block_id(y1, x0, core)
        arrived(part, block)
        for device in (right, left, sibling):
            send(part, block, device)

    def gather_far(part, y):
        block = block_id(y, x_far, core)
        arrived(part, block, 0)
        arrived(part, block, 1)
        send(part, block, sibling)

    gather_own(0)

    def zigzag(step, size):
        return jnp.where(lax.rem(step, 2) == 1, (step + 1) // 2, lax.rem(size - step // 2, size))

    def at_offset(dz, dy):
        z = lax.rem(me_d // 4 + dz + 16, 8)
        y = lax.rem(lax.rem(me_d, 4) + dy + 8, 4)
        return z * 4 + y

    def legs(step, way):
        along_z = step < 4
        dz = jnp.where(along_z, 4, zigzag(step - 4, 8))
        dy = jnp.where(along_z, step, 2)
        first_z = jnp.where(along_z, 2 * way, dz)
        first_y = jnp.where(dy == 2, way, dy)
        return dz, dy, first_z, first_y

    def push(source, target, send_sem, recv_sem, group):
        pltpu.make_async_remote_copy(
            src_ref=source,
            dst_ref=target,
            send_sem=send_sem,
            recv_sem=recv_sem,
            device_id=(group, me_b),
            device_id_type=MESH,
        ).start()

    def exchange(source, relay, target, send_sem, mid_sem, recv_sem, phase):
        way = 1 - 2 * phase

        def indirect(step, carry):
            dz, dy, first_z, first_y = legs(step, way)
            push(
                source.at[phase, at_offset(dz, dy)], relay.at[phase, step],
                send_sem.at[phase], mid_sem.at[phase], at_offset(first_z, first_y),
            )
            return carry

        def direct(step, carry):
            group = at_offset(zigzag(step // 3, 8), zigzag(lax.rem(step, 3), 4))
            push(source.at[phase, group], target.at[phase, me_d], send_sem.at[phase], recv_sem.at[phase], group)
            return carry

        lax.fori_loop(0, RELAYED, indirect, 0)
        lax.fori_loop(1, 21, direct, 0)

    def pass_on(relay, target, mid_sem, next_sem, recv_sem, phase):
        way = 1 - 2 * phase
        pltpu.make_async_copy(relay.at[phase], relay.at[phase], mid_sem.at[phase]).wait()

        def one(step, carry):
            dz, dy, first_z, first_y = legs(step, way)
            push(
                relay.at[phase, step], target.at[phase, at_offset(-first_z, -first_y)],
                next_sem.at[phase], recv_sem.at[phase], at_offset(dz - first_z, dy - first_y),
            )
            return carry

        lax.fori_loop(0, RELAYED, one, 0)

    def exchanged(buffer, sem, phase):
        ref = buffer.at[phase, pl.ds(0, n_dom - 1)]
        pltpu.make_async_copy(ref, ref, sem.at[phase]).wait()

    for phase in range(PHASES):
        exchange(far_out, out_relay, far_in, far_send, far_mid, far_recv, phase)

    for pair in range(PAIRS):
        lanes = slice(pair * 128, pair * 128 + 128)
        for target, source, scale in ((qst, q_ref, 0.125), (gst, g_ref, 1.0), (kst, k_ref, 0.125), (vst, v_ref, 1.0)):
            wide = source[:, lanes].astype(F32) * scale
            target[pair, 0:BLOCK, :] = jnp.where(low, wide, 0.0).astype(BF16)
            target[pair, BLOCK : 2 * BLOCK, :] = jnp.where(low, 0.0, wide).astype(BF16)
    blank = jnp.zeros((SLOT, PER_PHASE * 256), BF16)
    for phase in range(PHASES):
        far_in[phase, me_d] = blank
        ret[phase, me_d] = blank
    tile = lax.broadcasted_iota(jnp.int32, (1, near_rows), 1) // BLOCK
    hidden = jnp.full((1, near_rows), HIDDEN, F32)
    for t in range(n_blk):
        wanted = jnp.where(t < count_ref[0], order_ref[0, t], -1)
        hidden = jnp.where(tile == wanted, 0.0, hidden)
    bias[...] = hidden
    slot_group = lax.broadcasted_iota(jnp.int32, (1, far_rows), 1) // SLOT
    far_bias[...] = jnp.where(slot_group == me_d, HIDDEN, 0.0)
    peak[...] = jnp.full(peak.shape, -3e38, F32)

    def score_chip(row, y, x):
        chip = y * 4 + x
        hidden_keys = bias[:, pl.ds(pl.multiple_of(chip * 256, 256), 256)]
        lanes = pl.ds(pl.multiple_of(x * 256, 256), 256)
        for pair in range(PAIRS):
            key_rows = kv[pl.ds(2 * chip, 2), 0, :, pair * 128 : pair * 128 + 128].reshape(256, 128)
            scores = dot_nt(qst[pair], key_rows) + hidden_keys
            s_near[row, pair, :, lanes] = scores
            peak[row, pair] = jnp.maximum(peak[row, pair], jnp.maximum(scores[:, :128], scores[:, 128:]))

    def score_sibling(row, x):
        y = (y0, y1)[row]
        arrived(0, block_id(y, x, other))
        score_chip(row, y, x)

    def weigh(row, y):
        def one(pair, carry):
            top = jnp.max(peak[row, pair], axis=1, keepdims=True)
            exps = jnp.exp(s_near[row, pair] - top)
            narrow = exps.astype(BF16)
            p_near[row, pair] = narrow
            value_rows = kv[pl.ds(y * row_blocks, row_blocks), 1, :, lanes_of(pair)].reshape(row_keys, 128)
            m_near[row, pair] = top
            l_near[row, pair] = jnp.sum(exps, axis=1, keepdims=True)
            a_near[row, pair] = dot_nn(narrow, value_rows)
            return carry

        lax.fori_loop(0, PAIRS, one, 0)

    out_path = (out_relay, far_in, far_mid, far_next, far_recv)
    back_path = (back_relay, ret, ret_mid, ret_next, ret_recv)

    score_sibling(0, x0)
    gather_ring(0, y0)
    gather_across(0)
    score_sibling(0, x_left)
    score_sibling(0, x_right)
    gather_far(0, y0)
    pass_on(*out_path, 0)
    score_sibling(0, x_far)
    score_sibling(1, x0)
    gather_ring(0, y1)
    weigh(0, y0)
    pass_on(*out_path, 1)
    gather_far(0, y1)
    gather_own(1)
    score_sibling(1, x_left)
    score_sibling(1, x_right)
    score_sibling(1, x_far)
    weigh(1, y1)

    column = lax.broadcasted_iota(jnp.int32, (BLOCK, 128), 1)

    def far_pair(phase, place):
        pair = phase * PER_PHASE + place
        lanes = lanes_of(pair)
        k_lanes, v_lanes = pl.ds(place * 256, 128), pl.ds(place * 256 + 128, 128)
        key_rows = far_in[phase, :, :, k_lanes].reshape(far_rows, 128)
        value_rows = far_in[phase, :, :, v_lanes].reshape(far_rows, 128)
        queries, cotangent = qst[pair], gst[pair]
        scores = dot_nt(queries, key_rows) + far_bias[...]
        moves = dot_nt(cotangent, value_rows)
        top = jnp.max(scores, axis=1, keepdims=True)
        exps = jnp.exp(scores - top)
        total = jnp.sum(exps, axis=1, keepdims=True)
        far_att = dot_nn(exps.astype(BF16), value_rows)
        top0, top1 = m_near[0, pair], m_near[1, pair]
        highest = jnp.maximum(top, jnp.maximum(top0, top1))
        scale0, scale1 = jnp.exp(top0 - highest), jnp.exp(top1 - highest)
        far_scale = jnp.exp(top - highest)
        whole = scale0 * l_near[0, pair] + scale1 * l_near[1, pair] + far_scale * total
        scale0, scale1, far_scale = scale0 / whole, scale1 / whole, far_scale / whole
        out = a_near[0, pair] * scale0 + a_near[1, pair] * scale1 + far_att * far_scale
        attended = jnp.where(low, out[:BLOCK], out[BLOCK:]).astype(BF16)
        att_ref[:, lanes] = attended
        product = g_ref[:, lanes].astype(F32) * attended.astype(F32)
        delta0 = jnp.sum(jnp.where(low, product, 0.0), axis=1, keepdims=True)
        delta1 = jnp.sum(jnp.where(low, 0.0, product), axis=1, keepdims=True)
        delta = jnp.concatenate([delta0, delta1], axis=0)
        log_total = highest + jnp.log(whole)
        chances = exps * far_scale
        weights = chances.astype(BF16)
        slopes = (chances * (moves - delta)).astype(BF16)
        terms[phase, :, :, k_lanes] = dot_tn(slopes, queries).astype(BF16).reshape(n_dom, SLOT, 128)
        terms[phase, :, :, v_lanes] = dot_tn(weights, cotangent).astype(BF16).reshape(n_dom, SLOT, 128)
        far_dq[pair] = dot_nn(slopes, key_rows)
        factor[0, pair] = scale0
        factor[1, pair] = scale1
        delta_ref[pair] = delta
        held = stat_cols[...]
        held = jnp.where(column == 2 * pair, log_total[:BLOCK], held)
        held = jnp.where(column == 2 * pair + 1, log_total[BLOCK:], held)
        held = jnp.where(column == HEADS + 2 * pair, delta0, held)
        held = jnp.where(column == HEADS + 2 * pair + 1, delta1, held)
        stat_cols[...] = held

    stat_cols[...] = jnp.zeros((BLOCK, 128), F32)
    for phase in range(PHASES):
        exchanged(far_in, far_recv, phase)
        if phase == PHASES - 1:
            send(1, me_b, across)
        for place in range(PER_PHASE):
            far_pair(phase, place)
        exchange(terms, back_relay, ret, ret_send, ret_mid, ret_recv, phase)
        if phase == 0:
            gather_ring(1, y0)

    stat_rows = stat_cols[...].T
    for block in range(n_blk):
        row = bias[:, block * BLOCK : (block + 1) * BLOCK]
        stats_out[block, 0:HEADS, :] = stat_rows[0:HEADS] - row
        stats_out[block, HEADS : 2 * HEADS, :] = stat_rows[HEADS : 2 * HEADS]
    stats_in[me_b] = stats_out[me_b]

    def tell(step, carry):
        block = lax.rem(me_b + step, n_blk)
        pltpu.make_async_remote_copy(
            src_ref=stats_out.at[block],
            dst_ref=stats_in.at[me_b],
            send_sem=stat_send.at[0],
            recv_sem=stat_recv.at[0],
            device_id=(me_d, block),
            device_id_type=MESH,
        ).start()
        return carry

    lax.fori_loop(1, n_blk, tell, 0)

    def query_pair(pair, carry):
        lanes = lanes_of(pair)
        cotangent, delta = gst[pair], delta_ref[pair]
        both = far_dq[pair]
        for row, y in enumerate((y0, y1)):
            blocks = pl.ds(y * row_blocks, row_blocks)
            key_rows = kv[blocks, 0, :, lanes].reshape(row_keys, 128)
            value_rows = kv[blocks, 1, :, lanes].reshape(row_keys, 128)
            moves = dot_nt(cotangent, value_rows)
            slopes = (p_near[row, pair].astype(F32) * (moves - delta)).astype(BF16)
            both += dot_nn(slopes, key_rows) * factor[row, pair]
        both *= 0.125
        dq_ref[:, lanes] = jnp.where(low, both[:BLOCK], both[BLOCK:]).astype(BF16)
        return carry

    gather_far(1, y0)
    lax.fori_loop(0, PAIRS // 2, query_pair, 0)
    pass_on(*back_path, 0)
    gather_across(1)
    lax.fori_loop(PAIRS // 2, PAIRS, query_pair, 0)
    pass_on(*back_path, 1)

    def written(number, source, target):
        return pltpu.make_async_copy(source, target, out_sem.at[number])

    att_copy, dq_copy = written(0, att_ref, att_out), written(1, dq_ref, dq_out)
    att_copy.start()
    dq_copy.start()

    all_stats = stats_in.at[pl.ds(0, n_blk - 1)]
    pltpu.make_async_copy(all_stats, all_stats, stat_recv.at[0]).wait()

    def key_pair(row, y, pair, carry):
        lanes = lanes_of(pair)
        own_keys, own_values = kst[pair], vst[pair]

        def stat_row(start, row):
            return jnp.concatenate([stats_in[y * row_blocks + start + n, pl.ds(row, 1), :] for n in range(4)], axis=1)

        sum_k = sum_v = jnp.zeros((256, 128), F32)
        for start in range(0, row_blocks, 4):
            blocks = pl.ds(y * row_blocks + start, 4)
            query_rows = qg[blocks, 0, :, lanes].reshape(4 * BLOCK, 128)
            grad_rows = qg[blocks, 1, :, lanes].reshape(4 * BLOCK, 128)
            scores = dot_nt(own_keys, query_rows)
            moves = dot_nt(own_values, grad_rows)
            weights, slopes = [], []
            for head in range(2):
                rows = slice(head * BLOCK, head * BLOCK + BLOCK)
                chances = jnp.exp(scores[rows] - stat_row(start, 2 * pair + head))
                weights.append(chances.astype(BF16))
                slopes.append((chances * (moves[rows] - stat_row(start, HEADS + 2 * pair + head))).astype(BF16))
            sum_k += dot_nn(jnp.concatenate(slopes, axis=0), query_rows)
            sum_v += dot_nn(jnp.concatenate(weights, axis=0), grad_rows)
        own_dk = jnp.where(low, sum_k[:BLOCK], sum_k[BLOCK:])
        own_dv = jnp.where(low, sum_v[:BLOCK], sum_v[BLOCK:])
        near_dk[pair] = own_dk if row == 0 else near_dk[pair] + own_dk
        near_dv[pair] = own_dv if row == 0 else near_dv[pair] + own_dv
        return carry

    def gathered(y):
        for x in (x0, x_left, x_right, x_far):
            arrived(1, block_id(y, x, other))

    gathered(y0)
    lax.fori_loop(0, PAIRS // 2, functools.partial(key_pair, 0, y0), 0)
    gather_ring(1, y1)
    lax.fori_loop(PAIRS // 2, PAIRS, functools.partial(key_pair, 0, y0), 0)
    gather_far(1, y1)
    gathered(y1)
    lax.fori_loop(0, PAIRS, functools.partial(key_pair, 1, y1), 0)

    for phase in range(PHASES):
        exchanged(ret, ret_recv, phase)
        for place in range(PER_PHASE):
            pair = phase * PER_PHASE + place
            cols = slice(pair * 128, pair * 128 + 128)
            hits = picks[...]
            back_k = ret[phase, :, :, place * 256 : place * 256 + 128].reshape(far_rows, 128)
            back_v = ret[phase, :, :, place * 256 + 128 : place * 256 + 256].reshape(far_rows, 128)
            dk_ref[:, cols] = (near_dk[pair] * 0.125 + dot_nn(hits, back_k)).astype(BF16)
            dv_ref[:, cols] = (near_dv[pair] + dot_nn(hits, back_v)).astype(BF16)

    dk_copy, dv_copy = written(2, dk_ref, dk_out), written(3, dv_ref, dv_out)
    dk_copy.start()
    dv_copy.start()
    for copy in started:
        copy.wait_send()
    for phase in range(PHASES):
        exchanged(far_out, far_send, phase)
        exchanged(terms, ret_send, phase)
        pltpu.make_async_copy(out_relay.at[phase], out_relay.at[phase], far_next.at[phase]).wait()
        pltpu.make_async_copy(back_relay.at[phase], back_relay.at[phase], ret_next.at[phase]).wait()
    sent_stats = stats_out.at[pl.ds(0, n_blk - 1)]
    pltpu.make_async_copy(sent_stats, sent_stats, stat_send.at[0]).wait()
    for copy in (att_copy, dq_copy, dk_copy, dv_copy):
        copy.wait()


def write_out(a, b, c, d, a_out, b_out, c_out, d_out, stage, sems):
    pairs = ((a, a_out), (b, b_out), (c, c_out), (d, d_out))
    reads = [pltpu.make_async_copy(pair[0], stage.at[n], sems.at[0, n]) for n, pair in enumerate(pairs)]
    writes = [pltpu.make_async_copy(stage.at[n], pair[1], sems.at[1, n]) for n, pair in enumerate(pairs)]
    for read in reads:
        read.start()
    for read, write in zip(reads, writes):
        read.wait()
        write.start()
    for write in writes:
        write.wait()


def on_device(n_dom, n_blk, queries, keys, values, grad_out, tile_keys, tile_count, send_rows):
    rows, width = queries.shape
    far_rows = n_dom * SLOT
    row_keys = n_blk // 2 * BLOCK
    hbm = pl.BlockSpec(memory_space=pltpu.HBM)
    smem = pl.BlockSpec(memory_space=pltpu.SMEM)
    far_shape = (PHASES, n_dom, SLOT, PER_PHASE * 256)
    stack = pltpu.VMEM((PAIRS, 256, 128), BF16)
    relay = pltpu.VMEM((PHASES, RELAYED, SLOT, PER_PHASE * 256), BF16)
    wide = pltpu.VMEM((PAIRS, 256, 128), F32)
    wide_rows = pltpu.VMEM((2, PAIRS, 256, 128), F32)
    thin = pltpu.VMEM((PAIRS, 256, 1), F32)
    thin_rows = pltpu.VMEM((2, PAIRS, 256, 1), F32)
    whole = pltpu.VMEM((rows, width), BF16)
    own = pltpu.VMEM((PAIRS, BLOCK, 128), F32)
    dma = pltpu.SemaphoreType.DMA
    held = pl.pallas_call(
        functools.partial(kernel, n_dom, n_blk),
        out_shape=[jax.ShapeDtypeStruct((rows, width), BF16)] * 4,
        in_specs=[hbm, hbm, hbm, hbm, hbm, smem, hbm],
        out_specs=[hbm] * 4,
        scratch_shapes=[
            pltpu.VMEM((n_blk, 2, BLOCK, width), BF16),
            pltpu.VMEM((n_blk, 2, BLOCK, width), BF16),
            pltpu.VMEM(far_shape, BF16),
            pltpu.VMEM(far_shape, BF16),
            pltpu.VMEM(far_shape, BF16),
            pltpu.VMEM(far_shape, BF16),
            relay, relay,
            pltpu.VMEM((n_blk, 2 * HEADS, BLOCK), F32),
            pltpu.VMEM((n_blk, 2 * HEADS, BLOCK), F32),
            pltpu.SMEM((1, n_blk), jnp.int32),
            pltpu.VMEM((1, SLOT, n_dom), jnp.int32),
            stack, stack, stack, stack,
            pltpu.VMEM((BLOCK, far_rows), BF16),
            pltpu.VMEM((1, n_blk * BLOCK), F32),
            pltpu.VMEM((1, far_rows), F32),
            pltpu.VMEM((2, PAIRS, 256, row_keys), F32),
            pltpu.VMEM((2, PAIRS, 256, row_keys), BF16),
            wide_rows,
            thin_rows, thin_rows,
            wide_rows,
            thin_rows, thin,
            wide,
            own, own,
            pltpu.VMEM((BLOCK, 128), F32),
            dma((6,)), dma((34,)), dma((2, n_blk, 2)),
            dma((PHASES,)), dma((PHASES,)), dma((PHASES,)), dma((PHASES,)),
            dma((PHASES,)), dma((PHASES,)), dma((PHASES,)), dma((PHASES,)),
            dma((1,)), dma((1,)),
            whole, whole, whole, whole, dma((4,)),
        ],
        compiler_params=pltpu.CompilerParams(
            collective_id=0, has_side_effects=True, vmem_limit_bytes=63 * 1024 * 1024
        ),
        cost_estimate=pl.CostEstimate(flops=2_500_000_000, bytes_accessed=2_000_000, transcendentals=5_000_000),
    )(queries, keys, values, grad_out, tile_keys, tile_count, send_rows.transpose(0, 2, 1))
    return pl.pallas_call(
        write_out,
        out_shape=[jax.ShapeDtypeStruct((rows, width), BF16)] * 4,
        in_specs=[hbm] * 4,
        out_specs=[hbm] * 4,
        scratch_shapes=[pltpu.VMEM((4, rows, width), BF16), dma((2, 4))],
        compiler_params=pltpu.CompilerParams(vmem_limit_bytes=63 * 1024 * 1024),
    )(*held)


def solution(mesh):
    n_dom, n_blk = mesh.shape["dom"], mesh.shape["blk"]
    both = ("dom", "blk")
    flat = P(both, None)
    return jax.shard_map(
        functools.partial(on_device, n_dom, n_blk),
        mesh=mesh,
        in_specs=(flat, flat, flat, flat, flat, P(both), P(both, None, None)),
        out_specs=(flat,) * 4,
        check_vma=False,
    )
```

```python
import functools

import jax
import jax.numpy as jnp
from jax import lax
from jax.experimental import pallas as pl
from jax.experimental.pallas import tpu as pltpu
from jax.sharding import PartitionSpec as P

HEADS = 8
PAIRS = 4
PHASES = 2
PER_PHASE = PAIRS // PHASES
BLOCK = 128
SLOT = 16
RELAYED = 11
HIDDEN = -1e30
MESH = pl.DeviceIdType.MESH
F32 = jnp.float32
BF16 = jnp.bfloat16


def dot_nn(a, b):
    return lax.dot_general(a, b, (((1,), (0,)), ((), ())), preferred_element_type=F32)


def dot_nt(a, b):
    return lax.dot_general(a, b, (((1,), (1,)), ((), ())), preferred_element_type=F32)


def dot_tn(a, b):
    return lax.dot_general(a, b, (((0,), (0,)), ((), ())), preferred_element_type=F32)


def lanes_of(pair):
    return pl.ds(pl.multiple_of(pair * 128, 128), 128)


def kernel(
    n_dom, n_blk,
    q_in, k_in, v_in, g_in, order_in, count_ref, rows_in,
    att_out, dq_out, dk_out, dv_out,
    kv, qg, far_out, far_in, terms, ret, out_relay, back_relay, stats_out, stats_in,
    order_ref, rows_ref, qst, gst, kst, vst, picks, bias, far_bias,
    s_near, p_near, peak, m_near, l_near, a_near, factor, delta_ref, far_dq, near_dk, near_dv, stat_cols,
    in_sem, ag_send, ag_recv, far_send, far_recv, far_mid, far_next, ret_send, ret_recv, ret_mid, ret_next,
    stat_send, stat_recv, att_ref, dq_ref, dk_ref, dv_ref, out_sem,
):
    me_d = lax.axis_index("dom")
    me_b = lax.axis_index("blk")
    far_rows = n_dom * SLOT
    near_rows = n_blk * BLOCK
    row_blocks = n_blk // 2
    row_keys = row_blocks * BLOCK

    barrier = pltpu.get_barrier_semaphore()

    def greet_dom(step, carry):
        pl.semaphore_signal(barrier, inc=1, device_id=(lax.rem(me_d + step, n_dom), me_b), device_id_type=MESH)
        return carry

    def greet_blk(step, carry):
        pl.semaphore_signal(barrier, inc=1, device_id=(me_d, lax.rem(me_b + step, n_blk)), device_id_type=MESH)
        return carry

    lax.fori_loop(1, n_blk, greet_blk, 0)
    lax.fori_loop(1, n_dom, greet_dom, 0)

    loads = [
        pltpu.make_async_copy(source, target, in_sem.at[number])
        for number, (source, target) in enumerate(
            (
                (order_in, order_ref),
                (rows_in, rows_ref),
                (k_in, kv.at[me_b, 0]),
                (v_in, kv.at[me_b, 1]),
                (q_in, qg.at[me_b, 0]),
                (g_in, qg.at[me_b, 1]),
            )
        )
    ]
    for load in loads:
        load.start()
    for load in loads:
        load.wait()
    k_ref, v_ref, q_ref, g_ref = kv.at[me_b, 0], kv.at[me_b, 1], qg.at[me_b, 0], qg.at[me_b, 1]
    group_of = lax.broadcasted_iota(jnp.int32, (n_dom, far_rows), 1) // SLOT
    widen = jnp.where(group_of == lax.broadcasted_iota(jnp.int32, (n_dom, far_rows), 0), 1.0, 0.0).astype(BF16)
    repeated = dot_nn(rows_ref[0].astype(F32).astype(BF16), widen)
    slot_of = lax.rem(lax.broadcasted_iota(jnp.int32, (SLOT, far_rows), 1), SLOT)
    slot = lax.broadcasted_iota(jnp.int32, (SLOT, far_rows), 0)
    row_list = jnp.sum(jnp.where(slot_of == slot, repeated, 0.0), axis=0, keepdims=True)
    node = lax.broadcasted_iota(jnp.int32, (BLOCK, far_rows), 0).astype(F32)
    hits = jnp.where(row_list == node, 1.0, 0.0)
    picks[...] = hits.astype(BF16)
    spread = hits.T.astype(BF16)
    low = lax.broadcasted_iota(jnp.int32, (BLOCK, 128), 1) < 64

    for pair in range(PAIRS):
        lanes = slice(pair * 128, pair * 128 + 128)
        phase, place = divmod(pair, PER_PHASE)
        k_own, v_own = k_ref[:, lanes], v_ref[:, lanes]
        for own, first in ((k_own, place * 256), (v_own, place * 256 + 128)):
            moved = dot_nn(spread, own).astype(BF16).reshape(n_dom, SLOT, 128)
            far_out[phase, :, :, first : first + 128] = moved

    pl.semaphore_wait(barrier, n_dom + n_blk - 2)

    core = lax.rem(me_b, 2)
    x0 = lax.rem(me_b // 2, 4)
    y0 = me_b // 8
    x_right, x_left, x_far = lax.rem(x0 + 1, 4), lax.rem(x0 + 3, 4), lax.rem(x0 + 2, 4)
    y1, other = 1 - y0, 1 - core

    def block_id(y, x, c):
        return (y * 4 + x) * 2 + c

    sibling = block_id(y0, x0, other)
    right, left = block_id(y0, x_right, core), block_id(y0, x_left, core)
    across = block_id(y1, x0, core)
    started = []

    def send(part, block, device, half=None):
        buffer = (kv, qg)[part]
        ref = buffer.at[block] if half is None else buffer.at[block, half]
        copy = pltpu.make_async_remote_copy(
            src_ref=ref,
            dst_ref=ref,
            send_sem=ag_send.at[len(started)],
            recv_sem=ag_recv.at[part, block, 0 if half is None else half],
            device_id=(me_d, device),
            device_id_type=MESH,
        )
        copy.start()
        started.append(copy)

    def arrived(part, block, half=None):
        buffer = (kv, qg)[part]
        ref = buffer.at[block] if half is None else buffer.at[block, half]
        sem = ag_recv.at[part, block, 0 if half is None else half]
        pltpu.make_async_copy(ref, ref, sem).wait()

    def gather_own(part):
        for device in (across, right, left, sibling):
            send(part, me_b, device)

    def gather_ring(part, y):
        from_left, from_right = block_id(y, x_left, core), block_id(y, x_right, core)
        arrived(part, from_left)
        send(part, from_left, right, 0)
        send(part, from_left, sibling)
        arrived(part, from_right)
        send(part, from_right, left, 1)
        send(part, from_right, sibling)

    def gather_across(part):
        block = block_id(y1, x0, core)
        arrived(part, block)
        for device in (right, left, sibling):
            send(part, block, device)

    def gather_far(part, y):
        block = block_id(y, x_far, core)
        arrived(part, block, 0)
        arrived(part, block, 1)
        send(part, block, sibling)

    gather_own(0)

    def zigzag(step, size):
        return jnp.where(lax.rem(step, 2) == 1, (step + 1) // 2, lax.rem(size - step // 2, size))

    def at_offset(dz, dy):
        z = lax.rem(me_d // 4 + dz + 16, 8)
        y = lax.rem(lax.rem(me_d, 4) + dy + 8, 4)
        return z * 4 + y

    def legs(step, way):
        along_z = step < 4
        dz = jnp.where(along_z, 4, zigzag(step - 4, 8))
        dy = jnp.where(along_z, step, 2)
        first_z = jnp.where(along_z, 2 * way, dz)
        first_y = jnp.where(dy == 2, way, dy)
        return dz, dy, first_z, first_y

    def push(source, target, send_sem, recv_sem, group):
        pltpu.make_async_remote_copy(
            src_ref=source,
            dst_ref=target,
            send_sem=send_sem,
            recv_sem=recv_sem,
            device_id=(group, me_b),
            device_id_type=MESH,
        ).start()

    def exchange(source, relay, target, send_sem, mid_sem, recv_sem, phase):
        way = 1 - 2 * phase

        def indirect(step, carry):
            dz, dy, first_z, first_y = legs(step, way)
            push(
                source.at[phase, at_offset(dz, dy)], relay.at[phase, step],
                send_sem.at[phase], mid_sem.at[phase], at_offset(first_z, first_y),
            )
            return carry

        def direct(step, carry):
            group = at_offset(zigzag(step // 3, 8), zigzag(lax.rem(step, 3), 4))
            push(source.at[phase, group], target.at[phase, me_d], send_sem.at[phase], recv_sem.at[phase], group)
            return carry

        lax.fori_loop(0, RELAYED, indirect, 0)
        lax.fori_loop(1, 21, direct, 0)

    def pass_on(relay, target, mid_sem, next_sem, recv_sem, phase):
        way = 1 - 2 * phase
        pltpu.make_async_copy(relay.at[phase], relay.at[phase], mid_sem.at[phase]).wait()

        def one(step, carry):
            dz, dy, first_z, first_y = legs(step, way)
            push(
                relay.at[phase, step], target.at[phase, at_offset(-first_z, -first_y)],
                next_sem.at[phase], recv_sem.at[phase], at_offset(dz - first_z, dy - first_y),
            )
            return carry

        lax.fori_loop(0, RELAYED, one, 0)

    def exchanged(buffer, sem, phase):
        ref = buffer.at[phase, pl.ds(0, n_dom - 1)]
        pltpu.make_async_copy(ref, ref, sem.at[phase]).wait()

    for phase in range(PHASES):
        exchange(far_out, out_relay, far_in, far_send, far_mid, far_recv, phase)

    for pair in range(PAIRS):
        lanes = slice(pair * 128, pair * 128 + 128)
        for target, source, scale in ((qst, q_ref, 0.125), (gst, g_ref, 1.0), (kst, k_ref, 0.125), (vst, v_ref, 1.0)):
            wide = source[:, lanes].astype(F32) * scale
            target[pair, 0:BLOCK, :] = jnp.where(low, wide, 0.0).astype(BF16)
            target[pair, BLOCK : 2 * BLOCK, :] = jnp.where(low, 0.0, wide).astype(BF16)
    blank = jnp.zeros((SLOT, PER_PHASE * 256), BF16)
    for phase in range(PHASES):
        far_in[phase, me_d] = blank
        ret[phase, me_d] = blank
    tile = lax.broadcasted_iota(jnp.int32, (1, near_rows), 1) // BLOCK
    hidden = jnp.full((1, near_rows), HIDDEN, F32)
    for t in range(n_blk):
        wanted = jnp.where(t < count_ref[0], order_ref[0, t], -1)
        hidden = jnp.where(tile == wanted, 0.0, hidden)
    bias[...] = hidden
    slot_group = lax.broadcasted_iota(jnp.int32, (1, far_rows), 1) // SLOT
    far_bias[...] = jnp.where(slot_group == me_d, HIDDEN, 0.0)
    peak[...] = jnp.full(peak.shape, -3e38, F32)

    def score_chip(row, y, x):
        chip = y * 4 + x
        hidden_keys = bias[:, pl.ds(pl.multiple_of(chip * 256, 256), 256)]
        lanes = pl.ds(pl.multiple_of(x * 256, 256), 256)
        for pair in range(PAIRS):
            key_rows = kv[pl.ds(2 * chip, 2), 0, :, pair * 128 : pair * 128 + 128].reshape(256, 128)
            scores = dot_nt(qst[pair], key_rows) + hidden_keys
            s_near[row, pair, :, lanes] = scores
            peak[row, pair] = jnp.maximum(peak[row, pair], jnp.maximum(scores[:, :128], scores[:, 128:]))

    def score_sibling(row, x):
        y = (y0, y1)[row]
        arrived(0, block_id(y, x, other))
        score_chip(row, y, x)

    def weigh(row, y):
        def one(pair, carry):
            top = jnp.max(peak[row, pair], axis=1, keepdims=True)
            exps = jnp.exp(s_near[row, pair] - top)
            narrow = exps.astype(BF16)
            p_near[row, pair] = narrow
            value_rows = kv[pl.ds(y * row_blocks, row_blocks), 1, :, lanes_of(pair)].reshape(row_keys, 128)
            m_near[row, pair] = top
            l_near[row, pair] = jnp.sum(exps, axis=1, keepdims=True)
            a_near[row, pair] = dot_nn(narrow, value_rows)
            return carry

        lax.fori_loop(0, PAIRS, one, 0)

    out_path = (out_relay, far_in, far_mid, far_next, far_recv)
    back_path = (back_relay, ret, ret_mid, ret_next, ret_recv)

    score_sibling(0, x0)
    gather_ring(0, y0)
    gather_across(0)
    score_sibling(0, x_left)
    score_sibling(0, x_right)
    gather_far(0, y0)
    pass_on(*out_path, 0)
    score_sibling(0, x_far)
    score_sibling(1, x0)
    gather_ring(0, y1)
    weigh(0, y0)
    pass_on(*out_path, 1)
    gather_far(0, y1)
    gather_own(1)
    score_sibling(1, x_left)
    score_sibling(1, x_right)
    score_sibling(1, x_far)
    weigh(1, y1)

    column = lax.broadcasted_iota(jnp.int32, (BLOCK, 128), 1)

    def far_pair(phase, place):
        pair = phase * PER_PHASE + place
        lanes = lanes_of(pair)
        k_lanes, v_lanes = pl.ds(place * 256, 128), pl.ds(place * 256 + 128, 128)
        key_rows = far_in[phase, :, :, k_lanes].reshape(far_rows, 128)
        value_rows = far_in[phase, :, :, v_lanes].reshape(far_rows, 128)
        queries, cotangent = qst[pair], gst[pair]
        scores = dot_nt(queries, key_rows) + far_bias[...]
        moves = dot_nt(cotangent, value_rows)
        top = jnp.max(scores, axis=1, keepdims=True)
        exps = jnp.exp(scores - top)
        total = jnp.sum(exps, axis=1, keepdims=True)
        far_att = dot_nn(exps.astype(BF16), value_rows)
        top0, top1 = m_near[0, pair], m_near[1, pair]
        highest = jnp.maximum(top, jnp.maximum(top0, top1))
        scale0, scale1 = jnp.exp(top0 - highest), jnp.exp(top1 - highest)
        far_scale = jnp.exp(top - highest)
        whole = scale0 * l_near[0, pair] + scale1 * l_near[1, pair] + far_scale * total
        scale0, scale1, far_scale = scale0 / whole, scale1 / whole, far_scale / whole
        out = a_near[0, pair] * scale0 + a_near[1, pair] * scale1 + far_att * far_scale
        attended = jnp.where(low, out[:BLOCK], out[BLOCK:]).astype(BF16)
        att_ref[:, lanes] = attended
        product = g_ref[:, lanes].astype(F32) * attended.astype(F32)
        delta0 = jnp.sum(jnp.where(low, product, 0.0), axis=1, keepdims=True)
        delta1 = jnp.sum(jnp.where(low, 0.0, product), axis=1, keepdims=True)
        delta = jnp.concatenate([delta0, delta1], axis=0)
        log_total = highest + jnp.log(whole)
        chances = exps * far_scale
        weights = chances.astype(BF16)
        slopes = (chances * (moves - delta)).astype(BF16)
        terms[phase, :, :, k_lanes] = dot_tn(slopes, queries).astype(BF16).reshape(n_dom, SLOT, 128)
        terms[phase, :, :, v_lanes] = dot_tn(weights, cotangent).astype(BF16).reshape(n_dom, SLOT, 128)
        far_dq[pair] = dot_nn(slopes, key_rows)
        factor[0, pair] = scale0
        factor[1, pair] = scale1
        delta_ref[pair] = delta
        held = stat_cols[...]
        held = jnp.where(column == 2 * pair, log_total[:BLOCK], held)
        held = jnp.where(column == 2 * pair + 1, log_total[BLOCK:], held)
        held = jnp.where(column == HEADS + 2 * pair, delta0, held)
        held = jnp.where(column == HEADS + 2 * pair + 1, delta1, held)
        stat_cols[...] = held

    stat_cols[...] = jnp.zeros((BLOCK, 128), F32)
    for phase in range(PHASES):
        exchanged(far_in, far_recv, phase)
        for place in range(PER_PHASE):
            far_pair(phase, place)
        exchange(terms, back_relay, ret, ret_send, ret_mid, ret_recv, phase)
        if phase == 0:
            gather_ring(1, y0)
            gather_across(1)

    stat_rows = stat_cols[...].T
    for block in range(n_blk):
        row = bias[:, block * BLOCK : (block + 1) * BLOCK]
        stats_out[block, 0:HEADS, :] = stat_rows[0:HEADS] - row
        stats_out[block, HEADS : 2 * HEADS, :] = stat_rows[HEADS : 2 * HEADS]
    stats_in[me_b] = stats_out[me_b]

    def tell(step, carry):
        block = lax.rem(me_b + step, n_blk)
        pltpu.make_async_remote_copy(
            src_ref=stats_out.at[block],
            dst_ref=stats_in.at[me_b],
            send_sem=stat_send.at[0],
            recv_sem=stat_recv.at[0],
            device_id=(me_d, block),
            device_id_type=MESH,
        ).start()
        return carry

    lax.fori_loop(1, n_blk, tell, 0)

    def query_pair(pair, carry):
        lanes = lanes_of(pair)
        cotangent, delta = gst[pair], delta_ref[pair]
        both = far_dq[pair]
        for row, y in enumerate((y0, y1)):
            blocks = pl.ds(y * row_blocks, row_blocks)
            key_rows = kv[blocks, 0, :, lanes].reshape(row_keys, 128)
            value_rows = kv[blocks, 1, :, lanes].reshape(row_keys, 128)
            moves = dot_nt(cotangent, value_rows)
            slopes = (p_near[row, pair].astype(F32) * (moves - delta)).astype(BF16)
            both += dot_nn(slopes, key_rows) * factor[row, pair]
        both *= 0.125
        dq_ref[:, lanes] = jnp.where(low, both[:BLOCK], both[BLOCK:]).astype(BF16)
        return carry

    gather_far(1, y0)
    lax.fori_loop(0, 2, query_pair, 0)
    pass_on(*back_path, 0)
    lax.fori_loop(2, 3, query_pair, 0)
    pass_on(*back_path, 1)
    gather_ring(1, y1)
    lax.fori_loop(3, PAIRS, query_pair, 0)
    gather_far(1, y1)

    def written(number, source, target):
        return pltpu.make_async_copy(source, target, out_sem.at[number])

    att_copy, dq_copy = written(0, att_ref, att_out), written(1, dq_ref, dq_out)
    att_copy.start()
    dq_copy.start()

    all_stats = stats_in.at[pl.ds(0, n_blk - 1)]
    pltpu.make_async_copy(all_stats, all_stats, stat_recv.at[0]).wait()

    def key_pair(row, y, pair, carry):
        lanes = lanes_of(pair)
        own_keys, own_values = kst[pair], vst[pair]

        def stat_row(start, row):
            return jnp.concatenate([stats_in[y * row_blocks + start + n, pl.ds(row, 1), :] for n in range(4)], axis=1)

        sum_k = sum_v = jnp.zeros((256, 128), F32)
        for start in range(0, row_blocks, 4):
            blocks = pl.ds(y * row_blocks + start, 4)
            query_rows = qg[blocks, 0, :, lanes].reshape(4 * BLOCK, 128)
            grad_rows = qg[blocks, 1, :, lanes].reshape(4 * BLOCK, 128)
            scores = dot_nt(own_keys, query_rows)
            moves = dot_nt(own_values, grad_rows)
            weights, slopes = [], []
            for head in range(2):
                rows = slice(head * BLOCK, head * BLOCK + BLOCK)
                chances = jnp.exp(scores[rows] - stat_row(start, 2 * pair + head))
                weights.append(chances.astype(BF16))
                slopes.append((chances * (moves[rows] - stat_row(start, HEADS + 2 * pair + head))).astype(BF16))
            sum_k += dot_nn(jnp.concatenate(slopes, axis=0), query_rows)
            sum_v += dot_nn(jnp.concatenate(weights, axis=0), grad_rows)
        own_dk = jnp.where(low, sum_k[:BLOCK], sum_k[BLOCK:])
        own_dv = jnp.where(low, sum_v[:BLOCK], sum_v[BLOCK:])
        near_dk[pair] = own_dk if row == 0 else near_dk[pair] + own_dk
        near_dv[pair] = own_dv if row == 0 else near_dv[pair] + own_dv
        return carry

    def gathered(y):
        for x in (x0, x_left, x_right, x_far):
            arrived(1, block_id(y, x, other))

    gathered(y0)
    lax.fori_loop(0, PAIRS, functools.partial(key_pair, 0, y0), 0)
    gathered(y1)
    lax.fori_loop(0, PAIRS, functools.partial(key_pair, 1, y1), 0)

    for phase in range(PHASES):
        exchanged(ret, ret_recv, phase)
        for place in range(PER_PHASE):
            pair = phase * PER_PHASE + place
            cols = slice(pair * 128, pair * 128 + 128)
            hits = picks[...]
            back_k = ret[phase, :, :, place * 256 : place * 256 + 128].reshape(far_rows, 128)
            back_v = ret[phase, :, :, place * 256 + 128 : place * 256 + 256].reshape(far_rows, 128)
            dk_ref[:, cols] = (near_dk[pair] * 0.125 + dot_nn(hits, back_k)).astype(BF16)
            dv_ref[:, cols] = (near_dv[pair] + dot_nn(hits, back_v)).astype(BF16)

    dk_copy, dv_copy = written(2, dk_ref, dk_out), written(3, dv_ref, dv_out)
    dk_copy.start()
    dv_copy.start()
    for copy in started:
        copy.wait_send()
    for phase in range(PHASES):
        exchanged(far_out, far_send, phase)
        exchanged(terms, ret_send, phase)
        pltpu.make_async_copy(out_relay.at[phase], out_relay.at[phase], far_next.at[phase]).wait()
        pltpu.make_async_copy(back_relay.at[phase], back_relay.at[phase], ret_next.at[phase]).wait()
    sent_stats = stats_out.at[pl.ds(0, n_blk - 1)]
    pltpu.make_async_copy(sent_stats, sent_stats, stat_send.at[0]).wait()
    for copy in (att_copy, dq_copy, dk_copy, dv_copy):
        copy.wait()


def write_out(a, b, c, d, a_out, b_out, c_out, d_out, stage, sems):
    pairs = ((a, a_out), (b, b_out), (c, c_out), (d, d_out))
    reads = [pltpu.make_async_copy(pair[0], stage.at[n], sems.at[0, n]) for n, pair in enumerate(pairs)]
    writes = [pltpu.make_async_copy(stage.at[n], pair[1], sems.at[1, n]) for n, pair in enumerate(pairs)]
    for read in reads:
        read.start()
    for read, write in zip(reads, writes):
        read.wait()
        write.start()
    for write in writes:
        write.wait()


def on_device(n_dom, n_blk, queries, keys, values, grad_out, tile_keys, tile_count, send_rows):
    rows, width = queries.shape
    far_rows = n_dom * SLOT
    row_keys = n_blk // 2 * BLOCK
    hbm = pl.BlockSpec(memory_space=pltpu.HBM)
    smem = pl.BlockSpec(memory_space=pltpu.SMEM)
    far_shape = (PHASES, n_dom, SLOT, PER_PHASE * 256)
    stack = pltpu.VMEM((PAIRS, 256, 128), BF16)
    relay = pltpu.VMEM((PHASES, RELAYED, SLOT, PER_PHASE * 256), BF16)
    wide = pltpu.VMEM((PAIRS, 256, 128), F32)
    wide_rows = pltpu.VMEM((2, PAIRS, 256, 128), F32)
    thin = pltpu.VMEM((PAIRS, 256, 1), F32)
    thin_rows = pltpu.VMEM((2, PAIRS, 256, 1), F32)
    whole = pltpu.VMEM((rows, width), BF16)
    own = pltpu.VMEM((PAIRS, BLOCK, 128), F32)
    dma = pltpu.SemaphoreType.DMA
    held = pl.pallas_call(
        functools.partial(kernel, n_dom, n_blk),
        out_shape=[jax.ShapeDtypeStruct((rows, width), BF16)] * 4,
        in_specs=[hbm, hbm, hbm, hbm, hbm, smem, hbm],
        out_specs=[hbm] * 4,
        scratch_shapes=[
            pltpu.VMEM((n_blk, 2, BLOCK, width), BF16),
            pltpu.VMEM((n_blk, 2, BLOCK, width), BF16),
            pltpu.VMEM(far_shape, BF16),
            pltpu.VMEM(far_shape, BF16),
            pltpu.VMEM(far_shape, BF16),
            pltpu.VMEM(far_shape, BF16),
            relay, relay,
            pltpu.VMEM((n_blk, 2 * HEADS, BLOCK), F32),
            pltpu.VMEM((n_blk, 2 * HEADS, BLOCK), F32),
            pltpu.SMEM((1, n_blk), jnp.int32),
            pltpu.VMEM((1, SLOT, n_dom), jnp.int32),
            stack, stack, stack, stack,
            pltpu.VMEM((BLOCK, far_rows), BF16),
            pltpu.VMEM((1, n_blk * BLOCK), F32),
            pltpu.VMEM((1, far_rows), F32),
            pltpu.VMEM((2, PAIRS, 256, row_keys), F32),
            pltpu.VMEM((2, PAIRS, 256, row_keys), BF16),
            wide_rows,
            thin_rows, thin_rows,
            wide_rows,
            thin_rows, thin,
            wide,
            own, own,
            pltpu.VMEM((BLOCK, 128), F32),
            dma((6,)), dma((34,)), dma((2, n_blk, 2)),
            dma((PHASES,)), dma((PHASES,)), dma((PHASES,)), dma((PHASES,)),
            dma((PHASES,)), dma((PHASES,)), dma((PHASES,)), dma((PHASES,)),
            dma((1,)), dma((1,)),
            whole, whole, whole, whole, dma((4,)),
        ],
        compiler_params=pltpu.CompilerParams(
            collective_id=0, has_side_effects=True, vmem_limit_bytes=63 * 1024 * 1024
        ),
        cost_estimate=pl.CostEstimate(flops=2_500_000_000, bytes_accessed=2_000_000, transcendentals=5_000_000),
    )(queries, keys, values, grad_out, tile_keys, tile_count, send_rows.transpose(0, 2, 1))
    return pl.pallas_call(
        write_out,
        out_shape=[jax.ShapeDtypeStruct((rows, width), BF16)] * 4,
        in_specs=[hbm] * 4,
        out_specs=[hbm] * 4,
        scratch_shapes=[pltpu.VMEM((4, rows, width), BF16), dma((2, 4))],
        compiler_params=pltpu.CompilerParams(vmem_limit_bytes=63 * 1024 * 1024),
    )(*held)


def solution(mesh):
    n_dom, n_blk = mesh.shape["dom"], mesh.shape["blk"]
    both = ("dom", "blk")
    flat = P(both, None)
    return jax.shard_map(
        functools.partial(on_device, n_dom, n_blk),
        mesh=mesh,
        in_specs=(flat, flat, flat, flat, flat, P(both), P(both, None, None)),
        out_specs=(flat,) * 4,
        check_vma=False,
    )
```

```python
import functools

import jax
import jax.numpy as jnp
from jax import lax
from jax.experimental import pallas as pl
from jax.experimental.pallas import tpu as pltpu
from jax.sharding import PartitionSpec as P

HEADS = 8
PAIRS = 4
PHASES = 2
PER_PHASE = PAIRS // PHASES
BLOCK = 128
SLOT = 16
RELAYED = 11
HIDDEN = -1e30
MESH = pl.DeviceIdType.MESH
F32 = jnp.float32
BF16 = jnp.bfloat16


def dot_nn(a, b):
    return lax.dot_general(a, b, (((1,), (0,)), ((), ())), preferred_element_type=F32)


def dot_nt(a, b):
    return lax.dot_general(a, b, (((1,), (1,)), ((), ())), preferred_element_type=F32)


def dot_tn(a, b):
    return lax.dot_general(a, b, (((0,), (0,)), ((), ())), preferred_element_type=F32)


def lanes_of(pair):
    return pl.ds(pl.multiple_of(pair * 128, 128), 128)


def kernel(
    n_dom, n_blk,
    q_in, k_in, v_in, g_in, order_in, count_ref, rows_in,
    att_out, dq_out, dk_out, dv_out,
    kv, qg, far_out, far_in, terms, ret, out_relay, back_relay, stats_out, stats_in,
    order_ref, rows_ref, qst, gst, kst, vst, picks, bias, far_bias,
    s_near, p_near, peak, m_near, l_near, a_near, factor, delta_ref, far_dq, near_dk, near_dv, stat_cols,
    in_sem, ag_send, ag_recv, far_send, far_recv, far_mid, far_next, ret_send, ret_recv, ret_mid, ret_next,
    stat_send, stat_recv, att_ref, dq_ref, dk_ref, dv_ref, out_sem,
):
    me_d = lax.axis_index("dom")
    me_b = lax.axis_index("blk")
    far_rows = n_dom * SLOT
    near_rows = n_blk * BLOCK
    row_blocks = n_blk // 2
    row_keys = row_blocks * BLOCK

    loads = [
        pltpu.make_async_copy(source, target, in_sem.at[number])
        for number, (source, target) in enumerate(
            (
                (order_in, order_ref),
                (rows_in, rows_ref),
                (k_in, kv.at[me_b, 0]),
                (v_in, kv.at[me_b, 1]),
                (q_in, qg.at[me_b, 0]),
                (g_in, qg.at[me_b, 1]),
            )
        )
    ]
    for load in loads:
        load.start()

    barrier = pltpu.get_barrier_semaphore()

    def greet_dom(step, carry):
        pl.semaphore_signal(barrier, inc=1, device_id=(lax.rem(me_d + step, n_dom), me_b), device_id_type=MESH)
        return carry

    def greet_blk(step, carry):
        pl.semaphore_signal(barrier, inc=1, device_id=(me_d, lax.rem(me_b + step, n_blk)), device_id_type=MESH)
        return carry

    lax.fori_loop(1, n_blk, greet_blk, 0)
    lax.fori_loop(1, n_dom, greet_dom, 0)

    for load in loads[2:4]:
        load.wait()
    k_ref, v_ref, q_ref, g_ref = kv.at[me_b, 0], kv.at[me_b, 1], qg.at[me_b, 0], qg.at[me_b, 1]
    pl.semaphore_wait(barrier, n_dom + n_blk - 2)

    core = lax.rem(me_b, 2)
    x0 = lax.rem(me_b // 2, 4)
    y0 = me_b // 8
    x_right, x_left, x_far = lax.rem(x0 + 1, 4), lax.rem(x0 + 3, 4), lax.rem(x0 + 2, 4)
    y1, other = 1 - y0, 1 - core

    def block_id(y, x, c):
        return (y * 4 + x) * 2 + c

    sibling = block_id(y0, x0, other)
    right, left = block_id(y0, x_right, core), block_id(y0, x_left, core)
    across = block_id(y1, x0, core)
    started = []

    def send(part, block, device, half=None):
        buffer = (kv, qg)[part]
        ref = buffer.at[block] if half is None else buffer.at[block, half]
        copy = pltpu.make_async_remote_copy(
            src_ref=ref,
            dst_ref=ref,
            send_sem=ag_send.at[len(started)],
            recv_sem=ag_recv.at[part, block, 0 if half is None else half],
            device_id=(me_d, device),
            device_id_type=MESH,
        )
        copy.start()
        started.append(copy)

    def arrived(part, block, half=None):
        buffer = (kv, qg)[part]
        ref = buffer.at[block] if half is None else buffer.at[block, half]
        sem = ag_recv.at[part, block, 0 if half is None else half]
        pltpu.make_async_copy(ref, ref, sem).wait()

    def gather_own(part):
        for device in (across, right, left, sibling):
            send(part, me_b, device)

    def gather_ring(part, y):
        from_left, from_right = block_id(y, x_left, core), block_id(y, x_right, core)
        arrived(part, from_left)
        send(part, from_left, right, 0)
        send(part, from_left, sibling)
        arrived(part, from_right)
        send(part, from_right, left, 1)
        send(part, from_right, sibling)

    def gather_across(part):
        block = block_id(y1, x0, core)
        arrived(part, block)
        for device in (right, left, sibling):
            send(part, block, device)

    def gather_far(part, y):
        block = block_id(y, x_far, core)
        arrived(part, block, 0)
        arrived(part, block, 1)
        send(part, block, sibling)

    gather_own(0)

    for load in loads[:2] + loads[4:]:
        load.wait()
    group_of = lax.broadcasted_iota(jnp.int32, (n_dom, far_rows), 1) // SLOT
    widen = jnp.where(group_of == lax.broadcasted_iota(jnp.int32, (n_dom, far_rows), 0), 1.0, 0.0).astype(BF16)
    repeated = dot_nn(rows_ref[0].astype(F32).astype(BF16), widen)
    slot_of = lax.rem(lax.broadcasted_iota(jnp.int32, (SLOT, far_rows), 1), SLOT)
    slot = lax.broadcasted_iota(jnp.int32, (SLOT, far_rows), 0)
    row_list = jnp.sum(jnp.where(slot_of == slot, repeated, 0.0), axis=0, keepdims=True)
    node = lax.broadcasted_iota(jnp.int32, (BLOCK, far_rows), 0).astype(F32)
    hits = jnp.where(row_list == node, 1.0, 0.0)
    picks[...] = hits.astype(BF16)
    spread = hits.T.astype(BF16)
    low = lax.broadcasted_iota(jnp.int32, (BLOCK, 128), 1) < 64

    for pair in range(PAIRS):
        lanes = slice(pair * 128, pair * 128 + 128)
        phase, place = divmod(pair, PER_PHASE)
        k_own, v_own = k_ref[:, lanes], v_ref[:, lanes]
        for own, first in ((k_own, place * 256), (v_own, place * 256 + 128)):
            moved = dot_nn(spread, own).astype(BF16).reshape(n_dom, SLOT, 128)
            far_out[phase, :, :, first : first + 128] = moved

    def zigzag(step, size):
        return jnp.where(lax.rem(step, 2) == 1, (step + 1) // 2, lax.rem(size - step // 2, size))

    def at_offset(dz, dy):
        z = lax.rem(me_d // 4 + dz + 16, 8)
        y = lax.rem(lax.rem(me_d, 4) + dy + 8, 4)
        return z * 4 + y

    def legs(step, way):
        along_z = step < 4
        dz = jnp.where(along_z, 4, zigzag(step - 4, 8))
        dy = jnp.where(along_z, step, 2)
        first_z = jnp.where(along_z, 2 * way, dz)
        first_y = jnp.where(dy == 2, way, dy)
        return dz, dy, first_z, first_y

    def push(source, target, send_sem, recv_sem, group):
        pltpu.make_async_remote_copy(
            src_ref=source,
            dst_ref=target,
            send_sem=send_sem,
            recv_sem=recv_sem,
            device_id=(group, me_b),
            device_id_type=MESH,
        ).start()

    def exchange(part, source, relay, target, send_sem, mid_sem, recv_sem, phase):
        way = 1 - 2 * phase

        def indirect(step, carry):
            dz, dy, first_z, first_y = legs(step, way)
            push(
                source.at[phase, at_offset(dz, dy)], relay.at[phase, step],
                send_sem.at[phase], mid_sem.at[phase], at_offset(first_z, first_y),
            )
            return carry

        def direct(step, carry):
            group = at_offset(zigzag(lax.rem(step, 7), 8), zigzag(step // 7, 4))
            push(source.at[phase, group], target.at[phase, me_d], send_sem.at[phase], recv_sem.at[phase], group)
            return carry

        if "z" in part:
            lax.fori_loop(1, 7, direct, 0)
        if "y" in part:
            lax.fori_loop(0, RELAYED, indirect, 0)
            lax.fori_loop(7, 21, direct, 0)

    def pass_on(relay, target, mid_sem, next_sem, recv_sem, phase):
        way = 1 - 2 * phase
        pltpu.make_async_copy(relay.at[phase], relay.at[phase], mid_sem.at[phase]).wait()

        def one(step, carry):
            dz, dy, first_z, first_y = legs(step, way)
            push(
                relay.at[phase, step], target.at[phase, at_offset(-first_z, -first_y)],
                next_sem.at[phase], recv_sem.at[phase], at_offset(dz - first_z, dy - first_y),
            )
            return carry

        lax.fori_loop(0, RELAYED, one, 0)

    def exchanged(buffer, sem, phase):
        ref = buffer.at[phase, pl.ds(0, n_dom - 1)]
        pltpu.make_async_copy(ref, ref, sem.at[phase]).wait()

    for part in ("z", "y"):
        for phase in range(PHASES):
            exchange(part, far_out, out_relay, far_in, far_send, far_mid, far_recv, phase)

    for pair in range(PAIRS):
        lanes = slice(pair * 128, pair * 128 + 128)
        for target, source, scale in ((qst, q_ref, 0.125), (gst, g_ref, 1.0), (kst, k_ref, 0.125), (vst, v_ref, 1.0)):
            wide = source[:, lanes].astype(F32) * scale
            target[pair, 0:BLOCK, :] = jnp.where(low, wide, 0.0).astype(BF16)
            target[pair, BLOCK : 2 * BLOCK, :] = jnp.where(low, 0.0, wide).astype(BF16)
    blank = jnp.zeros((SLOT, PER_PHASE * 256), BF16)
    for phase in range(PHASES):
        far_in[phase, me_d] = blank
        ret[phase, me_d] = blank
    tile = lax.broadcasted_iota(jnp.int32, (1, near_rows), 1) // BLOCK
    hidden = jnp.full((1, near_rows), HIDDEN, F32)
    for t in range(n_blk):
        wanted = jnp.where(t < count_ref[0], order_ref[0, t], -1)
        hidden = jnp.where(tile == wanted, 0.0, hidden)
    bias[...] = hidden
    slot_group = lax.broadcasted_iota(jnp.int32, (1, far_rows), 1) // SLOT
    far_bias[...] = jnp.where(slot_group == me_d, HIDDEN, 0.0)
    peak[...] = jnp.full(peak.shape, -3e38, F32)

    def score_chip(row, y, x):
        chip = y * 4 + x
        hidden_keys = bias[:, pl.ds(pl.multiple_of(chip * 256, 256), 256)]
        lanes = pl.ds(pl.multiple_of(x * 256, 256), 256)
        for pair in range(PAIRS):
            key_rows = kv[pl.ds(2 * chip, 2), 0, :, pair * 128 : pair * 128 + 128].reshape(256, 128)
            scores = dot_nt(qst[pair], key_rows) + hidden_keys
            s_near[row, pair, :, lanes] = scores
            peak[row, pair] = jnp.maximum(peak[row, pair], jnp.maximum(scores[:, :128], scores[:, 128:]))

    def score_sibling(row, x):
        y = (y0, y1)[row]
        arrived(0, block_id(y, x, other))
        score_chip(row, y, x)

    def weigh(row, y):
        def one(pair, carry):
            top = jnp.max(peak[row, pair], axis=1, keepdims=True)
            exps = jnp.exp(s_near[row, pair] - top)
            narrow = exps.astype(BF16)
            p_near[row, pair] = narrow
            value_rows = kv[pl.ds(y * row_blocks, row_blocks), 1, :, lanes_of(pair)].reshape(row_keys, 128)
            m_near[row, pair] = top
            l_near[row, pair] = jnp.sum(exps, axis=1, keepdims=True)
            a_near[row, pair] = dot_nn(narrow, value_rows)
            return carry

        lax.fori_loop(0, PAIRS, one, 0)

    out_path = (out_relay, far_in, far_mid, far_next, far_recv)
    back_path = (back_relay, ret, ret_mid, ret_next, ret_recv)

    score_sibling(0, x0)
    gather_ring(0, y0)
    gather_across(0)
    score_sibling(0, x_left)
    score_sibling(0, x_right)
    gather_far(0, y0)
    pass_on(*out_path, 0)
    score_sibling(0, x_far)
    score_sibling(1, x0)
    gather_ring(0, y1)
    weigh(0, y0)
    pass_on(*out_path, 1)
    gather_far(0, y1)
    gather_own(1)
    score_sibling(1, x_left)
    score_sibling(1, x_right)
    score_sibling(1, x_far)
    weigh(1, y1)

    column = lax.broadcasted_iota(jnp.int32, (BLOCK, 128), 1)

    def far_pair(phase, place):
        pair = phase * PER_PHASE + place
        lanes = lanes_of(pair)
        k_lanes, v_lanes = pl.ds(place * 256, 128), pl.ds(place * 256 + 128, 128)
        key_rows = far_in[phase, :, :, k_lanes].reshape(far_rows, 128)
        value_rows = far_in[phase, :, :, v_lanes].reshape(far_rows, 128)
        queries, cotangent = qst[pair], gst[pair]
        scores = dot_nt(queries, key_rows) + far_bias[...]
        moves = dot_nt(cotangent, value_rows)
        top = jnp.max(scores, axis=1, keepdims=True)
        exps = jnp.exp(scores - top)
        total = jnp.sum(exps, axis=1, keepdims=True)
        far_att = dot_nn(exps.astype(BF16), value_rows)
        top0, top1 = m_near[0, pair], m_near[1, pair]
        highest = jnp.maximum(top, jnp.maximum(top0, top1))
        scale0, scale1 = jnp.exp(top0 - highest), jnp.exp(top1 - highest)
        far_scale = jnp.exp(top - highest)
        whole = scale0 * l_near[0, pair] + scale1 * l_near[1, pair] + far_scale * total
        scale0, scale1, far_scale = scale0 / whole, scale1 / whole, far_scale / whole
        out = a_near[0, pair] * scale0 + a_near[1, pair] * scale1 + far_att * far_scale
        attended = jnp.where(low, out[:BLOCK], out[BLOCK:]).astype(BF16)
        att_ref[:, lanes] = attended
        product = g_ref[:, lanes].astype(F32) * attended.astype(F32)
        delta0 = jnp.sum(jnp.where(low, product, 0.0), axis=1, keepdims=True)
        delta1 = jnp.sum(jnp.where(low, 0.0, product), axis=1, keepdims=True)
        delta = jnp.concatenate([delta0, delta1], axis=0)
        log_total = highest + jnp.log(whole)
        chances = exps * far_scale
        weights = chances.astype(BF16)
        slopes = (chances * (moves - delta)).astype(BF16)
        terms[phase, :, :, k_lanes] = dot_tn(slopes, queries).astype(BF16).reshape(n_dom, SLOT, 128)
        terms[phase, :, :, v_lanes] = dot_tn(weights, cotangent).astype(BF16).reshape(n_dom, SLOT, 128)
        far_dq[pair] = dot_nn(slopes, key_rows)
        factor[0, pair] = scale0
        factor[1, pair] = scale1
        delta_ref[pair] = delta
        held = stat_cols[...]
        held = jnp.where(column == 2 * pair, log_total[:BLOCK], held)
        held = jnp.where(column == 2 * pair + 1, log_total[BLOCK:], held)
        held = jnp.where(column == HEADS + 2 * pair, delta0, held)
        held = jnp.where(column == HEADS + 2 * pair + 1, delta1, held)
        stat_cols[...] = held

    stat_cols[...] = jnp.zeros((BLOCK, 128), F32)
    for phase in range(PHASES):
        exchanged(far_in, far_recv, phase)
        for place in range(PER_PHASE):
            far_pair(phase, place)
        exchange("zy", terms, back_relay, ret, ret_send, ret_mid, ret_recv, phase)
        if phase == 0:
            gather_ring(1, y0)
            gather_across(1)

    stat_rows = stat_cols[...].T
    for block in range(n_blk):
        row = bias[:, block * BLOCK : (block + 1) * BLOCK]
        stats_out[block, 0:HEADS, :] = stat_rows[0:HEADS] - row
        stats_out[block, HEADS : 2 * HEADS, :] = stat_rows[HEADS : 2 * HEADS]
    stats_in[me_b] = stats_out[me_b]

    def tell(step, carry):
        block = lax.rem(me_b + step, n_blk)
        pltpu.make_async_remote_copy(
            src_ref=stats_out.at[block],
            dst_ref=stats_in.at[me_b],
            send_sem=stat_send.at[0],
            recv_sem=stat_recv.at[0],
            device_id=(me_d, block),
            device_id_type=MESH,
        ).start()
        return carry

    lax.fori_loop(1, n_blk, tell, 0)

    def query_pair(pair, carry):
        lanes = lanes_of(pair)
        cotangent, delta = gst[pair], delta_ref[pair]
        both = far_dq[pair]
        for row, y in enumerate((y0, y1)):
            blocks = pl.ds(y * row_blocks, row_blocks)
            key_rows = kv[blocks, 0, :, lanes].reshape(row_keys, 128)
            value_rows = kv[blocks, 1, :, lanes].reshape(row_keys, 128)
            moves = dot_nt(cotangent, value_rows)
            slopes = (p_near[row, pair].astype(F32) * (moves - delta)).astype(BF16)
            both += dot_nn(slopes, key_rows) * factor[row, pair]
        both *= 0.125
        dq_ref[:, lanes] = jnp.where(low, both[:BLOCK], both[BLOCK:]).astype(BF16)
        return carry

    gather_far(1, y0)
    lax.fori_loop(0, 2, query_pair, 0)
    pass_on(*back_path, 0)
    lax.fori_loop(2, 3, query_pair, 0)
    pass_on(*back_path, 1)
    gather_ring(1, y1)
    lax.fori_loop(3, PAIRS, query_pair, 0)
    gather_far(1, y1)

    def written(number, source, target):
        return pltpu.make_async_copy(source, target, out_sem.at[number])

    att_copy, dq_copy = written(0, att_ref, att_out), written(1, dq_ref, dq_out)
    att_copy.start()
    dq_copy.start()

    all_stats = stats_in.at[pl.ds(0, n_blk - 1)]
    pltpu.make_async_copy(all_stats, all_stats, stat_recv.at[0]).wait()

    def key_pair(row, y, pair, carry):
        lanes = lanes_of(pair)
        own_keys, own_values = kst[pair], vst[pair]

        def stat_row(start, row):
            return jnp.concatenate([stats_in[y * row_blocks + start + n, pl.ds(row, 1), :] for n in range(4)], axis=1)

        sum_k = sum_v = jnp.zeros((256, 128), F32)
        for start in range(0, row_blocks, 4):
            blocks = pl.ds(y * row_blocks + start, 4)
            query_rows = qg[blocks, 0, :, lanes].reshape(4 * BLOCK, 128)
            grad_rows = qg[blocks, 1, :, lanes].reshape(4 * BLOCK, 128)
            scores = dot_nt(own_keys, query_rows)
            moves = dot_nt(own_values, grad_rows)
            weights, slopes = [], []
            for head in range(2):
                rows = slice(head * BLOCK, head * BLOCK + BLOCK)
                chances = jnp.exp(scores[rows] - stat_row(start, 2 * pair + head))
                weights.append(chances.astype(BF16))
                slopes.append((chances * (moves[rows] - stat_row(start, HEADS + 2 * pair + head))).astype(BF16))
            sum_k += dot_nn(jnp.concatenate(slopes, axis=0), query_rows)
            sum_v += dot_nn(jnp.concatenate(weights, axis=0), grad_rows)
        own_dk = jnp.where(low, sum_k[:BLOCK], sum_k[BLOCK:])
        own_dv = jnp.where(low, sum_v[:BLOCK], sum_v[BLOCK:])
        near_dk[pair] = own_dk if row == 0 else near_dk[pair] + own_dk
        near_dv[pair] = own_dv if row == 0 else near_dv[pair] + own_dv
        return carry

    def gathered(y):
        for x in (x0, x_left, x_right, x_far):
            arrived(1, block_id(y, x, other))

    gathered(y0)
    lax.fori_loop(0, PAIRS, functools.partial(key_pair, 0, y0), 0)
    gathered(y1)
    lax.fori_loop(0, PAIRS, functools.partial(key_pair, 1, y1), 0)

    for phase in range(PHASES):
        exchanged(ret, ret_recv, phase)
        for place in range(PER_PHASE):
            pair = phase * PER_PHASE + place
            cols = slice(pair * 128, pair * 128 + 128)
            hits = picks[...]
            back_k = ret[phase, :, :, place * 256 : place * 256 + 128].reshape(far_rows, 128)
            back_v = ret[phase, :, :, place * 256 + 128 : place * 256 + 256].reshape(far_rows, 128)
            dk_ref[:, cols] = (near_dk[pair] * 0.125 + dot_nn(hits, back_k)).astype(BF16)
            dv_ref[:, cols] = (near_dv[pair] + dot_nn(hits, back_v)).astype(BF16)

    dk_copy, dv_copy = written(2, dk_ref, dk_out), written(3, dv_ref, dv_out)
    dk_copy.start()
    dv_copy.start()
    for copy in started:
        copy.wait_send()
    for phase in range(PHASES):
        exchanged(far_out, far_send, phase)
        exchanged(terms, ret_send, phase)
        pltpu.make_async_copy(out_relay.at[phase], out_relay.at[phase], far_next.at[phase]).wait()
        pltpu.make_async_copy(back_relay.at[phase], back_relay.at[phase], ret_next.at[phase]).wait()
    sent_stats = stats_out.at[pl.ds(0, n_blk - 1)]
    pltpu.make_async_copy(sent_stats, sent_stats, stat_send.at[0]).wait()
    for copy in (att_copy, dq_copy, dk_copy, dv_copy):
        copy.wait()


def write_out(a, b, c, d, a_out, b_out, c_out, d_out, stage, sems):
    pairs = ((a, a_out), (b, b_out), (c, c_out), (d, d_out))
    reads = [pltpu.make_async_copy(pair[0], stage.at[n], sems.at[0, n]) for n, pair in enumerate(pairs)]
    writes = [pltpu.make_async_copy(stage.at[n], pair[1], sems.at[1, n]) for n, pair in enumerate(pairs)]
    for read in reads:
        read.start()
    for read, write in zip(reads, writes):
        read.wait()
        write.start()
    for write in writes:
        write.wait()


def on_device(n_dom, n_blk, queries, keys, values, grad_out, tile_keys, tile_count, send_rows):
    rows, width = queries.shape
    far_rows = n_dom * SLOT
    row_keys = n_blk // 2 * BLOCK
    hbm = pl.BlockSpec(memory_space=pltpu.HBM)
    smem = pl.BlockSpec(memory_space=pltpu.SMEM)
    far_shape = (PHASES, n_dom, SLOT, PER_PHASE * 256)
    stack = pltpu.VMEM((PAIRS, 256, 128), BF16)
    relay = pltpu.VMEM((PHASES, RELAYED, SLOT, PER_PHASE * 256), BF16)
    wide = pltpu.VMEM((PAIRS, 256, 128), F32)
    wide_rows = pltpu.VMEM((2, PAIRS, 256, 128), F32)
    thin = pltpu.VMEM((PAIRS, 256, 1), F32)
    thin_rows = pltpu.VMEM((2, PAIRS, 256, 1), F32)
    whole = pltpu.VMEM((rows, width), BF16)
    own = pltpu.VMEM((PAIRS, BLOCK, 128), F32)
    dma = pltpu.SemaphoreType.DMA
    held = pl.pallas_call(
        functools.partial(kernel, n_dom, n_blk),
        out_shape=[jax.ShapeDtypeStruct((rows, width), BF16)] * 4,
        in_specs=[hbm, hbm, hbm, hbm, hbm, smem, hbm],
        out_specs=[hbm] * 4,
        scratch_shapes=[
            pltpu.VMEM((n_blk, 2, BLOCK, width), BF16),
            pltpu.VMEM((n_blk, 2, BLOCK, width), BF16),
            pltpu.VMEM(far_shape, BF16),
            pltpu.VMEM(far_shape, BF16),
            pltpu.VMEM(far_shape, BF16),
            pltpu.VMEM(far_shape, BF16),
            relay, relay,
            pltpu.VMEM((n_blk, 2 * HEADS, BLOCK), F32),
            pltpu.VMEM((n_blk, 2 * HEADS, BLOCK), F32),
            pltpu.SMEM((1, n_blk), jnp.int32),
            pltpu.VMEM((1, SLOT, n_dom), jnp.int32),
            stack, stack, stack, stack,
            pltpu.VMEM((BLOCK, far_rows), BF16),
            pltpu.VMEM((1, n_blk * BLOCK), F32),
            pltpu.VMEM((1, far_rows), F32),
            pltpu.VMEM((2, PAIRS, 256, row_keys), F32),
            pltpu.VMEM((2, PAIRS, 256, row_keys), BF16),
            wide_rows,
            thin_rows, thin_rows,
            wide_rows,
            thin_rows, thin,
            wide,
            own, own,
            pltpu.VMEM((BLOCK, 128), F32),
            dma((6,)), dma((34,)), dma((2, n_blk, 2)),
            dma((PHASES,)), dma((PHASES,)), dma((PHASES,)), dma((PHASES,)),
            dma((PHASES,)), dma((PHASES,)), dma((PHASES,)), dma((PHASES,)),
            dma((1,)), dma((1,)),
            whole, whole, whole, whole, dma((4,)),
        ],
        compiler_params=pltpu.CompilerParams(
            collective_id=0, has_side_effects=True, vmem_limit_bytes=63 * 1024 * 1024
        ),
        cost_estimate=pl.CostEstimate(flops=2_500_000_000, bytes_accessed=2_000_000, transcendentals=5_000_000),
    )(queries, keys, values, grad_out, tile_keys, tile_count, send_rows.transpose(0, 2, 1))
    return pl.pallas_call(
        write_out,
        out_shape=[jax.ShapeDtypeStruct((rows, width), BF16)] * 4,
        in_specs=[hbm] * 4,
        out_specs=[hbm] * 4,
        scratch_shapes=[pltpu.VMEM((4, rows, width), BF16), dma((2, 4))],
        compiler_params=pltpu.CompilerParams(vmem_limit_bytes=63 * 1024 * 1024),
    )(*held)


def solution(mesh):
    n_dom, n_blk = mesh.shape["dom"], mesh.shape["blk"]
    both = ("dom", "blk")
    flat = P(both, None)
    return jax.shard_map(
        functools.partial(on_device, n_dom, n_blk),
        mesh=mesh,
        in_specs=(flat, flat, flat, flat, flat, P(both), P(both, None, None)),
        out_specs=(flat,) * 4,
        check_vma=False,
    )
```

```python
import functools

import jax
import jax.numpy as jnp
from jax import lax
from jax.experimental import pallas as pl
from jax.experimental.pallas import tpu as pltpu
from jax.sharding import PartitionSpec as P

HEADS = 8
PAIRS = 4
PHASES = 2
PER_PHASE = PAIRS // PHASES
BLOCK = 128
SLOT = 16
RELAYED = 11
HIDDEN = -1e30
MESH = pl.DeviceIdType.MESH
F32 = jnp.float32
BF16 = jnp.bfloat16


def dot_nn(a, b):
    return lax.dot_general(a, b, (((1,), (0,)), ((), ())), preferred_element_type=F32)


def dot_nt(a, b):
    return lax.dot_general(a, b, (((1,), (1,)), ((), ())), preferred_element_type=F32)


def dot_tn(a, b):
    return lax.dot_general(a, b, (((0,), (0,)), ((), ())), preferred_element_type=F32)


def lanes_of(pair):
    return pl.ds(pl.multiple_of(pair * 128, 128), 128)


def kernel(
    n_dom, n_blk,
    q_in, k_in, v_in, g_in, order_in, count_ref, rows_in,
    att_out, dq_out, dk_out, dv_out,
    kv, qg, far_out, far_in, terms, ret, out_relay, back_relay, stats_out, stats_in,
    order_ref, rows_ref, qst, gst, kst, vst, picks, bias, far_bias,
    s_near, p_near, d_near, peak, m_near, l_near, a_near, factor, delta_ref, far_slopes, near_dk, near_dv, stat_cols,
    in_sem, ag_send, ag_recv, far_send, far_recv, far_mid, far_next, ret_send, ret_recv, ret_mid, ret_next,
    stat_send, stat_recv, att_ref, dq_ref, dk_ref, dv_ref, out_sem,
):
    me_d = lax.axis_index("dom")
    me_b = lax.axis_index("blk")
    far_rows = n_dom * SLOT
    near_rows = n_blk * BLOCK
    row_blocks = n_blk // 2
    row_keys = row_blocks * BLOCK

    loads = [
        pltpu.make_async_copy(source, target, in_sem.at[number])
        for number, (source, target) in enumerate(
            (
                (order_in, order_ref),
                (rows_in, rows_ref),
                (k_in, kv.at[me_b, 0]),
                (v_in, kv.at[me_b, 1]),
                (q_in, qg.at[me_b, 0]),
                (g_in, qg.at[me_b, 1]),
            )
        )
    ]
    for load in loads:
        load.start()

    barrier = pltpu.get_barrier_semaphore()

    def greet_dom(step, carry):
        pl.semaphore_signal(barrier, inc=1, device_id=(lax.rem(me_d + step, n_dom), me_b), device_id_type=MESH)
        return carry

    def greet_blk(step, carry):
        pl.semaphore_signal(barrier, inc=1, device_id=(me_d, lax.rem(me_b + step, n_blk)), device_id_type=MESH)
        return carry

    lax.fori_loop(1, n_blk, greet_blk, 0)
    lax.fori_loop(1, n_dom, greet_dom, 0)

    for load in loads[2:4]:
        load.wait()
    k_ref, v_ref, q_ref, g_ref = kv.at[me_b, 0], kv.at[me_b, 1], qg.at[me_b, 0], qg.at[me_b, 1]
    pl.semaphore_wait(barrier, n_dom + n_blk - 2)

    core = lax.rem(me_b, 2)
    x0 = lax.rem(me_b // 2, 4)
    y0 = me_b // 8
    x_right, x_left, x_far = lax.rem(x0 + 1, 4), lax.rem(x0 + 3, 4), lax.rem(x0 + 2, 4)
    y1, other = 1 - y0, 1 - core

    def block_id(y, x, c):
        return (y * 4 + x) * 2 + c

    sibling = block_id(y0, x0, other)
    right, left = block_id(y0, x_right, core), block_id(y0, x_left, core)
    across = block_id(y1, x0, core)
    started = []

    def send(part, block, device, half=None):
        buffer = (kv, qg)[part]
        ref = buffer.at[block] if half is None else buffer.at[block, half]
        copy = pltpu.make_async_remote_copy(
            src_ref=ref,
            dst_ref=ref,
            send_sem=ag_send.at[len(started)],
            recv_sem=ag_recv.at[part, block, 0 if half is None else half],
            device_id=(me_d, device),
            device_id_type=MESH,
        )
        copy.start()
        started.append(copy)

    def arrived(part, block, half=None):
        buffer = (kv, qg)[part]
        ref = buffer.at[block] if half is None else buffer.at[block, half]
        sem = ag_recv.at[part, block, 0 if half is None else half]
        pltpu.make_async_copy(ref, ref, sem).wait()

    def gather_own(part):
        for device in (across, right, left, sibling):
            send(part, me_b, device)

    def gather_ring(part, y):
        from_left, from_right = block_id(y, x_left, core), block_id(y, x_right, core)
        arrived(part, from_left)
        send(part, from_left, right, 0)
        send(part, from_left, sibling)
        arrived(part, from_right)
        send(part, from_right, left, 1)
        send(part, from_right, sibling)

    def gather_across(part):
        block = block_id(y1, x0, core)
        arrived(part, block)
        for device in (right, left, sibling):
            send(part, block, device)

    def gather_far(part, y):
        block = block_id(y, x_far, core)
        arrived(part, block, 0)
        arrived(part, block, 1)
        send(part, block, sibling)

    gather_own(0)

    for load in loads[:2] + loads[4:]:
        load.wait()
    group_of = lax.broadcasted_iota(jnp.int32, (n_dom, far_rows), 1) // SLOT
    widen = jnp.where(group_of == lax.broadcasted_iota(jnp.int32, (n_dom, far_rows), 0), 1.0, 0.0).astype(BF16)
    repeated = dot_nn(rows_ref[0].astype(F32).astype(BF16), widen)
    slot_of = lax.rem(lax.broadcasted_iota(jnp.int32, (SLOT, far_rows), 1), SLOT)
    slot = lax.broadcasted_iota(jnp.int32, (SLOT, far_rows), 0)
    row_list = jnp.sum(jnp.where(slot_of == slot, repeated, 0.0), axis=0, keepdims=True)
    node = lax.broadcasted_iota(jnp.int32, (BLOCK, far_rows), 0).astype(F32)
    hits = jnp.where(row_list == node, 1.0, 0.0)
    picks[...] = hits.astype(BF16)
    spread = hits.T.astype(BF16)
    low = lax.broadcasted_iota(jnp.int32, (BLOCK, 128), 1) < 64

    for pair in range(PAIRS):
        lanes = slice(pair * 128, pair * 128 + 128)
        phase, place = divmod(pair, PER_PHASE)
        k_own, v_own = k_ref[:, lanes], v_ref[:, lanes]
        for own, first in ((k_own, place * 256), (v_own, place * 256 + 128)):
            moved = dot_nn(spread, own).astype(BF16).reshape(n_dom, SLOT, 128)
            far_out[phase, :, :, first : first + 128] = moved

    def zigzag(step, size):
        return jnp.where(lax.rem(step, 2) == 1, (step + 1) // 2, lax.rem(size - step // 2, size))

    def at_offset(dz, dy):
        z = lax.rem(me_d // 4 + dz + 16, 8)
        y = lax.rem(lax.rem(me_d, 4) + dy + 8, 4)
        return z * 4 + y

    def legs(step, way):
        along_z = step < 4
        dz = jnp.where(along_z, 4, zigzag(step - 4, 8))
        dy = jnp.where(along_z, step, 2)
        first_z = jnp.where(along_z, 2 * way, dz)
        first_y = jnp.where(dy == 2, way, dy)
        return dz, dy, first_z, first_y

    def push(source, target, send_sem, recv_sem, group):
        pltpu.make_async_remote_copy(
            src_ref=source,
            dst_ref=target,
            send_sem=send_sem,
            recv_sem=recv_sem,
            device_id=(group, me_b),
            device_id_type=MESH,
        ).start()

    def exchange(part, source, relay, target, send_sem, mid_sem, recv_sem, phase):
        way = 1 - 2 * phase

        def indirect(step, carry):
            dz, dy, first_z, first_y = legs(step, way)
            push(
                source.at[phase, at_offset(dz, dy)], relay.at[phase, step],
                send_sem.at[phase], mid_sem.at[phase], at_offset(first_z, first_y),
            )
            return carry

        def direct(step, carry):
            group = at_offset(zigzag(lax.rem(step, 7), 8), zigzag(step // 7, 4))
            push(source.at[phase, group], target.at[phase, me_d], send_sem.at[phase], recv_sem.at[phase], group)
            return carry

        if "z" in part:
            lax.fori_loop(1, 7, direct, 0)
        if "y" in part:
            lax.fori_loop(0, RELAYED, indirect, 0)
            lax.fori_loop(7, 21, direct, 0)

    def pass_on(relay, target, mid_sem, next_sem, recv_sem, phase):
        way = 1 - 2 * phase
        pltpu.make_async_copy(relay.at[phase], relay.at[phase], mid_sem.at[phase]).wait()

        def one(step, carry):
            dz, dy, first_z, first_y = legs(step, way)
            push(
                relay.at[phase, step], target.at[phase, at_offset(-first_z, -first_y)],
                next_sem.at[phase], recv_sem.at[phase], at_offset(dz - first_z, dy - first_y),
            )
            return carry

        lax.fori_loop(0, RELAYED, one, 0)

    def exchanged(buffer, sem, phase):
        ref = buffer.at[phase, pl.ds(0, n_dom - 1)]
        pltpu.make_async_copy(ref, ref, sem.at[phase]).wait()

    for part in ("z", "y"):
        for phase in range(PHASES):
            exchange(part, far_out, out_relay, far_in, far_send, far_mid, far_recv, phase)

    for pair in range(PAIRS):
        lanes = slice(pair * 128, pair * 128 + 128)
        for target, source, scale in ((qst, q_ref, 0.125), (gst, g_ref, 1.0), (kst, k_ref, 0.125), (vst, v_ref, 1.0)):
            wide = source[:, lanes].astype(F32) * scale
            target[pair, 0:BLOCK, :] = jnp.where(low, wide, 0.0).astype(BF16)
            target[pair, BLOCK : 2 * BLOCK, :] = jnp.where(low, 0.0, wide).astype(BF16)
    blank = jnp.zeros((SLOT, PER_PHASE * 256), BF16)
    for phase in range(PHASES):
        far_in[phase, me_d] = blank
        ret[phase, me_d] = blank
    tile = lax.broadcasted_iota(jnp.int32, (1, near_rows), 1) // BLOCK
    hidden = jnp.full((1, near_rows), HIDDEN, F32)
    for t in range(n_blk):
        wanted = jnp.where(t < count_ref[0], order_ref[0, t], -1)
        hidden = jnp.where(tile == wanted, 0.0, hidden)
    bias[...] = hidden
    slot_group = lax.broadcasted_iota(jnp.int32, (1, far_rows), 1) // SLOT
    far_bias[...] = jnp.where(slot_group == me_d, HIDDEN, 0.0)
    peak[...] = jnp.full(peak.shape, -3e38, F32)

    def score_chip(row, y, x):
        chip = y * 4 + x
        hidden_keys = bias[:, pl.ds(pl.multiple_of(chip * 256, 256), 256)]
        lanes = pl.ds(pl.multiple_of(x * 256, 256), 256)
        for pair in range(PAIRS):
            key_rows = kv[pl.ds(2 * chip, 2), 0, :, pair * 128 : pair * 128 + 128].reshape(256, 128)
            scores = dot_nt(qst[pair], key_rows) + hidden_keys
            s_near[row, pair, :, lanes] = scores
            peak[row, pair] = jnp.maximum(peak[row, pair], jnp.maximum(scores[:, :128], scores[:, 128:]))

    def score_sibling(row, x):
        y = (y0, y1)[row]
        arrived(0, block_id(y, x, other))
        score_chip(row, y, x)

    def weigh(row, y):
        def one(pair, carry):
            top = jnp.max(peak[row, pair], axis=1, keepdims=True)
            exps = jnp.exp(s_near[row, pair] - top)
            narrow = exps.astype(BF16)
            p_near[row, pair] = narrow
            value_rows = kv[pl.ds(y * row_blocks, row_blocks), 1, :, lanes_of(pair)].reshape(row_keys, 128)
            m_near[row, pair] = top
            l_near[row, pair] = jnp.sum(exps, axis=1, keepdims=True)
            a_near[row, pair] = dot_nn(narrow, value_rows)
            return carry

        lax.fori_loop(0, PAIRS, one, 0)

    def move(row, y):
        def one(pair, carry):
            value_rows = kv[pl.ds(y * row_blocks, row_blocks), 1, :, lanes_of(pair)].reshape(row_keys, 128)
            d_near[row, pair] = dot_nt(gst[pair], value_rows)
            return carry

        lax.fori_loop(0, PAIRS, one, 0)

    out_path = (out_relay, far_in, far_mid, far_next, far_recv)
    back_path = (back_relay, ret, ret_mid, ret_next, ret_recv)

    score_sibling(0, x0)
    gather_ring(0, y0)
    gather_across(0)
    score_sibling(0, x_left)
    score_sibling(0, x_right)
    gather_far(0, y0)
    pass_on(*out_path, 0)
    score_sibling(0, x_far)
    score_sibling(1, x0)
    gather_ring(0, y1)
    weigh(0, y0)
    pass_on(*out_path, 1)
    gather_far(0, y1)
    gather_own(1)
    move(0, y0)
    score_sibling(1, x_left)
    score_sibling(1, x_right)
    score_sibling(1, x_far)
    weigh(1, y1)
    move(1, y1)

    column = lax.broadcasted_iota(jnp.int32, (BLOCK, 128), 1)

    def far_pair(phase, place):
        pair = phase * PER_PHASE + place
        lanes = lanes_of(pair)
        k_lanes, v_lanes = pl.ds(place * 256, 128), pl.ds(place * 256 + 128, 128)
        key_rows = far_in[phase, :, :, k_lanes].reshape(far_rows, 128)
        value_rows = far_in[phase, :, :, v_lanes].reshape(far_rows, 128)
        queries, cotangent = qst[pair], gst[pair]
        scores = dot_nt(queries, key_rows) + far_bias[...]
        moves = dot_nt(cotangent, value_rows)
        top = jnp.max(scores, axis=1, keepdims=True)
        exps = jnp.exp(scores - top)
        total = jnp.sum(exps, axis=1, keepdims=True)
        far_att = dot_nn(exps.astype(BF16), value_rows)
        top0, top1 = m_near[0, pair], m_near[1, pair]
        highest = jnp.maximum(top, jnp.maximum(top0, top1))
        scale0, scale1 = jnp.exp(top0 - highest), jnp.exp(top1 - highest)
        far_scale = jnp.exp(top - highest)
        whole = scale0 * l_near[0, pair] + scale1 * l_near[1, pair] + far_scale * total
        scale0, scale1, far_scale = scale0 / whole, scale1 / whole, far_scale / whole
        out = a_near[0, pair] * scale0 + a_near[1, pair] * scale1 + far_att * far_scale
        attended = jnp.where(low, out[:BLOCK], out[BLOCK:]).astype(BF16)
        att_ref[:, lanes] = attended
        product = g_ref[:, lanes].astype(F32) * attended.astype(F32)
        delta0 = jnp.sum(jnp.where(low, product, 0.0), axis=1, keepdims=True)
        delta1 = jnp.sum(jnp.where(low, 0.0, product), axis=1, keepdims=True)
        delta = jnp.concatenate([delta0, delta1], axis=0)
        log_total = highest + jnp.log(whole)
        chances = exps * far_scale
        weights = chances.astype(BF16)
        slopes = (chances * (moves - delta)).astype(BF16)
        terms[phase, :, :, k_lanes] = dot_tn(slopes, queries).astype(BF16).reshape(n_dom, SLOT, 128)
        terms[phase, :, :, v_lanes] = dot_tn(weights, cotangent).astype(BF16).reshape(n_dom, SLOT, 128)
        far_slopes[pair] = slopes
        factor[0, pair] = scale0
        factor[1, pair] = scale1
        delta_ref[pair] = delta
        held = stat_cols[...]
        held = jnp.where(column == 2 * pair, log_total[:BLOCK], held)
        held = jnp.where(column == 2 * pair + 1, log_total[BLOCK:], held)
        held = jnp.where(column == HEADS + 2 * pair, delta0, held)
        held = jnp.where(column == HEADS + 2 * pair + 1, delta1, held)
        stat_cols[...] = held

    stat_cols[...] = jnp.zeros((BLOCK, 128), F32)
    for phase in range(PHASES):
        exchanged(far_in, far_recv, phase)
        for place in range(PER_PHASE):
            far_pair(phase, place)
        exchange("zy", terms, back_relay, ret, ret_send, ret_mid, ret_recv, phase)
        if phase == 0:
            gather_ring(1, y0)
            gather_across(1)

    stat_rows = stat_cols[...].T
    for block in range(n_blk):
        row = bias[:, block * BLOCK : (block + 1) * BLOCK]
        stats_out[block, 0:HEADS, :] = stat_rows[0:HEADS] - row
        stats_out[block, HEADS : 2 * HEADS, :] = stat_rows[HEADS : 2 * HEADS]
    stats_in[me_b] = stats_out[me_b]

    def tell(step, carry):
        block = lax.rem(me_b + step, n_blk)
        pltpu.make_async_remote_copy(
            src_ref=stats_out.at[block],
            dst_ref=stats_in.at[me_b],
            send_sem=stat_send.at[0],
            recv_sem=stat_recv.at[0],
            device_id=(me_d, block),
            device_id_type=MESH,
        ).start()
        return carry

    lax.fori_loop(1, n_blk, tell, 0)

    def query_pair(pair, carry):
        lanes = lanes_of(pair)
        delta = delta_ref[pair]
        phase = pair // PER_PHASE
        first = pl.multiple_of(lax.rem(pair, PER_PHASE) * 256, 256)
        both = dot_nn(far_slopes[pair], far_in[phase, :, :, pl.ds(first, 128)].reshape(far_rows, 128))
        for row, y in enumerate((y0, y1)):
            blocks = pl.ds(y * row_blocks, row_blocks)
            key_rows = kv[blocks, 0, :, lanes].reshape(row_keys, 128)
            slopes = (p_near[row, pair].astype(F32) * (d_near[row, pair] - delta)).astype(BF16)
            both += dot_nn(slopes, key_rows) * factor[row, pair]
        both *= 0.125
        dq_ref[:, lanes] = jnp.where(low, both[:BLOCK], both[BLOCK:]).astype(BF16)
        return carry

    gather_far(1, y0)
    lax.fori_loop(0, 2, query_pair, 0)
    pass_on(*back_path, 0)
    lax.fori_loop(2, 3, query_pair, 0)
    pass_on(*back_path, 1)
    gather_ring(1, y1)
    lax.fori_loop(3, PAIRS, query_pair, 0)
    gather_far(1, y1)

    def written(number, source, target):
        return pltpu.make_async_copy(source, target, out_sem.at[number])

    att_copy, dq_copy = written(0, att_ref, att_out), written(1, dq_ref, dq_out)
    att_copy.start()
    dq_copy.start()

    all_stats = stats_in.at[pl.ds(0, n_blk - 1)]
    pltpu.make_async_copy(all_stats, all_stats, stat_recv.at[0]).wait()

    def key_pair(row, y, pair, carry):
        lanes = lanes_of(pair)
        own_keys, own_values = kst[pair], vst[pair]

        def stat_row(start, row):
            return jnp.concatenate([stats_in[y * row_blocks + start + n, pl.ds(row, 1), :] for n in range(4)], axis=1)

        sum_k = sum_v = jnp.zeros((256, 128), F32)
        for start in range(0, row_blocks, 4):
            blocks = pl.ds(y * row_blocks + start, 4)
            query_rows = qg[blocks, 0, :, lanes].reshape(4 * BLOCK, 128)
            grad_rows = qg[blocks, 1, :, lanes].reshape(4 * BLOCK, 128)
            scores = dot_nt(own_keys, query_rows)
            moves = dot_nt(own_values, grad_rows)
            weights, slopes = [], []
            for head in range(2):
                rows = slice(head * BLOCK, head * BLOCK + BLOCK)
                chances = jnp.exp(scores[rows] - stat_row(start, 2 * pair + head))
                weights.append(chances.astype(BF16))
                slopes.append((chances * (moves[rows] - stat_row(start, HEADS + 2 * pair + head))).astype(BF16))
            sum_k += dot_nn(jnp.concatenate(slopes, axis=0), query_rows)
            sum_v += dot_nn(jnp.concatenate(weights, axis=0), grad_rows)
        own_dk = jnp.where(low, sum_k[:BLOCK], sum_k[BLOCK:])
        own_dv = jnp.where(low, sum_v[:BLOCK], sum_v[BLOCK:])
        near_dk[pair] = own_dk if row == 0 else near_dk[pair] + own_dk
        near_dv[pair] = own_dv if row == 0 else near_dv[pair] + own_dv
        return carry

    def gathered(y):
        for x in (x0, x_left, x_right, x_far):
            arrived(1, block_id(y, x, other))

    gathered(y0)
    lax.fori_loop(0, PAIRS, functools.partial(key_pair, 0, y0), 0)
    gathered(y1)
    lax.fori_loop(0, PAIRS, functools.partial(key_pair, 1, y1), 0)

    for phase in range(PHASES):
        exchanged(ret, ret_recv, phase)
        for place in range(PER_PHASE):
            pair = phase * PER_PHASE + place
            cols = slice(pair * 128, pair * 128 + 128)
            hits = picks[...]
            back_k = ret[phase, :, :, place * 256 : place * 256 + 128].reshape(far_rows, 128)
            back_v = ret[phase, :, :, place * 256 + 128 : place * 256 + 256].reshape(far_rows, 128)
            dk_ref[:, cols] = (near_dk[pair] * 0.125 + dot_nn(hits, back_k)).astype(BF16)
            dv_ref[:, cols] = (near_dv[pair] + dot_nn(hits, back_v)).astype(BF16)

    dk_copy, dv_copy = written(2, dk_ref, dk_out), written(3, dv_ref, dv_out)
    dk_copy.start()
    dv_copy.start()
    for copy in started:
        copy.wait_send()
    for phase in range(PHASES):
        exchanged(far_out, far_send, phase)
        exchanged(terms, ret_send, phase)
        pltpu.make_async_copy(out_relay.at[phase], out_relay.at[phase], far_next.at[phase]).wait()
        pltpu.make_async_copy(back_relay.at[phase], back_relay.at[phase], ret_next.at[phase]).wait()
    sent_stats = stats_out.at[pl.ds(0, n_blk - 1)]
    pltpu.make_async_copy(sent_stats, sent_stats, stat_send.at[0]).wait()
    for copy in (att_copy, dq_copy, dk_copy, dv_copy):
        copy.wait()


def write_out(a, b, c, d, a_out, b_out, c_out, d_out, stage, sems):
    pairs = ((a, a_out), (b, b_out), (c, c_out), (d, d_out))
    reads = [pltpu.make_async_copy(pair[0], stage.at[n], sems.at[0, n]) for n, pair in enumerate(pairs)]
    writes = [pltpu.make_async_copy(stage.at[n], pair[1], sems.at[1, n]) for n, pair in enumerate(pairs)]
    for read in reads:
        read.start()
    for read, write in zip(reads, writes):
        read.wait()
        write.start()
    for write in writes:
        write.wait()


def on_device(n_dom, n_blk, queries, keys, values, grad_out, tile_keys, tile_count, send_rows):
    rows, width = queries.shape
    far_rows = n_dom * SLOT
    row_keys = n_blk // 2 * BLOCK
    hbm = pl.BlockSpec(memory_space=pltpu.HBM)
    smem = pl.BlockSpec(memory_space=pltpu.SMEM)
    far_shape = (PHASES, n_dom, SLOT, PER_PHASE * 256)
    stack = pltpu.VMEM((PAIRS, 256, 128), BF16)
    relay = pltpu.VMEM((PHASES, RELAYED, SLOT, PER_PHASE * 256), BF16)
    wide = pltpu.VMEM((PAIRS, 256, 128), F32)
    wide_rows = pltpu.VMEM((2, PAIRS, 256, 128), F32)
    thin = pltpu.VMEM((PAIRS, 256, 1), F32)
    thin_rows = pltpu.VMEM((2, PAIRS, 256, 1), F32)
    whole = pltpu.VMEM((rows, width), BF16)
    own = pltpu.VMEM((PAIRS, BLOCK, 128), F32)
    dma = pltpu.SemaphoreType.DMA
    held = pl.pallas_call(
        functools.partial(kernel, n_dom, n_blk),
        out_shape=[jax.ShapeDtypeStruct((rows, width), BF16)] * 4,
        in_specs=[hbm, hbm, hbm, hbm, hbm, smem, hbm],
        out_specs=[hbm] * 4,
        scratch_shapes=[
            pltpu.VMEM((n_blk, 2, BLOCK, width), BF16),
            pltpu.VMEM((n_blk, 2, BLOCK, width), BF16),
            pltpu.VMEM(far_shape, BF16),
            pltpu.VMEM(far_shape, BF16),
            pltpu.VMEM(far_shape, BF16),
            pltpu.VMEM(far_shape, BF16),
            relay, relay,
            pltpu.VMEM((n_blk, 2 * HEADS, BLOCK), F32),
            pltpu.VMEM((n_blk, 2 * HEADS, BLOCK), F32),
            pltpu.SMEM((1, n_blk), jnp.int32),
            pltpu.VMEM((1, SLOT, n_dom), jnp.int32),
            stack, stack, stack, stack,
            pltpu.VMEM((BLOCK, far_rows), BF16),
            pltpu.VMEM((1, n_blk * BLOCK), F32),
            pltpu.VMEM((1, far_rows), F32),
            pltpu.VMEM((2, PAIRS, 256, row_keys), F32),
            pltpu.VMEM((2, PAIRS, 256, row_keys), BF16),
            pltpu.VMEM((2, PAIRS, 256, row_keys), F32),
            wide_rows,
            thin_rows, thin_rows,
            wide_rows,
            thin_rows, thin,
            pltpu.VMEM((PAIRS, 256, far_rows), BF16),
            own, own,
            pltpu.VMEM((BLOCK, 128), F32),
            dma((6,)), dma((34,)), dma((2, n_blk, 2)),
            dma((PHASES,)), dma((PHASES,)), dma((PHASES,)), dma((PHASES,)),
            dma((PHASES,)), dma((PHASES,)), dma((PHASES,)), dma((PHASES,)),
            dma((1,)), dma((1,)),
            whole, whole, whole, whole, dma((4,)),
        ],
        compiler_params=pltpu.CompilerParams(
            collective_id=0, has_side_effects=True, vmem_limit_bytes=63 * 1024 * 1024
        ),
        cost_estimate=pl.CostEstimate(flops=2_500_000_000, bytes_accessed=2_000_000, transcendentals=5_000_000),
    )(queries, keys, values, grad_out, tile_keys, tile_count, send_rows.transpose(0, 2, 1))
    return pl.pallas_call(
        write_out,
        out_shape=[jax.ShapeDtypeStruct((rows, width), BF16)] * 4,
        in_specs=[hbm] * 4,
        out_specs=[hbm] * 4,
        scratch_shapes=[pltpu.VMEM((4, rows, width), BF16), dma((2, 4))],
        compiler_params=pltpu.CompilerParams(vmem_limit_bytes=63 * 1024 * 1024),
    )(*held)


def solution(mesh):
    n_dom, n_blk = mesh.shape["dom"], mesh.shape["blk"]
    both = ("dom", "blk")
    flat = P(both, None)
    return jax.shard_map(
        functools.partial(on_device, n_dom, n_blk),
        mesh=mesh,
        in_specs=(flat, flat, flat, flat, flat, P(both), P(both, None, None)),
        out_specs=(flat,) * 4,
        check_vma=False,
    )
```

```python
import functools

import jax
import jax.numpy as jnp
from jax import lax
from jax.experimental import pallas as pl
from jax.experimental.pallas import tpu as pltpu
from jax.sharding import PartitionSpec as P

HEADS = 8
PAIRS = 4
PHASES = 2
PER_PHASE = PAIRS // PHASES
BLOCK = 128
SLOT = 16
RELAYED = 11
STRIP = 16
HIDDEN = -1e30
MESH = pl.DeviceIdType.MESH
F32 = jnp.float32
BF16 = jnp.bfloat16


def dot_nn(a, b):
    return lax.dot_general(a, b, (((1,), (0,)), ((), ())), preferred_element_type=F32)


def dot_nt(a, b):
    return lax.dot_general(a, b, (((1,), (1,)), ((), ())), preferred_element_type=F32)


def dot_tn(a, b):
    return lax.dot_general(a, b, (((0,), (0,)), ((), ())), preferred_element_type=F32)


def lanes_of(pair):
    return pl.ds(pl.multiple_of(pair * 128, 128), 128)


def kernel(
    n_dom, n_blk,
    q_in, k_in, v_in, g_in, order_in, count_ref, rows_in,
    att_out, dq_out, dk_out, dv_out,
    kv, qg, far_out, far_in, terms, ret, out_relay, back_relay, stats_out, stats_in,
    order_ref, rows_ref, qst, gst, kst, vst, picks, bias, far_bias,
    s_near, p_near, wide_a, wide_b, thin_a, thin_b, peak, m_near, l_near, a_near, factor, delta_ref, far_dq, near_dk, near_dv, stat_cols,
    in_sem, ag_send, ag_recv, far_send, far_recv, far_mid, far_next, ret_send, ret_recv, ret_mid, ret_next,
    stat_send, stat_recv, att_ref, dq_ref, dk_ref, dv_ref, out_sem,
):
    me_d = lax.axis_index("dom")
    me_b = lax.axis_index("blk")
    far_rows = n_dom * SLOT
    near_rows = n_blk * BLOCK
    row_blocks = n_blk // 2
    row_keys = row_blocks * BLOCK

    barrier = pltpu.get_barrier_semaphore()

    def greet_dom(step, carry):
        pl.semaphore_signal(barrier, inc=1, device_id=(lax.rem(me_d + step, n_dom), me_b), device_id_type=MESH)
        return carry

    def greet_blk(step, carry):
        pl.semaphore_signal(barrier, inc=1, device_id=(me_d, lax.rem(me_b + step, n_blk)), device_id_type=MESH)
        return carry

    lax.fori_loop(1, n_blk, greet_blk, 0)
    lax.fori_loop(1, n_dom, greet_dom, 0)

    loads = [
        pltpu.make_async_copy(source, target, in_sem.at[number])
        for number, (source, target) in enumerate(
            (
                (order_in, order_ref),
                (rows_in, rows_ref),
                (k_in, kv.at[me_b, 0]),
                (v_in, kv.at[me_b, 1]),
                (q_in, qg.at[me_b, 0]),
                (g_in, qg.at[me_b, 1]),
            )
        )
    ]
    for load in loads:
        load.start()
    for load in loads:
        load.wait()
    k_ref, v_ref, q_ref, g_ref = kv.at[me_b, 0], kv.at[me_b, 1], qg.at[me_b, 0], qg.at[me_b, 1]
    group_of = lax.broadcasted_iota(jnp.int32, (n_dom, far_rows), 1) // SLOT
    widen = jnp.where(group_of == lax.broadcasted_iota(jnp.int32, (n_dom, far_rows), 0), 1.0, 0.0).astype(BF16)
    repeated = dot_nn(rows_ref[0].astype(F32).astype(BF16), widen)
    slot_of = lax.rem(lax.broadcasted_iota(jnp.int32, (SLOT, far_rows), 1), SLOT)
    slot = lax.broadcasted_iota(jnp.int32, (SLOT, far_rows), 0)
    row_list = jnp.sum(jnp.where(slot_of == slot, repeated, 0.0), axis=0, keepdims=True)
    node = lax.broadcasted_iota(jnp.int32, (BLOCK, far_rows), 0).astype(F32)
    hits = jnp.where(row_list == node, 1.0, 0.0)
    picks[...] = hits.astype(BF16)
    spread = hits.T.astype(BF16)
    low = lax.broadcasted_iota(jnp.int32, (BLOCK, 128), 1) < 64

    for pair in range(PAIRS):
        lanes = slice(pair * 128, pair * 128 + 128)
        phase, place = divmod(pair, PER_PHASE)
        k_own, v_own = k_ref[:, lanes], v_ref[:, lanes]
        for own, first in ((k_own, place * 256), (v_own, place * 256 + 128)):
            moved = dot_nn(spread, own).astype(BF16).reshape(n_dom, SLOT, 128)
            far_out[phase, :, :, first : first + 128] = moved

    pl.semaphore_wait(barrier, n_dom + n_blk - 2)

    core = lax.rem(me_b, 2)
    x0 = lax.rem(me_b // 2, 4)
    y0 = me_b // 8
    x_right, x_left, x_far = lax.rem(x0 + 1, 4), lax.rem(x0 + 3, 4), lax.rem(x0 + 2, 4)
    y1, other = 1 - y0, 1 - core

    def block_id(y, x, c):
        return (y * 4 + x) * 2 + c

    sibling = block_id(y0, x0, other)
    right, left = block_id(y0, x_right, core), block_id(y0, x_left, core)
    across = block_id(y1, x0, core)
    started = []

    def send(part, block, device, half=None):
        buffer = (kv, qg)[part]
        ref = buffer.at[block] if half is None else buffer.at[block, half]
        copy = pltpu.make_async_remote_copy(
            src_ref=ref,
            dst_ref=ref,
            send_sem=ag_send.at[len(started)],
            recv_sem=ag_recv.at[part, block, 0 if half is None else half],
            device_id=(me_d, device),
            device_id_type=MESH,
        )
        copy.start()
        started.append(copy)

    def arrived(part, block, half=None):
        buffer = (kv, qg)[part]
        ref = buffer.at[block] if half is None else buffer.at[block, half]
        sem = ag_recv.at[part, block, 0 if half is None else half]
        pltpu.make_async_copy(ref, ref, sem).wait()

    def gather_own(part):
        for device in (across, right, left, sibling):
            send(part, me_b, device)

    def gather_ring(part, y):
        from_left, from_right = block_id(y, x_left, core), block_id(y, x_right, core)
        arrived(part, from_left)
        send(part, from_left, right, 0)
        send(part, from_left, sibling)
        arrived(part, from_right)
        send(part, from_right, left, 1)
        send(part, from_right, sibling)

    def gather_across(part):
        block = block_id(y1, x0, core)
        arrived(part, block)
        for device in (right, left, sibling):
            send(part, block, device)

    def gather_far(part, y):
        block = block_id(y, x_far, core)
        arrived(part, block, 0)
        arrived(part, block, 1)
        send(part, block, sibling)

    gather_own(0)

    def zigzag(step, size):
        return jnp.where(lax.rem(step, 2) == 1, (step + 1) // 2, lax.rem(size - step // 2, size))

    def at_offset(dz, dy):
        z = lax.rem(me_d // 4 + dz + 16, 8)
        y = lax.rem(lax.rem(me_d, 4) + dy + 8, 4)
        return z * 4 + y

    def legs(step, way):
        along_z = step < 4
        dz = jnp.where(along_z, 4, zigzag(step - 4, 8))
        dy = jnp.where(along_z, step, 2)
        first_z = jnp.where(along_z, 2 * way, dz)
        first_y = jnp.where(dy == 2, way, dy)
        return dz, dy, first_z, first_y

    def push(source, target, send_sem, recv_sem, group):
        pltpu.make_async_remote_copy(
            src_ref=source,
            dst_ref=target,
            send_sem=send_sem,
            recv_sem=recv_sem,
            device_id=(group, me_b),
            device_id_type=MESH,
        ).start()

    def exchange(source, relay, target, send_sem, mid_sem, recv_sem, phase):
        way = 1 - 2 * phase

        def indirect(step, carry):
            dz, dy, first_z, first_y = legs(step, way)
            push(
                source.at[phase, at_offset(dz, dy)], relay.at[phase, step],
                send_sem.at[phase], mid_sem.at[phase], at_offset(first_z, first_y),
            )
            return carry

        def direct(step, carry):
            group = at_offset(zigzag(step // 3, 8), zigzag(lax.rem(step, 3), 4))
            push(source.at[phase, group], target.at[phase, me_d], send_sem.at[phase], recv_sem.at[phase], group)
            return carry

        lax.fori_loop(0, RELAYED, indirect, 0)
        lax.fori_loop(1, 21, direct, 0)

    def pass_on(relay, target, mid_sem, next_sem, recv_sem, phase):
        way = 1 - 2 * phase
        pltpu.make_async_copy(relay.at[phase], relay.at[phase], mid_sem.at[phase]).wait()

        def one(step, carry):
            dz, dy, first_z, first_y = legs(step, way)
            push(
                relay.at[phase, step], target.at[phase, at_offset(-first_z, -first_y)],
                next_sem.at[phase], recv_sem.at[phase], at_offset(dz - first_z, dy - first_y),
            )
            return carry

        lax.fori_loop(0, RELAYED, one, 0)

    def exchanged(buffer, sem, phase):
        ref = buffer.at[phase, pl.ds(0, n_dom - 1)]
        pltpu.make_async_copy(ref, ref, sem.at[phase]).wait()

    for phase in range(PHASES):
        exchange(far_out, out_relay, far_in, far_send, far_mid, far_recv, phase)

    for pair in range(PAIRS):
        lanes = slice(pair * 128, pair * 128 + 128)
        for target, source, scale in ((qst, q_ref, 0.125), (gst, g_ref, 1.0), (kst, k_ref, 0.125), (vst, v_ref, 1.0)):
            wide = source[:, lanes].astype(F32) * scale
            target[pair, 0:BLOCK, :] = jnp.where(low, wide, 0.0).astype(BF16)
            target[pair, BLOCK : 2 * BLOCK, :] = jnp.where(low, 0.0, wide).astype(BF16)
    blank = jnp.zeros((SLOT, PER_PHASE * 256), BF16)
    for phase in range(PHASES):
        far_in[phase, me_d] = blank
        ret[phase, me_d] = blank
    tile = lax.broadcasted_iota(jnp.int32, (1, near_rows), 1) // BLOCK
    hidden = jnp.full((1, near_rows), HIDDEN, F32)
    for t in range(n_blk):
        wanted = jnp.where(t < count_ref[0], order_ref[0, t], -1)
        hidden = jnp.where(tile == wanted, 0.0, hidden)
    bias[...] = hidden
    slot_group = lax.broadcasted_iota(jnp.int32, (1, far_rows), 1) // SLOT
    far_bias[...] = jnp.where(slot_group == me_d, HIDDEN, 0.0)
    peak[...] = jnp.full(peak.shape, -3e38, F32)

    def score_chip(row, y, x):
        chip = y * 4 + x
        hidden_keys = bias[:, pl.ds(pl.multiple_of(chip * 256, 256), 256)]
        lanes = pl.ds(pl.multiple_of(x * 256, 256), 256)
        for pair in range(PAIRS):
            key_rows = kv[pl.ds(2 * chip, 2), 0, :, pair * 128 : pair * 128 + 128].reshape(256, 128)
            scores = dot_nt(qst[pair], key_rows) + hidden_keys
            s_near[row, pair, :, lanes] = scores
            peak[row, pair] = jnp.maximum(peak[row, pair], jnp.maximum(scores[:, :128], scores[:, 128:]))

    def score_sibling(row, x):
        y = (y0, y1)[row]
        arrived(0, block_id(y, x, other))
        score_chip(row, y, x)

    def weigh(row, y):
        def one(pair, carry):
            top = jnp.max(peak[row, pair], axis=1, keepdims=True)
            m_near[row, pair] = top
            for first in range(0, 256, STRIP):
                strip = slice(first, first + STRIP)
                exps = jnp.exp(s_near[row, pair, strip, :] - top[strip])
                p_near[row, pair, strip, :] = exps.astype(BF16)
                l_near[row, pair, strip, :] = jnp.sum(exps, axis=1, keepdims=True)
            value_rows = kv[pl.ds(y * row_blocks, row_blocks), 1, :, lanes_of(pair)].reshape(row_keys, 128)
            a_near[row, pair] = dot_nn(p_near[row, pair], value_rows)
            return carry

        lax.fori_loop(0, PAIRS, one, 0)

    out_path = (out_relay, far_in, far_mid, far_next, far_recv)
    back_path = (back_relay, ret, ret_mid, ret_next, ret_recv)

    score_sibling(0, x0)
    gather_ring(0, y0)
    gather_across(0)
    score_sibling(0, x_left)
    score_sibling(0, x_right)
    gather_far(0, y0)
    pass_on(*out_path, 0)
    score_sibling(0, x_far)
    score_sibling(1, x0)
    gather_ring(0, y1)
    weigh(0, y0)
    pass_on(*out_path, 1)
    gather_far(0, y1)
    gather_own(1)
    score_sibling(1, x_left)
    score_sibling(1, x_right)
    score_sibling(1, x_far)
    weigh(1, y1)

    column = lax.broadcasted_iota(jnp.int32, (BLOCK, 128), 1)

    def far_pair(phase, place):
        pair = phase * PER_PHASE + place
        lanes = lanes_of(pair)
        k_lanes, v_lanes = pl.ds(place * 256, 128), pl.ds(place * 256 + 128, 128)
        key_rows = far_in[phase, :, :, k_lanes].reshape(far_rows, 128)
        value_rows = far_in[phase, :, :, v_lanes].reshape(far_rows, 128)
        queries, cotangent = qst[pair], gst[pair]
        wide_a[place, :, :far_rows] = dot_nt(queries, key_rows) + far_bias[...]
        wide_b[place, :, :far_rows] = dot_nt(cotangent, value_rows)
        strips = [slice(first, first + STRIP) for first in range(0, 256, STRIP)]
        tops, totals = [], []
        for strip in strips:
            scores = wide_a[place, strip, :far_rows]
            tops.append(jnp.max(scores, axis=1, keepdims=True))
            exps = jnp.exp(scores - tops[-1])
            totals.append(jnp.sum(exps, axis=1, keepdims=True))
            wide_a[place, strip, :far_rows] = exps
            thin_a[place, strip, :far_rows] = exps.astype(BF16)
        top, total = jnp.concatenate(tops, axis=0), jnp.concatenate(totals, axis=0)
        far_att = dot_nn(thin_a[place, :, :far_rows], value_rows)
        top0, top1 = m_near[0, pair], m_near[1, pair]
        highest = jnp.maximum(top, jnp.maximum(top0, top1))
        scale0, scale1 = jnp.exp(top0 - highest), jnp.exp(top1 - highest)
        far_scale = jnp.exp(top - highest)
        whole = scale0 * l_near[0, pair] + scale1 * l_near[1, pair] + far_scale * total
        scale0, scale1, far_scale = scale0 / whole, scale1 / whole, far_scale / whole
        out = a_near[0, pair] * scale0 + a_near[1, pair] * scale1 + far_att * far_scale
        attended = jnp.where(low, out[:BLOCK], out[BLOCK:]).astype(BF16)
        att_ref[:, lanes] = attended
        product = g_ref[:, lanes].astype(F32) * attended.astype(F32)
        delta0 = jnp.sum(jnp.where(low, product, 0.0), axis=1, keepdims=True)
        delta1 = jnp.sum(jnp.where(low, 0.0, product), axis=1, keepdims=True)
        delta = jnp.concatenate([delta0, delta1], axis=0)
        log_total = highest + jnp.log(whole)
        for strip in strips:
            chances = wide_a[place, strip, :far_rows] * far_scale[strip]
            thin_a[place, strip, :far_rows] = chances.astype(BF16)
            thin_b[place, strip, :far_rows] = (chances * (wide_b[place, strip, :far_rows] - delta[strip])).astype(BF16)
        weights, slopes = thin_a[place, :, :far_rows], thin_b[place, :, :far_rows]
        terms[phase, :, :, k_lanes] = dot_tn(slopes, queries).astype(BF16).reshape(n_dom, SLOT, 128)
        terms[phase, :, :, v_lanes] = dot_tn(weights, cotangent).astype(BF16).reshape(n_dom, SLOT, 128)
        far_dq[pair] = dot_nn(slopes, key_rows)
        factor[0, pair] = scale0
        factor[1, pair] = scale1
        delta_ref[pair] = delta
        held = stat_cols[...]
        held = jnp.where(column == 2 * pair, log_total[:BLOCK], held)
        held = jnp.where(column == 2 * pair + 1, log_total[BLOCK:], held)
        held = jnp.where(column == HEADS + 2 * pair, delta0, held)
        held = jnp.where(column == HEADS + 2 * pair + 1, delta1, held)
        stat_cols[...] = held

    stat_cols[...] = jnp.zeros((BLOCK, 128), F32)
    for phase in range(PHASES):
        exchanged(far_in, far_recv, phase)
        for place in range(PER_PHASE):
            far_pair(phase, place)
        exchange(terms, back_relay, ret, ret_send, ret_mid, ret_recv, phase)
        if phase == 0:
            gather_ring(1, y0)
            gather_across(1)

    stat_rows = stat_cols[...].T
    for block in range(n_blk):
        row = bias[:, block * BLOCK : (block + 1) * BLOCK]
        stats_out[block, 0:HEADS, :] = stat_rows[0:HEADS] - row
        stats_out[block, HEADS : 2 * HEADS, :] = stat_rows[HEADS : 2 * HEADS]
    stats_in[me_b] = stats_out[me_b]

    def tell(step, carry):
        block = lax.rem(me_b + step, n_blk)
        pltpu.make_async_remote_copy(
            src_ref=stats_out.at[block],
            dst_ref=stats_in.at[me_b],
            send_sem=stat_send.at[0],
            recv_sem=stat_recv.at[0],
            device_id=(me_d, block),
            device_id_type=MESH,
        ).start()
        return carry

    lax.fori_loop(1, n_blk, tell, 0)

    def query_pair(pair, carry):
        lanes = lanes_of(pair)
        cotangent, delta = gst[pair], delta_ref[pair]
        both = far_dq[pair]
        for row, y in enumerate((y0, y1)):
            blocks = pl.ds(y * row_blocks, row_blocks)
            key_rows = kv[blocks, 0, :, lanes].reshape(row_keys, 128)
            value_rows = kv[blocks, 1, :, lanes].reshape(row_keys, 128)
            wide_a[row] = dot_nt(cotangent, value_rows)
            for first in range(0, 256, STRIP):
                strip = slice(first, first + STRIP)
                slopes = p_near[row, pair, strip, :].astype(F32) * (wide_a[row, strip, :] - delta[strip])
                thin_a[row, strip, :] = slopes.astype(BF16)
            both += dot_nn(thin_a[row], key_rows) * factor[row, pair]
        both *= 0.125
        dq_ref[:, lanes] = jnp.where(low, both[:BLOCK], both[BLOCK:]).astype(BF16)
        return carry

    gather_far(1, y0)
    lax.fori_loop(0, 2, query_pair, 0)
    pass_on(*back_path, 0)
    lax.fori_loop(2, 3, query_pair, 0)
    pass_on(*back_path, 1)
    gather_ring(1, y1)
    lax.fori_loop(3, PAIRS, query_pair, 0)
    gather_far(1, y1)

    def written(number, source, target):
        return pltpu.make_async_copy(source, target, out_sem.at[number])

    att_copy, dq_copy = written(0, att_ref, att_out), written(1, dq_ref, dq_out)
    att_copy.start()
    dq_copy.start()

    all_stats = stats_in.at[pl.ds(0, n_blk - 1)]
    pltpu.make_async_copy(all_stats, all_stats, stat_recv.at[0]).wait()

    def key_pair(row, y, pair, carry):
        lanes = lanes_of(pair)
        own_keys, own_values = kst[pair], vst[pair]

        def stat_row(line):
            return jnp.concatenate(
                [stats_in[y * row_blocks + n, pl.ds(line, 1), :] for n in range(row_blocks)], axis=1
            )

        blocks = pl.ds(y * row_blocks, row_blocks)
        query_rows = qg[blocks, 0, :, lanes].reshape(row_keys, 128)
        grad_rows = qg[blocks, 1, :, lanes].reshape(row_keys, 128)
        wide_a[row] = dot_nt(own_keys, query_rows)
        wide_b[row] = dot_nt(own_values, grad_rows)
        for head in range(2):
            log_row, delta_row = stat_row(2 * pair + head), stat_row(HEADS + 2 * pair + head)
            for first in range(head * BLOCK, head * BLOCK + BLOCK, STRIP):
                strip = slice(first, first + STRIP)
                chances = jnp.exp(wide_a[row, strip, :] - log_row)
                thin_a[row, strip, :] = chances.astype(BF16)
                thin_b[row, strip, :] = (chances * (wide_b[row, strip, :] - delta_row)).astype(BF16)
        sum_k = dot_nn(thin_b[row], query_rows)
        sum_v = dot_nn(thin_a[row], grad_rows)
        own_dk = jnp.where(low, sum_k[:BLOCK], sum_k[BLOCK:])
        own_dv = jnp.where(low, sum_v[:BLOCK], sum_v[BLOCK:])
        near_dk[pair] = own_dk if row == 0 else near_dk[pair] + own_dk
        near_dv[pair] = own_dv if row == 0 else near_dv[pair] + own_dv
        return carry

    def gathered(y):
        for x in (x0, x_left, x_right, x_far):
            arrived(1, block_id(y, x, other))

    gathered(y0)
    lax.fori_loop(0, PAIRS, functools.partial(key_pair, 0, y0), 0)
    gathered(y1)
    lax.fori_loop(0, PAIRS, functools.partial(key_pair, 1, y1), 0)

    for phase in range(PHASES):
        exchanged(ret, ret_recv, phase)
        for place in range(PER_PHASE):
            pair = phase * PER_PHASE + place
            cols = slice(pair * 128, pair * 128 + 128)
            hits = picks[...]
            back_k = ret[phase, :, :, place * 256 : place * 256 + 128].reshape(far_rows, 128)
            back_v = ret[phase, :, :, place * 256 + 128 : place * 256 + 256].reshape(far_rows, 128)
            dk_ref[:, cols] = (near_dk[pair] * 0.125 + dot_nn(hits, back_k)).astype(BF16)
            dv_ref[:, cols] = (near_dv[pair] + dot_nn(hits, back_v)).astype(BF16)

    dk_copy, dv_copy = written(2, dk_ref, dk_out), written(3, dv_ref, dv_out)
    dk_copy.start()
    dv_copy.start()
    for copy in started:
        copy.wait_send()
    for phase in range(PHASES):
        exchanged(far_out, far_send, phase)
        exchanged(terms, ret_send, phase)
        pltpu.make_async_copy(out_relay.at[phase], out_relay.at[phase], far_next.at[phase]).wait()
        pltpu.make_async_copy(back_relay.at[phase], back_relay.at[phase], ret_next.at[phase]).wait()
    sent_stats = stats_out.at[pl.ds(0, n_blk - 1)]
    pltpu.make_async_copy(sent_stats, sent_stats, stat_send.at[0]).wait()
    for copy in (att_copy, dq_copy, dk_copy, dv_copy):
        copy.wait()


def write_out(a, b, c, d, a_out, b_out, c_out, d_out, stage, sems):
    pairs = ((a, a_out), (b, b_out), (c, c_out), (d, d_out))
    reads = [pltpu.make_async_copy(pair[0], stage.at[n], sems.at[0, n]) for n, pair in enumerate(pairs)]
    writes = [pltpu.make_async_copy(stage.at[n], pair[1], sems.at[1, n]) for n, pair in enumerate(pairs)]
    for read in reads:
        read.start()
    for read, write in zip(reads, writes):
        read.wait()
        write.start()
    for write in writes:
        write.wait()


def on_device(n_dom, n_blk, queries, keys, values, grad_out, tile_keys, tile_count, send_rows):
    rows, width = queries.shape
    far_rows = n_dom * SLOT
    row_keys = n_blk // 2 * BLOCK
    hbm = pl.BlockSpec(memory_space=pltpu.HBM)
    smem = pl.BlockSpec(memory_space=pltpu.SMEM)
    far_shape = (PHASES, n_dom, SLOT, PER_PHASE * 256)
    stack = pltpu.VMEM((PAIRS, 256, 128), BF16)
    relay = pltpu.VMEM((PHASES, RELAYED, SLOT, PER_PHASE * 256), BF16)
    wide = pltpu.VMEM((PAIRS, 256, 128), F32)
    wide_rows = pltpu.VMEM((2, PAIRS, 256, 128), F32)
    thin = pltpu.VMEM((PAIRS, 256, 1), F32)
    thin_rows = pltpu.VMEM((2, PAIRS, 256, 1), F32)
    whole = pltpu.VMEM((rows, width), BF16)
    own = pltpu.VMEM((PAIRS, BLOCK, 128), F32)
    dma = pltpu.SemaphoreType.DMA
    held = pl.pallas_call(
        functools.partial(kernel, n_dom, n_blk),
        out_shape=[jax.ShapeDtypeStruct((rows, width), BF16)] * 4,
        in_specs=[hbm, hbm, hbm, hbm, hbm, smem, hbm],
        out_specs=[hbm] * 4,
        scratch_shapes=[
            pltpu.VMEM((n_blk, 2, BLOCK, width), BF16),
            pltpu.VMEM((n_blk, 2, BLOCK, width), BF16),
            pltpu.VMEM(far_shape, BF16),
            pltpu.VMEM(far_shape, BF16),
            pltpu.VMEM(far_shape, BF16),
            pltpu.VMEM(far_shape, BF16),
            relay, relay,
            pltpu.VMEM((n_blk, 2 * HEADS, BLOCK), F32),
            pltpu.VMEM((n_blk, 2 * HEADS, BLOCK), F32),
            pltpu.SMEM((1, n_blk), jnp.int32),
            pltpu.VMEM((1, SLOT, n_dom), jnp.int32),
            stack, stack, stack, stack,
            pltpu.VMEM((BLOCK, far_rows), BF16),
            pltpu.VMEM((1, n_blk * BLOCK), F32),
            pltpu.VMEM((1, far_rows), F32),
            pltpu.VMEM((2, PAIRS, 256, row_keys), F32),
            pltpu.VMEM((2, PAIRS, 256, row_keys), BF16),
            pltpu.VMEM((2, 256, row_keys), F32),
            pltpu.VMEM((2, 256, row_keys), F32),
            pltpu.VMEM((2, 256, row_keys), BF16),
            pltpu.VMEM((2, 256, row_keys), BF16),
            wide_rows,
            thin_rows, thin_rows,
            wide_rows,
            thin_rows, thin,
            wide,
            own, own,
            pltpu.VMEM((BLOCK, 128), F32),
            dma((6,)), dma((34,)), dma((2, n_blk, 2)),
            dma((PHASES,)), dma((PHASES,)), dma((PHASES,)), dma((PHASES,)),
            dma((PHASES,)), dma((PHASES,)), dma((PHASES,)), dma((PHASES,)),
            dma((1,)), dma((1,)),
            whole, whole, whole, whole, dma((4,)),
        ],
        compiler_params=pltpu.CompilerParams(
            collective_id=0, has_side_effects=True, vmem_limit_bytes=63 * 1024 * 1024
        ),
        cost_estimate=pl.CostEstimate(flops=2_500_000_000, bytes_accessed=2_000_000, transcendentals=5_000_000),
    )(queries, keys, values, grad_out, tile_keys, tile_count, send_rows.transpose(0, 2, 1))
    return pl.pallas_call(
        write_out,
        out_shape=[jax.ShapeDtypeStruct((rows, width), BF16)] * 4,
        in_specs=[hbm] * 4,
        out_specs=[hbm] * 4,
        scratch_shapes=[pltpu.VMEM((4, rows, width), BF16), dma((2, 4))],
        compiler_params=pltpu.CompilerParams(vmem_limit_bytes=63 * 1024 * 1024),
    )(*held)


def solution(mesh):
    n_dom, n_blk = mesh.shape["dom"], mesh.shape["blk"]
    both = ("dom", "blk")
    flat = P(both, None)
    return jax.shard_map(
        functools.partial(on_device, n_dom, n_blk),
        mesh=mesh,
        in_specs=(flat, flat, flat, flat, flat, P(both), P(both, None, None)),
        out_specs=(flat,) * 4,
        check_vma=False,
    )
```

```python
import functools

import jax
import jax.numpy as jnp
from jax import lax
from jax.experimental import pallas as pl
from jax.experimental.pallas import tpu as pltpu
from jax.sharding import PartitionSpec as P

HEADS = 8
PAIRS = 4
PHASES = 2
PER_PHASE = PAIRS // PHASES
BLOCK = 128
SLOT = 16
STRIP = 16
HIDDEN = -1e30
MESH = pl.DeviceIdType.MESH
F32 = jnp.float32
BF16 = jnp.bfloat16


def dot_nn(a, b):
    return lax.dot_general(a, b, (((1,), (0,)), ((), ())), preferred_element_type=F32)


def dot_nt(a, b):
    return lax.dot_general(a, b, (((1,), (1,)), ((), ())), preferred_element_type=F32)


def dot_tn(a, b):
    return lax.dot_general(a, b, (((0,), (0,)), ((), ())), preferred_element_type=F32)


def lanes_of(pair):
    return pl.ds(pl.multiple_of(pair * 128, 128), 128)


def kernel(
    n_dom, n_blk,
    q_in, k_in, v_in, g_in, order_in, count_ref, rows_in,
    att_out, dq_out, dk_out, dv_out,
    kv, qg, far_out, far_in, terms, ret, stats_out, stats_in,
    order_ref, rows_ref, qst, gst, kst, vst, picks, bias, far_bias,
    s_near, p_near, wide_a, wide_b, thin_a, thin_b, peak, m_near, l_near, a_near, factor, delta_ref, far_dq, near_dk, near_dv, stat_cols,
    in_sem, ag_send, ag_recv, far_send, far_recv, ret_send, ret_recv,
    stat_send, stat_recv, att_ref, dq_ref, dk_ref, dv_ref, out_sem,
):
    me_d = lax.axis_index("dom")
    me_b = lax.axis_index("blk")
    far_rows = n_dom * SLOT
    near_rows = n_blk * BLOCK
    row_blocks = n_blk // 2
    row_keys = row_blocks * BLOCK

    barrier = pltpu.get_barrier_semaphore()

    def greet_dom(step, carry):
        pl.semaphore_signal(barrier, inc=1, device_id=(lax.rem(me_d + step, n_dom), me_b), device_id_type=MESH)
        return carry

    def greet_blk(step, carry):
        pl.semaphore_signal(barrier, inc=1, device_id=(me_d, lax.rem(me_b + step, n_blk)), device_id_type=MESH)
        return carry

    lax.fori_loop(1, n_blk, greet_blk, 0)
    lax.fori_loop(1, n_dom, greet_dom, 0)

    loads = [
        pltpu.make_async_copy(source, target, in_sem.at[number])
        for number, (source, target) in enumerate(
            (
                (order_in, order_ref),
                (rows_in, rows_ref),
                (k_in, kv.at[me_b, 0]),
                (v_in, kv.at[me_b, 1]),
                (q_in, qg.at[me_b, 0]),
                (g_in, qg.at[me_b, 1]),
            )
        )
    ]
    for load in loads:
        load.start()
    for load in loads:
        load.wait()
    k_ref, v_ref, q_ref, g_ref = kv.at[me_b, 0], kv.at[me_b, 1], qg.at[me_b, 0], qg.at[me_b, 1]
    group_of = lax.broadcasted_iota(jnp.int32, (n_dom, far_rows), 1) // SLOT
    widen = jnp.where(group_of == lax.broadcasted_iota(jnp.int32, (n_dom, far_rows), 0), 1.0, 0.0).astype(BF16)
    repeated = dot_nn(rows_ref[0].astype(F32).astype(BF16), widen)
    slot_of = lax.rem(lax.broadcasted_iota(jnp.int32, (SLOT, far_rows), 1), SLOT)
    slot = lax.broadcasted_iota(jnp.int32, (SLOT, far_rows), 0)
    row_list = jnp.sum(jnp.where(slot_of == slot, repeated, 0.0), axis=0, keepdims=True)
    node = lax.broadcasted_iota(jnp.int32, (BLOCK, far_rows), 0).astype(F32)
    hits = jnp.where(row_list == node, 1.0, 0.0)
    picks[...] = hits.astype(BF16)
    spread = hits.T.astype(BF16)
    low = lax.broadcasted_iota(jnp.int32, (BLOCK, 128), 1) < 64

    for pair in range(PAIRS):
        lanes = slice(pair * 128, pair * 128 + 128)
        phase, place = divmod(pair, PER_PHASE)
        k_own, v_own = k_ref[:, lanes], v_ref[:, lanes]
        for own, first in ((k_own, place * 256), (v_own, place * 256 + 128)):
            moved = dot_nn(spread, own).astype(BF16).reshape(n_dom, SLOT, 128)
            far_out[phase, :, :, first : first + 128] = moved

    pl.semaphore_wait(barrier, n_dom + n_blk - 2)

    core = lax.rem(me_b, 2)
    x0 = lax.rem(me_b // 2, 4)
    y0 = me_b // 8
    x_right, x_left, x_far = lax.rem(x0 + 1, 4), lax.rem(x0 + 3, 4), lax.rem(x0 + 2, 4)
    y1, other = 1 - y0, 1 - core

    def block_id(y, x, c):
        return (y * 4 + x) * 2 + c

    sibling = block_id(y0, x0, other)
    right, left = block_id(y0, x_right, core), block_id(y0, x_left, core)
    across = block_id(y1, x0, core)
    started = []

    def send(part, block, device, half=None):
        buffer = (kv, qg)[part]
        ref = buffer.at[block] if half is None else buffer.at[block, half]
        copy = pltpu.make_async_remote_copy(
            src_ref=ref,
            dst_ref=ref,
            send_sem=ag_send.at[len(started)],
            recv_sem=ag_recv.at[part, block, 0 if half is None else half],
            device_id=(me_d, device),
            device_id_type=MESH,
        )
        copy.start()
        started.append(copy)

    def arrived(part, block, half=None):
        buffer = (kv, qg)[part]
        ref = buffer.at[block] if half is None else buffer.at[block, half]
        sem = ag_recv.at[part, block, 0 if half is None else half]
        pltpu.make_async_copy(ref, ref, sem).wait()

    def gather_own(part):
        for device in (across, right, left, sibling):
            send(part, me_b, device)

    def gather_ring(part, y):
        from_left, from_right = block_id(y, x_left, core), block_id(y, x_right, core)
        arrived(part, from_left)
        send(part, from_left, right, 0)
        send(part, from_left, sibling)
        arrived(part, from_right)
        send(part, from_right, left, 1)
        send(part, from_right, sibling)

    def gather_across(part):
        block = block_id(y1, x0, core)
        arrived(part, block)
        for device in (right, left, sibling):
            send(part, block, device)

    def gather_far(part, y):
        block = block_id(y, x_far, core)
        arrived(part, block, 0)
        arrived(part, block, 1)
        send(part, block, sibling)

    gather_own(0)

    def zigzag(step, size):
        return jnp.where(lax.rem(step, 2) == 1, (step + 1) // 2, lax.rem(size - step // 2, size))

    def at_offset(dz, dy):
        z = lax.rem(me_d // 4 + dz + 16, 8)
        y = lax.rem(lax.rem(me_d, 4) + dy + 8, 4)
        return z * 4 + y

    def push(source, target, send_sem, recv_sem, group):
        pltpu.make_async_remote_copy(
            src_ref=source,
            dst_ref=target,
            send_sem=send_sem,
            recv_sem=recv_sem,
            device_id=(group, me_b),
            device_id_type=MESH,
        ).start()

    def exchange(source, target, send_sem, recv_sem, phase):
        def direct(step, carry):
            group = at_offset(zigzag(lax.rem(step, 8), 8), zigzag(step // 8, 4))
            push(source.at[phase, group], target.at[phase, me_d], send_sem.at[phase], recv_sem.at[phase], group)
            return carry

        lax.fori_loop(1, n_dom, direct, 0)

    def exchanged(buffer, sem, phase):
        ref = buffer.at[phase, pl.ds(0, n_dom - 1)]
        pltpu.make_async_copy(ref, ref, sem.at[phase]).wait()

    for phase in range(PHASES):
        exchange(far_out, far_in, far_send, far_recv, phase)

    for pair in range(PAIRS):
        lanes = slice(pair * 128, pair * 128 + 128)
        for target, source, scale in ((qst, q_ref, 0.125), (gst, g_ref, 1.0), (kst, k_ref, 0.125), (vst, v_ref, 1.0)):
            wide = source[:, lanes].astype(F32) * scale
            target[pair, 0:BLOCK, :] = jnp.where(low, wide, 0.0).astype(BF16)
            target[pair, BLOCK : 2 * BLOCK, :] = jnp.where(low, 0.0, wide).astype(BF16)
    blank = jnp.zeros((SLOT, PER_PHASE * 256), BF16)
    for phase in range(PHASES):
        far_in[phase, me_d] = blank
        ret[phase, me_d] = blank
    tile = lax.broadcasted_iota(jnp.int32, (1, near_rows), 1) // BLOCK
    hidden = jnp.full((1, near_rows), HIDDEN, F32)
    for t in range(n_blk):
        wanted = jnp.where(t < count_ref[0], order_ref[0, t], -1)
        hidden = jnp.where(tile == wanted, 0.0, hidden)
    bias[...] = hidden
    slot_group = lax.broadcasted_iota(jnp.int32, (1, far_rows), 1) // SLOT
    far_bias[...] = jnp.where(slot_group == me_d, HIDDEN, 0.0)
    peak[...] = jnp.full(peak.shape, -3e38, F32)

    def score_chip(row, y, x):
        chip = y * 4 + x
        hidden_keys = bias[:, pl.ds(pl.multiple_of(chip * 256, 256), 256)]
        lanes = pl.ds(pl.multiple_of(x * 256, 256), 256)
        for pair in range(PAIRS):
            key_rows = kv[pl.ds(2 * chip, 2), 0, :, pair * 128 : pair * 128 + 128].reshape(256, 128)
            scores = dot_nt(qst[pair], key_rows) + hidden_keys
            s_near[row, pair, :, lanes] = scores
            peak[row, pair] = jnp.maximum(peak[row, pair], jnp.maximum(scores[:, :128], scores[:, 128:]))

    def score_sibling(row, x):
        y = (y0, y1)[row]
        arrived(0, block_id(y, x, other))
        score_chip(row, y, x)

    def weigh(row, y):
        def one(pair, carry):
            top = jnp.max(peak[row, pair], axis=1, keepdims=True)
            m_near[row, pair] = top
            for first in range(0, 256, STRIP):
                strip = slice(first, first + STRIP)
                exps = jnp.exp(s_near[row, pair, strip, :] - top[strip])
                p_near[row, pair, strip, :] = exps.astype(BF16)
                l_near[row, pair, strip, :] = jnp.sum(exps, axis=1, keepdims=True)
            value_rows = kv[pl.ds(y * row_blocks, row_blocks), 1, :, lanes_of(pair)].reshape(row_keys, 128)
            a_near[row, pair] = dot_nn(p_near[row, pair], value_rows)
            return carry

        lax.fori_loop(0, PAIRS, one, 0)

    score_sibling(0, x0)
    gather_ring(0, y0)
    gather_across(0)
    score_sibling(0, x_left)
    score_sibling(0, x_right)
    gather_far(0, y0)
    score_sibling(0, x_far)
    score_sibling(1, x0)
    gather_ring(0, y1)
    weigh(0, y0)
    gather_far(0, y1)
    gather_own(1)
    score_sibling(1, x_left)
    score_sibling(1, x_right)
    score_sibling(1, x_far)
    weigh(1, y1)

    column = lax.broadcasted_iota(jnp.int32, (BLOCK, 128), 1)

    def far_pair(phase, place):
        pair = phase * PER_PHASE + place
        lanes = lanes_of(pair)
        k_lanes, v_lanes = pl.ds(place * 256, 128), pl.ds(place * 256 + 128, 128)
        key_rows = far_in[phase, :, :, k_lanes].reshape(far_rows, 128)
        value_rows = far_in[phase, :, :, v_lanes].reshape(far_rows, 128)
        queries, cotangent = qst[pair], gst[pair]
        wide_a[place, :, :far_rows] = dot_nt(queries, key_rows) + far_bias[...]
        wide_b[place, :, :far_rows] = dot_nt(cotangent, value_rows)
        strips = [slice(first, first + STRIP) for first in range(0, 256, STRIP)]
        tops, totals = [], []
        for strip in strips:
            scores = wide_a[place, strip, :far_rows]
            tops.append(jnp.max(scores, axis=1, keepdims=True))
            exps = jnp.exp(scores - tops[-1])
            totals.append(jnp.sum(exps, axis=1, keepdims=True))
            wide_a[place, strip, :far_rows] = exps
            thin_a[place, strip, :far_rows] = exps.astype(BF16)
        top, total = jnp.concatenate(tops, axis=0), jnp.concatenate(totals, axis=0)
        far_att = dot_nn(thin_a[place, :, :far_rows], value_rows)
        top0, top1 = m_near[0, pair], m_near[1, pair]
        highest = jnp.maximum(top, jnp.maximum(top0, top1))
        scale0, scale1 = jnp.exp(top0 - highest), jnp.exp(top1 - highest)
        far_scale = jnp.exp(top - highest)
        whole = scale0 * l_near[0, pair] + scale1 * l_near[1, pair] + far_scale * total
        scale0, scale1, far_scale = scale0 / whole, scale1 / whole, far_scale / whole
        out = a_near[0, pair] * scale0 + a_near[1, pair] * scale1 + far_att * far_scale
        attended = jnp.where(low, out[:BLOCK], out[BLOCK:]).astype(BF16)
        att_ref[:, lanes] = attended
        product = g_ref[:, lanes].astype(F32) * attended.astype(F32)
        delta0 = jnp.sum(jnp.where(low, product, 0.0), axis=1, keepdims=True)
        delta1 = jnp.sum(jnp.where(low, 0.0, product), axis=1, keepdims=True)
        delta = jnp.concatenate([delta0, delta1], axis=0)
        log_total = highest + jnp.log(whole)
        for strip in strips:
            chances = wide_a[place, strip, :far_rows] * far_scale[strip]
            thin_a[place, strip, :far_rows] = chances.astype(BF16)
            thin_b[place, strip, :far_rows] = (chances * (wide_b[place, strip, :far_rows] - delta[strip])).astype(BF16)
        weights, slopes = thin_a[place, :, :far_rows], thin_b[place, :, :far_rows]
        terms[phase, :, :, k_lanes] = dot_tn(slopes, queries).astype(BF16).reshape(n_dom, SLOT, 128)
        terms[phase, :, :, v_lanes] = dot_tn(weights, cotangent).astype(BF16).reshape(n_dom, SLOT, 128)
        far_dq[pair] = dot_nn(slopes, key_rows)
        factor[0, pair] = scale0
        factor[1, pair] = scale1
        delta_ref[pair] = delta
        held = stat_cols[...]
        held = jnp.where(column == 2 * pair, log_total[:BLOCK], held)
        held = jnp.where(column == 2 * pair + 1, log_total[BLOCK:], held)
        held = jnp.where(column == HEADS + 2 * pair, delta0, held)
        held = jnp.where(column == HEADS + 2 * pair + 1, delta1, held)
        stat_cols[...] = held

    stat_cols[...] = jnp.zeros((BLOCK, 128), F32)
    for phase in range(PHASES):
        exchanged(far_in, far_recv, phase)
        for place in range(PER_PHASE):
            far_pair(phase, place)
        exchange(terms, ret, ret_send, ret_recv, phase)
        if phase == 0:
            gather_ring(1, y0)
            gather_across(1)

    stat_rows = stat_cols[...].T
    for block in range(n_blk):
        row = bias[:, block * BLOCK : (block + 1) * BLOCK]
        stats_out[block, 0:HEADS, :] = stat_rows[0:HEADS] - row
        stats_out[block, HEADS : 2 * HEADS, :] = stat_rows[HEADS : 2 * HEADS]
    stats_in[me_b] = stats_out[me_b]

    def tell(step, carry):
        block = lax.rem(me_b + step, n_blk)
        pltpu.make_async_remote_copy(
            src_ref=stats_out.at[block],
            dst_ref=stats_in.at[me_b],
            send_sem=stat_send.at[0],
            recv_sem=stat_recv.at[0],
            device_id=(me_d, block),
            device_id_type=MESH,
        ).start()
        return carry

    lax.fori_loop(1, n_blk, tell, 0)

    def query_pair(pair, carry):
        lanes = lanes_of(pair)
        cotangent, delta = gst[pair], delta_ref[pair]
        both = far_dq[pair]
        for row, y in enumerate((y0, y1)):
            blocks = pl.ds(y * row_blocks, row_blocks)
            key_rows = kv[blocks, 0, :, lanes].reshape(row_keys, 128)
            value_rows = kv[blocks, 1, :, lanes].reshape(row_keys, 128)
            wide_a[row] = dot_nt(cotangent, value_rows)
            for first in range(0, 256, STRIP):
                strip = slice(first, first + STRIP)
                slopes = p_near[row, pair, strip, :].astype(F32) * (wide_a[row, strip, :] - delta[strip])
                thin_a[row, strip, :] = slopes.astype(BF16)
            both += dot_nn(thin_a[row], key_rows) * factor[row, pair]
        both *= 0.125
        dq_ref[:, lanes] = jnp.where(low, both[:BLOCK], both[BLOCK:]).astype(BF16)
        return carry

    gather_far(1, y0)
    lax.fori_loop(0, 3, query_pair, 0)
    gather_ring(1, y1)
    lax.fori_loop(3, PAIRS, query_pair, 0)
    gather_far(1, y1)

    def written(number, source, target):
        return pltpu.make_async_copy(source, target, out_sem.at[number])

    att_copy, dq_copy = written(0, att_ref, att_out), written(1, dq_ref, dq_out)
    att_copy.start()
    dq_copy.start()

    all_stats = stats_in.at[pl.ds(0, n_blk - 1)]
    pltpu.make_async_copy(all_stats, all_stats, stat_recv.at[0]).wait()

    def key_pair(row, y, pair, carry):
        lanes = lanes_of(pair)
        own_keys, own_values = kst[pair], vst[pair]

        def stat_row(line):
            return jnp.concatenate(
                [stats_in[y * row_blocks + n, pl.ds(line, 1), :] for n in range(row_blocks)], axis=1
            )

        blocks = pl.ds(y * row_blocks, row_blocks)
        query_rows = qg[blocks, 0, :, lanes].reshape(row_keys, 128)
        grad_rows = qg[blocks, 1, :, lanes].reshape(row_keys, 128)
        wide_a[row] = dot_nt(own_keys, query_rows)
        wide_b[row] = dot_nt(own_values, grad_rows)
        for head in range(2):
            log_row, delta_row = stat_row(2 * pair + head), stat_row(HEADS + 2 * pair + head)
            for first in range(head * BLOCK, head * BLOCK + BLOCK, STRIP):
                strip = slice(first, first + STRIP)
                chances = jnp.exp(wide_a[row, strip, :] - log_row)
                thin_a[row, strip, :] = chances.astype(BF16)
                thin_b[row, strip, :] = (chances * (wide_b[row, strip, :] - delta_row)).astype(BF16)
        sum_k = dot_nn(thin_b[row], query_rows)
        sum_v = dot_nn(thin_a[row], grad_rows)
        own_dk = jnp.where(low, sum_k[:BLOCK], sum_k[BLOCK:])
        own_dv = jnp.where(low, sum_v[:BLOCK], sum_v[BLOCK:])
        near_dk[pair] = own_dk if row == 0 else near_dk[pair] + own_dk
        near_dv[pair] = own_dv if row == 0 else near_dv[pair] + own_dv
        return carry

    def gathered(y):
        for x in (x0, x_left, x_right, x_far):
            arrived(1, block_id(y, x, other))

    gathered(y0)
    lax.fori_loop(0, PAIRS, functools.partial(key_pair, 0, y0), 0)
    gathered(y1)
    lax.fori_loop(0, PAIRS, functools.partial(key_pair, 1, y1), 0)

    for phase in range(PHASES):
        exchanged(ret, ret_recv, phase)
        for place in range(PER_PHASE):
            pair = phase * PER_PHASE + place
            cols = slice(pair * 128, pair * 128 + 128)
            hits = picks[...]
            back_k = ret[phase, :, :, place * 256 : place * 256 + 128].reshape(far_rows, 128)
            back_v = ret[phase, :, :, place * 256 + 128 : place * 256 + 256].reshape(far_rows, 128)
            dk_ref[:, cols] = (near_dk[pair] * 0.125 + dot_nn(hits, back_k)).astype(BF16)
            dv_ref[:, cols] = (near_dv[pair] + dot_nn(hits, back_v)).astype(BF16)

    dk_copy, dv_copy = written(2, dk_ref, dk_out), written(3, dv_ref, dv_out)
    dk_copy.start()
    dv_copy.start()
    for copy in started:
        copy.wait_send()
    for phase in range(PHASES):
        exchanged(far_out, far_send, phase)
        exchanged(terms, ret_send, phase)
    sent_stats = stats_out.at[pl.ds(0, n_blk - 1)]
    pltpu.make_async_copy(sent_stats, sent_stats, stat_send.at[0]).wait()
    for copy in (att_copy, dq_copy, dk_copy, dv_copy):
        copy.wait()


def write_out(a, b, c, d, a_out, b_out, c_out, d_out, stage, sems):
    pairs = ((a, a_out), (b, b_out), (c, c_out), (d, d_out))
    reads = [pltpu.make_async_copy(pair[0], stage.at[n], sems.at[0, n]) for n, pair in enumerate(pairs)]
    writes = [pltpu.make_async_copy(stage.at[n], pair[1], sems.at[1, n]) for n, pair in enumerate(pairs)]
    for read in reads:
        read.start()
    for read, write in zip(reads, writes):
        read.wait()
        write.start()
    for write in writes:
        write.wait()


def on_device(n_dom, n_blk, queries, keys, values, grad_out, tile_keys, tile_count, send_rows):
    rows, width = queries.shape
    far_rows = n_dom * SLOT
    row_keys = n_blk // 2 * BLOCK
    hbm = pl.BlockSpec(memory_space=pltpu.HBM)
    smem = pl.BlockSpec(memory_space=pltpu.SMEM)
    far_shape = (PHASES, n_dom, SLOT, PER_PHASE * 256)
    stack = pltpu.VMEM((PAIRS, 256, 128), BF16)
    wide = pltpu.VMEM((PAIRS, 256, 128), F32)
    wide_rows = pltpu.VMEM((2, PAIRS, 256, 128), F32)
    thin = pltpu.VMEM((PAIRS, 256, 1), F32)
    thin_rows = pltpu.VMEM((2, PAIRS, 256, 1), F32)
    whole = pltpu.VMEM((rows, width), BF16)
    own = pltpu.VMEM((PAIRS, BLOCK, 128), F32)
    dma = pltpu.SemaphoreType.DMA
    held = pl.pallas_call(
        functools.partial(kernel, n_dom, n_blk),
        out_shape=[jax.ShapeDtypeStruct((rows, width), BF16)] * 4,
        in_specs=[hbm, hbm, hbm, hbm, hbm, smem, hbm],
        out_specs=[hbm] * 4,
        scratch_shapes=[
            pltpu.VMEM((n_blk, 2, BLOCK, width), BF16),
            pltpu.VMEM((n_blk, 2, BLOCK, width), BF16),
            pltpu.VMEM(far_shape, BF16),
            pltpu.VMEM(far_shape, BF16),
            pltpu.VMEM(far_shape, BF16),
            pltpu.VMEM(far_shape, BF16),
            pltpu.VMEM((n_blk, 2 * HEADS, BLOCK), F32),
            pltpu.VMEM((n_blk, 2 * HEADS, BLOCK), F32),
            pltpu.SMEM((1, n_blk), jnp.int32),
            pltpu.VMEM((1, SLOT, n_dom), jnp.int32),
            stack, stack, stack, stack,
            pltpu.VMEM((BLOCK, far_rows), BF16),
            pltpu.VMEM((1, n_blk * BLOCK), F32),
            pltpu.VMEM((1, far_rows), F32),
            pltpu.VMEM((2, PAIRS, 256, row_keys), F32),
            pltpu.VMEM((2, PAIRS, 256, row_keys), BF16),
            pltpu.VMEM((2, 256, row_keys), F32),
            pltpu.VMEM((2, 256, row_keys), F32),
            pltpu.VMEM((2, 256, row_keys), BF16),
            pltpu.VMEM((2, 256, row_keys), BF16),
            wide_rows,
            thin_rows, thin_rows,
            wide_rows,
            thin_rows, thin,
            wide,
            own, own,
            pltpu.VMEM((BLOCK, 128), F32),
            dma((6,)), dma((34,)), dma((2, n_blk, 2)),
            dma((PHASES,)), dma((PHASES,)), dma((PHASES,)), dma((PHASES,)),
            dma((1,)), dma((1,)),
            whole, whole, whole, whole, dma((4,)),
        ],
        compiler_params=pltpu.CompilerParams(
            collective_id=0, has_side_effects=True, vmem_limit_bytes=63 * 1024 * 1024
        ),
        cost_estimate=pl.CostEstimate(flops=2_500_000_000, bytes_accessed=2_000_000, transcendentals=5_000_000),
    )(queries, keys, values, grad_out, tile_keys, tile_count, send_rows.transpose(0, 2, 1))
    return pl.pallas_call(
        write_out,
        out_shape=[jax.ShapeDtypeStruct((rows, width), BF16)] * 4,
        in_specs=[hbm] * 4,
        out_specs=[hbm] * 4,
        scratch_shapes=[pltpu.VMEM((4, rows, width), BF16), dma((2, 4))],
        compiler_params=pltpu.CompilerParams(vmem_limit_bytes=63 * 1024 * 1024),
    )(*held)


def solution(mesh):
    n_dom, n_blk = mesh.shape["dom"], mesh.shape["blk"]
    both = ("dom", "blk")
    flat = P(both, None)
    return jax.shard_map(
        functools.partial(on_device, n_dom, n_blk),
        mesh=mesh,
        in_specs=(flat, flat, flat, flat, flat, P(both), P(both, None, None)),
        out_specs=(flat,) * 4,
        check_vma=False,
    )
```
